512 devices in a mesh: grp: 8 (over z_lo, core), blk: 8 (over y), set: 8 (over z_hi, x).
Axes of the slice: x: 4, y: 8, z: 8 (z_hi: 2, z_lo: 4; z = z_hi * 4 + z_lo), core: 2. Of those that a mesh axis runs over, the one named last changes fastest.
Arguments:
- queries: bfloat16 [65536, 384], P(('grp', 'blk', 'set')), may hold values from -8 to 8
- keys: bfloat16 [65536, 384], P(('grp', 'blk', 'set')), may hold values from -8 to 8
- values: bfloat16 [65536, 384], P(('grp', 'blk', 'set')), may hold values from -6 to 6
- valid: int32 [65536], P(('grp', 'blk', 'set')), may hold values 0 or 1
- offsets: int32 [2, 6], replicated, may hold values from 0 to 63, as said below
- w_out: bfloat16 [384, 768], replicated, may hold values from -0.3125 to 0.3125
Outputs:
- projected: bfloat16 [65536, 768], P(('grp', 'blk', 'set'))
The draws below stay inside these ranges and needn't reach their ends.
Inputs may be any that keep to these rules, and one draw needn't show every extreme that they name: offsets[0, h] lies in 0 to 7 and offsets[1, h] - offsets[0, h] is a multiple of 8 for every head h.
All inputs are finite; a program needn't handle non-finite values. No bound on the sum of `valid` on one device may be relied on, other than what follows from the above.
Results may differ from the reference program's by a relative error of at most 0.0015.
The reference program's roundings to bfloat16 on the way count: a program that leaves them out, or rounds other values in their place, can miss the bound.
Values may be sent and summed in bfloat16 or wider, within the bound.
No kernel may reach another device: no remote copies, remote signals or barrier semaphores. Data moves between devices by JAX's collectives and lax.ppermute only.
A program may use at most 64 MiB of HBM per device.

```python
import math
import jax
import jax.numpy as jnp
from jax import lax

MODEL_WIDTH = 768
HEAD_COUNT = 6
HD = 64
ATT_WIDTH = 384
FIRST_SEGMENT = 1024
TOKENS = 65536
SECOND_DILATION = 8
THIRD_DILATION = 64


def drawn_pair(key):
    base_key = jax.random.fold_in(key, 17)
    first_key, second_key = jax.random.split(base_key, 2)
    full_shape = (TOKENS, ATT_WIDTH)
    query_draw = jnp.clip(1.5 * jax.random.normal(first_key, full_shape, jnp.float32), -8.0, 8.0)
    key_draw = jnp.clip(1.5 * jax.random.normal(second_key, full_shape, jnp.float32), -8.0, 8.0)
    return (query_draw, key_draw)


def draw_queries(key, part):
    return drawn_pair(key)[0].astype(jnp.bfloat16)


def draw_keys(key, part):
    return drawn_pair(key)[1].astype(jnp.bfloat16)


def draw_offsets(key, part):
    base_key = jax.random.fold_in(key, 29)
    bottom_key, ceiling_key = jax.random.split(base_key)
    middle_shift = jax.random.randint(bottom_key, (HEAD_COUNT,), 0, SECOND_DILATION)
    outer_shift = middle_shift + SECOND_DILATION * jax.random.randint(ceiling_key, (HEAD_COUNT,), 0, THIRD_DILATION // SECOND_DILATION)
    return jnp.stack([middle_shift, outer_shift]).astype(jnp.int32)


def set_ends(drawn, own_key, low, high):
    longest = drawn.shape.index(max(drawn.shape))
    spots = []
    for shift in (0, 1):
        where = [jax.random.randint(jax.random.fold_in(own_key, axis), (), 0, length) for axis, length in enumerate(drawn.shape)]
        where[longest] = (where[longest] + shift) % drawn.shape[longest]
        spots.append(tuple(where))
    return drawn.at[spots[0]].set(low).at[spots[1]].set(high)


def level_of(key, shape, cuts, least, largest):
    def one(dim, parts):
        steps = jax.random.uniform(jax.random.fold_in(jax.random.fold_in(key, 6), dim), (parts,), jnp.float32, least / len(cuts), largest / len(cuts))
        return jnp.repeat(jnp.exp(steps), shape[dim] // parts).reshape((-1,) + (1,) * (len(shape) - dim - 1))

    loudness = one(*cuts[0])
    for cut in cuts[1:]:
        loudness = loudness * one(*cut)
    return loudness


def normal_values(own_key, extent, width, limit, cuts=(), kind=jnp.bfloat16):
    array = jax.random.normal(own_key, extent, jnp.float32) * width
    if len(cuts) > 0:
        array = level_of(own_key, extent, cuts, -0.22, 0.18) * array
    return jnp.clip(array, min=-limit, max=limit).astype(kind)


def setup_inputs(seed: int = 0) -> dict:
    streams_of = jax.random.split(jax.random.key(seed), 7)
    return {
        "queries": draw_queries(jax.random.fold_in(streams_of[6], 71), 0),
        "keys": draw_keys(jax.random.fold_in(streams_of[6], 71), 0),
        "values": normal_values(streams_of[2], (TOKENS, ATT_WIDTH), 1.0, 6.0, ((0, 512),)),
        "valid": set_ends((jax.random.randint(streams_of[3], (TOKENS,), 0, 4) < 3).astype(jnp.int32), jax.random.fold_in(streams_of[3], 1), 0, 1),
        "offsets": draw_offsets(jax.random.fold_in(streams_of[6], 71), 0),
        "w_out": normal_values(streams_of[5], (ATT_WIDTH, MODEL_WIDTH), ATT_WIDTH ** -0.5, 0.3125),
    }


def head_attend(query_head, key_head, value_head, key_allowed, self_slot, scaling):
    scores = lax.dot_general(query_head, key_head, (((1,), (1,)), ((), ())), preferred_element_type=jnp.float32) * scaling
    columns = jnp.arange(key_head.shape[0], dtype=jnp.int32)
    allowed = key_allowed[None, :] | (columns[None, :] == self_slot[:, None])
    scores = jnp.where(allowed, scores, jnp.float32(-1e+30))
    highest = lax.optimization_barrier(jnp.max(scores, axis=1, keepdims=True))
    weights = jnp.exp(scores - highest)
    totals = lax.optimization_barrier(jnp.sum(weights, axis=1))
    mixture = jnp.dot(weights.astype(jnp.bfloat16), value_head, preferred_element_type=jnp.float32) / totals[:, None]
    return (mixture, highest[:, 0] + jnp.log(totals))

def attend(queries, keys, values, key_allowed, self_slot):
    row_count = queries.shape[0]
    length = keys.shape[0]
    heads_query = queries.reshape(row_count, HEAD_COUNT, HD).transpose(1, 0, 2)
    heads_key = keys.reshape(length, HEAD_COUNT, HD).transpose(1, 0, 2)
    heads_value = values.reshape(length, HEAD_COUNT, HD).transpose(1, 0, 2)
    scaling = 1.0 / math.sqrt(HD)
    mixture, log_totals = lax.map(lambda packed: head_attend(packed[0], packed[1], packed[2], packed[3], self_slot, scaling), (heads_query, heads_key, heads_value, key_allowed.T))
    return (mixture.transpose(1, 0, 2).reshape(row_count, HEAD_COUNT * HD), log_totals.T)

def selector_table(shift_amount, cycle_length):
    return jnp.arange(cycle_length, dtype=jnp.int32)[:, None] == shift_amount[None, :]

def pick_rows(matrix, shift_amount, cycle_length):
    row_total = matrix.shape[0]
    selector = selector_table(shift_amount, cycle_length)
    blocks = matrix.reshape(row_total // cycle_length, cycle_length, HEAD_COUNT, HD)
    chosen = lax.optimization_barrier(jnp.sum(jnp.where(selector[None, :, :, None], blocks, jnp.zeros((), matrix.dtype)), axis=1))
    return chosen.reshape(row_total // cycle_length, HEAD_COUNT * HD)

def pick_flags(key_flags, shift_amount, cycle_length):
    row_total = key_flags.shape[0]
    selector = selector_table(shift_amount, cycle_length)
    blocks = key_flags.reshape(row_total // cycle_length, cycle_length)
    return lax.optimization_barrier(jnp.sum(jnp.where(selector[None, :, :], blocks[:, :, None], jnp.zeros((), key_flags.dtype)), axis=1))

def spread_back(mixture, log_totals, shift_amount, cycle_length):
    row_count = mixture.shape[0]
    selector = selector_table(shift_amount, cycle_length)
    wide = jnp.where(selector[None, :, :, None], mixture.reshape(row_count, 1, HEAD_COUNT, HD), jnp.float32(0.0))
    spread_totals = jnp.where(selector[None, :, :], log_totals[:, None, :], jnp.float32(0.0))
    present = jnp.broadcast_to(selector[None, :, :], (row_count, cycle_length, HEAD_COUNT))
    return (wide.reshape(row_count * cycle_length, HEAD_COUNT * HD), spread_totals.reshape(row_count * cycle_length, HEAD_COUNT), present.reshape(row_count * cycle_length, HEAD_COUNT))

def combine(levels):
    highest = levels[0][1]
    for entry in levels[1:]:
        highest = jnp.maximum(highest, jnp.where(entry[2], entry[1], highest))
    numerator = jnp.zeros(levels[0][0].shape, jnp.float32)
    denominator = jnp.zeros(levels[0][1].shape, jnp.float32)
    for entry in levels:
        scaled = jnp.where(entry[2], jnp.exp(entry[1] - highest), jnp.float32(0.0))
        expanded = jnp.broadcast_to(scaled[:, :, None], (scaled.shape[0], HEAD_COUNT, HD)).reshape(scaled.shape[0], HEAD_COUNT * HD)
        numerator = numerator + entry[0] * expanded
        denominator = denominator + scaled
    wide_denominator = jnp.broadcast_to(denominator[:, :, None], (denominator.shape[0], HEAD_COUNT, HD)).reshape(denominator.shape[0], HEAD_COUNT * HD)
    return numerator / wide_denominator

def segmented(queries, keys, values, key_allowed, segment):
    total_rows = queries.shape[0]
    pieces = total_rows // segment
    slot_index = jnp.arange(segment, dtype=jnp.int32)
    mixture, log_totals = lax.map(lambda packed: attend(packed[0], packed[1], packed[2], packed[3], slot_index), (queries.reshape(pieces, segment, HEAD_COUNT * HD), keys.reshape(pieces, segment, HEAD_COUNT * HD), values.reshape(pieces, segment, HEAD_COUNT * HD), key_allowed.reshape(pieces, segment, HEAD_COUNT)))
    return (mixture.reshape(total_rows, HEAD_COUNT * HD), log_totals.reshape(total_rows, HEAD_COUNT))

def reference(queries, keys, values, valid, offsets, w_out):
    total_rows = queries.shape[0]
    key_flags = valid.astype(jnp.float32)
    dense_allowed = jnp.broadcast_to((valid == 1)[:, None], (total_rows, HEAD_COUNT))
    dense_level = segmented(queries, keys, values, dense_allowed, FIRST_SEGMENT)
    levels = [(dense_level[0], dense_level[1], jnp.ones((total_rows, HEAD_COUNT), jnp.bool_))]
    for shift_amount, cycle_length in ((offsets[0], SECOND_DILATION), (offsets[1], THIRD_DILATION)):
        sparse_query = pick_rows(queries, shift_amount, cycle_length)
        sparse_key = pick_rows(keys, shift_amount, cycle_length)
        sparse_value = pick_rows(values, shift_amount, cycle_length)
        sparse_allowed = pick_flags(key_flags, shift_amount, cycle_length) > 0.5
        mixture, log_totals = segmented(sparse_query, sparse_key, sparse_value, sparse_allowed, FIRST_SEGMENT)
        levels.append(spread_back(mixture, log_totals, shift_amount, cycle_length))
    attention = combine(levels).astype(jnp.bfloat16)
    return jnp.dot(attention, w_out, preferred_element_type=jnp.float32).astype(jnp.bfloat16)
```

```python
import functools
import math

import jax
import jax.numpy as jnp
from jax import lax
from jax.experimental import pallas as pl
from jax.experimental.pallas import tpu as pltpu
from jax.sharding import PartitionSpec as P

HEADS = 6
HD = 64
PEERS = 8
ROWS = 128
FLAG_ROWS = 16
KEY_BLOCK = ROWS + FLAG_ROWS
FIRST_BLOCK = KEY_BLOCK + ROWS // 2
EXP_SCALE = math.log2(math.e) / math.sqrt(HD)
FAR = -1e30
F32 = jnp.float32
BF16 = jnp.bfloat16

VMEM = pl.BlockSpec(memory_space=pltpu.VMEM)
SMEM = pl.BlockSpec(memory_space=pltpu.SMEM)


def lanes(shape):
    return lax.broadcasted_iota(jnp.int32, shape, len(shape) - 1)


def rows(shape):
    return lax.broadcasted_iota(jnp.int32, shape, len(shape) - 2)


def my_head():
    return jnp.minimum(lax.axis_index("set"), HEADS - 1)


def shifts(offsets_ref):
    head = my_head()
    middle = offsets_ref[0, head]
    return middle, (offsets_ref[1, head] - middle) // 8


def scores(query, block_ref, index, self_mask):
    raw = lax.dot_general(
        query, block_ref[index, 0:ROWS, :], (((1,), (1,)), ((), ())), preferred_element_type=F32
    )
    flags = block_ref[index, ROWS:KEY_BLOCK, :].astype(F32)[0:1, :]
    bias = jnp.where(flags > 0.5, F32(0.0), F32(FAR))
    if self_mask is not None:
        bias = jnp.where(self_mask, F32(0.0), bias)
    return raw + bias


def level(query, block_ref, self_masks):
    parts = [scores(query, block_ref, c, self_masks[c]) for c in range(PEERS)]
    best = functools.reduce(jnp.maximum, parts)
    top = jnp.max(best, axis=1, keepdims=True)
    sums = None
    mixture = None
    for c in range(PEERS):
        weight = jnp.exp2((parts[c] - top) * F32(EXP_SCALE))
        sums = weight if sums is None else sums + weight
        add = jnp.dot(weight.astype(BF16), block_ref[c, 0:ROWS, :], preferred_element_type=F32)
        mixture = add if mixture is None else mixture + add
    total = jnp.sum(sums, axis=1, keepdims=True)
    lane = lanes(mixture.shape)
    return jnp.where(lane < 32, top, jnp.where(lane < 64, total, mixture))


def merge(one, two):
    top_one, top_two = one[:, 0:1], two[:, 0:1]
    top = jnp.maximum(top_one, top_two)
    scale_one = jnp.exp2((top_one - top) * F32(EXP_SCALE))
    scale_two = jnp.exp2((top_two - top) * F32(EXP_SCALE))
    both = one * scale_one + two * scale_two
    return jnp.where(lanes(both.shape) < 32, top, both)


def divided(state):
    return state / state[:, 32:33]


def pack_kernel(query_ref, key_ref, value_ref, valid_ref, out_ref):
    flags = jnp.broadcast_to(valid_ref[...].astype(F32), (FLAG_ROWS, ROWS)).astype(BF16)
    half = ROWS // 2
    for h in range(HEADS):
        at = slice(h * HD, (h + 1) * HD)
        out_ref[h, 0:ROWS, 0:HD] = key_ref[:, at]
        out_ref[h, 0:ROWS, HD : 2 * HD] = value_ref[:, at]
        out_ref[h, ROWS:KEY_BLOCK, :] = flags
        out_ref[h, KEY_BLOCK:FIRST_BLOCK, 0:HD] = query_ref[0:half, at]
        out_ref[h, KEY_BLOCK:FIRST_BLOCK, HD : 2 * HD] = query_ref[half:ROWS, at]
    for h in range(HEADS, PEERS):
        out_ref[h] = jnp.zeros((FIRST_BLOCK, 2 * HD), BF16)


def pick_kernel(which, offsets_ref, blocks_ref, out_ref, wide):
    shift = shifts(offsets_ref)[which]
    flag_rows = jnp.zeros((PEERS, ROWS), F32)
    for c in range(PEERS):
        wide[c * ROWS : (c + 1) * ROWS, :] = blocks_ref[c, 0:ROWS, :].astype(F32)
        flags = blocks_ref[c, ROWS:KEY_BLOCK, :].astype(F32)[0:PEERS, :]
        flag_rows = jnp.where(rows((PEERS, ROWS)) == c, flags, flag_rows)
    picked = wide[pl.ds(shift, ROWS, stride=8), :].astype(BF16)
    square = (ROWS, ROWS)
    selector = rows(square) == shift + 8 * (lanes(square) % 16)
    spread = jnp.dot(
        flag_rows.astype(BF16), selector.astype(F32).astype(BF16), preferred_element_type=F32
    )
    own = rows((PEERS, ROWS)) == lanes((PEERS, ROWS)) // 16
    flags = jnp.sum(jnp.where(own, spread, F32(0.0)), axis=0, keepdims=True)
    flags = jnp.broadcast_to(flags, (FLAG_ROWS, ROWS)).astype(BF16)
    for c in range(PEERS):
        out_ref[c, 0:ROWS, :] = picked
        out_ref[c, ROWS:KEY_BLOCK, :] = flags


def first_kernel(offsets_ref, blocks_ref, state_ref, middle_ref, outer_ref, wide, narrow):
    middle, stride = shifts(offsets_ref)
    half = ROWS // 2
    low = lanes((half, 2 * HD)) < HD
    diagonal = rows((ROWS, ROWS)) == lanes((ROWS, ROWS))
    for j in range(PEERS):
        pair = blocks_ref[j, KEY_BLOCK:FIRST_BLOCK, :].astype(F32)
        wide[j * ROWS : j * ROWS + half, :] = jnp.where(low, pair, F32(0.0))
        wide[j * ROWS + half : (j + 1) * ROWS, :] = jnp.where(
            low, pltpu.roll(pair, HD, 1), F32(0.0)
        )
        query = wide[j * ROWS : (j + 1) * ROWS, :].astype(BF16)
        masks = [diagonal if c == j else None for c in range(PEERS)]
        state_ref[j * ROWS : (j + 1) * ROWS, :] = level(query, blocks_ref, masks)
    picked = wide[pl.ds(middle, ROWS, stride=8), :]
    middle_ref[...] = picked.astype(BF16)
    narrow[...] = picked
    outer_ref[...] = narrow[pl.ds(stride, ROWS // 8, stride=8), :].astype(BF16)


def middle_kernel(offsets_ref, state_ref, query_ref, blocks_ref, out_ref, merged_ref, wide):
    middle, _ = shifts(offsets_ref)
    mine = lax.axis_index("blk")
    diagonal = rows((ROWS, ROWS)) == lanes((ROWS, ROWS))
    masks = [diagonal & (mine == c) for c in range(PEERS)]
    found = level(query_ref[...], blocks_ref, masks)
    both = merge(state_ref[pl.ds(middle, ROWS, stride=8), :], found)
    merged_ref[...] = both
    wide[...] = state_ref[...]
    wide[pl.ds(middle, ROWS, stride=8), :] = both
    half = ROWS // 2
    low = lanes((half, 2 * HD)) < HD
    for j in range(PEERS):
        one = divided(wide[j * ROWS : j * ROWS + half, :])
        two = divided(wide[j * ROWS + half : (j + 1) * ROWS, :])
        out_ref[j] = jnp.where(low, pltpu.roll(one, HD, 1), two).astype(BF16)


def outer_kernel(offsets_ref, merged_ref, query_ref, blocks_ref, before_ref, out_ref):
    middle, stride = shifts(offsets_ref)
    block, group = lax.axis_index("blk"), lax.axis_index("grp")
    count = ROWS // 8
    shape = (count, ROWS)
    diagonal = lanes(shape) == block * count + rows(shape)
    masks = [diagonal & (group == c) for c in range(PEERS)]
    found = level(query_ref[...], blocks_ref, masks)
    both = divided(merge(merged_ref[pl.ds(stride, count, stride=8), :], found))
    turned = pltpu.roll(both, HD, 1)
    half = ROWS // 2
    here = rows((half, 2 * HD)) == middle + 8 * stride
    low = lanes((1, 2 * HD)) < HD
    for j in range(PEERS):
        row = jnp.where(low, turned[2 * j : 2 * j + 1, :], both[2 * j + 1 : 2 * j + 2, :])
        out_ref[j] = jnp.where(here, row, before_ref[j].astype(F32)).astype(BF16)


def project_kernel(blocks_ref, weight_ref, out_ref):
    half = ROWS // 2
    for part in range(2):
        total = None
        for h in range(HEADS):
            add = jnp.dot(
                blocks_ref[h, :, part * HD : (part + 1) * HD],
                weight_ref[h * HD : (h + 1) * HD, :],
                preferred_element_type=F32,
            )
            total = add if total is None else total + add
        out_ref[part * half : (part + 1) * half, :] = total.astype(BF16)


def call(kernel, name, out_shape, in_specs, scratch=(), flops=0, moved=0):
    outs = jax.tree.map(lambda _: VMEM, out_shape)
    return pl.pallas_call(
        kernel,
        name=name,
        out_shape=out_shape,
        in_specs=in_specs,
        out_specs=outs,
        scratch_shapes=list(scratch),
        compiler_params=pltpu.CompilerParams(vmem_limit_bytes=40 * 2**20),
        cost_estimate=pl.CostEstimate(flops=flops, bytes_accessed=moved, transcendentals=0),
    )


def shaped(*shape, dtype=BF16):
    return jax.ShapeDtypeStruct(shape, dtype)


def per_device(queries, keys, values, valid, offsets, w_out):
    wide = pltpu.VMEM((PEERS * ROWS, 2 * HD), F32)
    narrow = pltpu.VMEM((ROWS, 2 * HD), F32)
    swap = functools.partial(lax.all_to_all, split_axis=0, concat_axis=0, tiled=True)

    packed = call(pack_kernel, "pack", shaped(PEERS, FIRST_BLOCK, 2 * HD), [VMEM] * 4)(
        queries, keys, values, valid.reshape(1, ROWS)
    )
    dense = swap(packed, "set")

    def pick(which, name, blocks):
        return call(
            functools.partial(pick_kernel, which),
            name,
            shaped(PEERS, KEY_BLOCK, 2 * HD),
            [SMEM, VMEM],
            [wide],
        )(offsets, blocks)

    middle_blocks = swap(pick(0, "pick_middle", dense), "blk")
    state, middle_query, outer_query = call(
        first_kernel,
        "first",
        (shaped(PEERS * ROWS, 2 * HD, dtype=F32), shaped(ROWS, 2 * HD), shaped(ROWS // 8, 2 * HD)),
        [SMEM, VMEM],
        [wide, narrow],
        flops=6_000_000_000,
        moved=2_000_000,
    )(offsets, dense)
    outer_blocks = swap(pick(1, "pick_outer", middle_blocks), "grp")
    before, merged = call(
        middle_kernel,
        "middle",
        (shaped(PEERS, ROWS // 2, 2 * HD), shaped(ROWS, 2 * HD, dtype=F32)),
        [SMEM, VMEM, VMEM, VMEM],
        [wide],
        flops=2_000_000_000,
        moved=2_000_000,
    )(offsets, state, middle_query, middle_blocks)
    combined = call(
        outer_kernel,
        "outer",
        shaped(PEERS, ROWS // 2, 2 * HD),
        [SMEM, VMEM, VMEM, VMEM, VMEM],
    )(offsets, merged, outer_query, outer_blocks, before)
    home = swap(combined, "set")
    return call(project_kernel, "project", shaped(ROWS, 768), [VMEM, VMEM])(home, w_out)


def solution(mesh):
    spread = P(("grp", "blk", "set"), None)
    return jax.shard_map(
        per_device,
        mesh=mesh,
        in_specs=(spread, spread, spread, P(("grp", "blk", "set")), P(), P()),
        out_specs=spread,
        check_vma=False,
    )
```

```python
import functools
import math

import jax
import jax.numpy as jnp
from jax import lax
from jax.experimental import pallas as pl
from jax.experimental.pallas import tpu as pltpu
from jax.sharding import PartitionSpec as P

HEADS = 6
HD = 64
PEERS = 8
ROWS = 128
FLAG_ROWS = 16
KEY_BLOCK = ROWS + FLAG_ROWS
FIRST_BLOCK = KEY_BLOCK + ROWS // 2
EXP_SCALE = math.log2(math.e) / math.sqrt(HD)
FAR = -1e30
ROOM = 60 * 2**20
F32 = jnp.float32
BF16 = jnp.bfloat16

VMEM = pl.BlockSpec(memory_space=pltpu.VMEM)
SMEM = pl.BlockSpec(memory_space=pltpu.SMEM)
HBM = pl.BlockSpec(memory_space=pltpu.HBM)


def lanes(shape):
    return lax.broadcasted_iota(jnp.int32, shape, len(shape) - 1)


def rows(shape):
    return lax.broadcasted_iota(jnp.int32, shape, len(shape) - 2)


def my_head():
    return jnp.minimum(lax.axis_index("set"), HEADS - 1)


def shifts(offsets_ref):
    head = my_head()
    middle = offsets_ref[0, head]
    return middle, (offsets_ref[1, head] - middle) // 8


def scores(query, block_ref, index, self_mask):
    raw = lax.dot_general(
        query, block_ref[index, 0:ROWS, :], (((1,), (1,)), ((), ())), preferred_element_type=F32
    )
    flags = block_ref[index, ROWS:KEY_BLOCK, :].astype(F32)[0:1, :]
    bias = jnp.where(flags > 0.5, F32(0.0), F32(FAR))
    if self_mask is not None:
        bias = jnp.where(self_mask, F32(0.0), bias)
    return raw + bias


def level(query, block_ref, self_masks):
    parts = [scores(query, block_ref, c, self_masks[c]) for c in range(PEERS)]
    best = functools.reduce(jnp.maximum, parts)
    top = jnp.max(best, axis=1, keepdims=True)
    sums = None
    mixture = None
    for c in range(PEERS):
        weight = jnp.exp2((parts[c] - top) * F32(EXP_SCALE))
        sums = weight if sums is None else sums + weight
        add = jnp.dot(weight.astype(BF16), block_ref[c, 0:ROWS, :], preferred_element_type=F32)
        mixture = add if mixture is None else mixture + add
    total = jnp.sum(sums, axis=1, keepdims=True)
    lane = lanes(mixture.shape)
    return jnp.where(lane < 32, top, jnp.where(lane < 64, total, mixture))


def merge(one, two):
    top_one, top_two = one[:, 0:1], two[:, 0:1]
    top = jnp.maximum(top_one, top_two)
    scale_one = jnp.exp2((top_one - top) * F32(EXP_SCALE))
    scale_two = jnp.exp2((top_two - top) * F32(EXP_SCALE))
    both = one * scale_one + two * scale_two
    return jnp.where(lanes(both.shape) < 32, top, both)


def divided(state):
    return state / state[:, 32:33]


def pack_kernel(query_hbm, key_hbm, value_hbm, valid_hbm, out_ref, query_ref, key_ref, value_ref, valid_ref, sems):
    pairs = (
        (valid_hbm, valid_ref),
        (key_hbm, key_ref),
        (value_hbm, value_ref),
        (query_hbm, query_ref),
    )
    copies = [pltpu.make_async_copy(a, b, sems.at[i]) for i, (a, b) in enumerate(pairs)]
    for copy in copies:
        copy.start()
    for h in range(HEADS, PEERS):
        out_ref[h] = jnp.zeros((FIRST_BLOCK, 2 * HD), BF16)
    for copy in copies:
        copy.wait()
    flags = jnp.broadcast_to(valid_ref[...].astype(F32), (FLAG_ROWS, ROWS)).astype(BF16)
    half = ROWS // 2
    for h in range(HEADS):
        at = slice(h * HD, (h + 1) * HD)
        out_ref[h, 0:ROWS, 0:HD] = key_ref[:, at]
        out_ref[h, 0:ROWS, HD : 2 * HD] = value_ref[:, at]
        out_ref[h, ROWS:KEY_BLOCK, :] = flags
        out_ref[h, KEY_BLOCK:FIRST_BLOCK, 0:HD] = query_ref[0:half, at]
        out_ref[h, KEY_BLOCK:FIRST_BLOCK, HD : 2 * HD] = query_ref[half:ROWS, at]


def pick_kernel(which, offsets_ref, blocks_ref, out_ref):
    shift = shifts(offsets_ref)[which]
    count = ROWS // 8
    shape = (count, ROWS)
    selector = (lanes(shape) == shift + 8 * rows(shape)).astype(F32).astype(BF16)
    flag_rows = jnp.zeros((PEERS, ROWS), F32)
    for c in range(PEERS):
        picked = jnp.dot(selector, blocks_ref[c, 0:ROWS, :], preferred_element_type=F32).astype(BF16)
        for d in range(PEERS):
            out_ref[d, c * count : (c + 1) * count, :] = picked
        flags = blocks_ref[c, ROWS:KEY_BLOCK, :].astype(F32)[0:PEERS, :]
        flag_rows = jnp.where(rows((PEERS, ROWS)) == c, flags, flag_rows)
    square = (ROWS, ROWS)
    chosen = rows(square) == shift + 8 * (lanes(square) % count)
    spread = jnp.dot(
        flag_rows.astype(BF16), chosen.astype(F32).astype(BF16), preferred_element_type=F32
    )
    own = rows((PEERS, ROWS)) == lanes((PEERS, ROWS)) // count
    flags = jnp.sum(jnp.where(own, spread, F32(0.0)), axis=0, keepdims=True)
    flags = jnp.broadcast_to(flags, (FLAG_ROWS, ROWS)).astype(BF16)
    for d in range(PEERS):
        out_ref[d, ROWS:KEY_BLOCK, :] = flags


def first_kernel(offsets_ref, blocks_ref, state_ref, middle_ref, outer_ref, wide, narrow):
    middle, stride = shifts(offsets_ref)
    half = ROWS // 2
    low = lanes((half, 2 * HD)) < HD
    diagonal = rows((ROWS, ROWS)) == lanes((ROWS, ROWS))
    for j in range(PEERS):
        pair = blocks_ref[j, KEY_BLOCK:FIRST_BLOCK, :].astype(F32)
        wide[j * ROWS : j * ROWS + half, :] = jnp.where(low, pair, F32(0.0))
        wide[j * ROWS + half : (j + 1) * ROWS, :] = jnp.where(
            low, pltpu.roll(pair, HD, 1), F32(0.0)
        )
        query = wide[j * ROWS : (j + 1) * ROWS, :].astype(BF16)
        masks = [diagonal if c == j else None for c in range(PEERS)]
        state_ref[j * ROWS : (j + 1) * ROWS, :] = level(query, blocks_ref, masks)
    picked = wide[pl.ds(middle, ROWS, stride=8), :]
    middle_ref[...] = picked.astype(BF16)
    narrow[...] = picked
    outer_ref[...] = narrow[pl.ds(stride, ROWS // 8, stride=8), :].astype(BF16)


def middle_kernel(offsets_ref, state_ref, query_ref, blocks_ref, out_ref, merged_ref, wide):
    middle, _ = shifts(offsets_ref)
    mine = lax.axis_index("blk")
    diagonal = rows((ROWS, ROWS)) == lanes((ROWS, ROWS))
    masks = [diagonal & (mine == c) for c in range(PEERS)]
    found = level(query_ref[...], blocks_ref, masks)
    both = merge(state_ref[pl.ds(middle, ROWS, stride=8), :], found)
    merged_ref[...] = both
    wide[...] = state_ref[...]
    wide[pl.ds(middle, ROWS, stride=8), :] = both
    half = ROWS // 2
    low = lanes((half, 2 * HD)) < HD
    for j in range(PEERS):
        one = divided(wide[j * ROWS : j * ROWS + half, :])
        two = divided(wide[j * ROWS + half : (j + 1) * ROWS, :])
        out_ref[j] = jnp.where(low, pltpu.roll(one, HD, 1), two).astype(BF16)


def outer_kernel(offsets_ref, merged_ref, query_ref, blocks_ref, before_ref, out_ref):
    middle, stride = shifts(offsets_ref)
    block, group = lax.axis_index("blk"), lax.axis_index("grp")
    count = ROWS // 8
    shape = (count, ROWS)
    diagonal = lanes(shape) == block * count + rows(shape)
    masks = [diagonal & (group == c) for c in range(PEERS)]
    found = level(query_ref[...], blocks_ref, masks)
    both = divided(merge(merged_ref[pl.ds(stride, count, stride=8), :], found))
    turned = pltpu.roll(both, HD, 1)
    tile = 16
    token = middle + 8 * stride
    start = pl.multiple_of((token // tile) * tile, tile)
    here = rows((tile, 2 * HD)) == token - start
    low = lanes((1, 2 * HD)) < HD
    for j in range(PEERS):
        row = jnp.where(low, turned[2 * j : 2 * j + 1, :], both[2 * j + 1 : 2 * j + 2, :])
        kept = before_ref[j, pl.ds(start, tile), :].astype(F32)
        out_ref[j, pl.ds(start, tile), :] = jnp.where(here, row, kept).astype(BF16)


def project_kernel(blocks_ref, weight_ref, out_ref):
    half = ROWS // 2
    low = lanes((half, 2 * HD)) < HD
    tops, bottoms = [], []
    for h in range(0, HEADS, 2):
        one, two = blocks_ref[h].astype(F32), blocks_ref[h + 1].astype(F32)
        tops.append(jnp.where(low, one, pltpu.roll(two, HD, 1)).astype(BF16))
        bottoms.append(jnp.where(low, pltpu.roll(one, HD, 1), two).astype(BF16))
    combined = jnp.concatenate(
        [jnp.concatenate(tops, axis=1), jnp.concatenate(bottoms, axis=1)], axis=0
    )
    out_ref[...] = jnp.dot(combined, weight_ref[...], preferred_element_type=F32).astype(BF16)


def call(kernel, name, out_shape, in_specs, scratch=(), flops=0, moved=0, aliases=None, room=40 * 2**20):
    outs = jax.tree.map(lambda _: VMEM, out_shape)
    return pl.pallas_call(
        kernel,
        name=name,
        out_shape=out_shape,
        in_specs=in_specs,
        out_specs=outs,
        scratch_shapes=list(scratch),
        input_output_aliases=aliases or {},
        compiler_params=pltpu.CompilerParams(vmem_limit_bytes=room),
        cost_estimate=pl.CostEstimate(flops=flops, bytes_accessed=moved, transcendentals=0),
    )


def shaped(*shape, dtype=BF16):
    return jax.ShapeDtypeStruct(shape, dtype)


def per_device(queries, keys, values, valid, offsets, w_out):
    wide = pltpu.VMEM((PEERS * ROWS, 2 * HD), F32)
    narrow = pltpu.VMEM((ROWS, 2 * HD), F32)
    swap = functools.partial(lax.all_to_all, split_axis=0, concat_axis=0, tiled=True)

    whole = pltpu.VMEM((ROWS, HEADS * HD), BF16)
    packed = call(
        pack_kernel,
        "pack",
        shaped(PEERS, FIRST_BLOCK, 2 * HD),
        [HBM] * 4,
        [whole, whole, whole, pltpu.VMEM((1, ROWS), jnp.int32), pltpu.SemaphoreType.DMA((4,))],
        room=ROOM,
    )(queries, keys, values, valid.reshape(1, ROWS))
    dense = swap(packed, "set")

    def pick(which, name, blocks):
        return call(
            functools.partial(pick_kernel, which),
            name,
            shaped(PEERS, KEY_BLOCK, 2 * HD),
            [SMEM, VMEM],
        )(offsets, blocks)

    middle_blocks = swap(pick(0, "pick_middle", dense), "blk")
    state, middle_query, outer_query = call(
        first_kernel,
        "first",
        (shaped(PEERS * ROWS, 2 * HD, dtype=F32), shaped(ROWS, 2 * HD), shaped(ROWS // 8, 2 * HD)),
        [SMEM, VMEM],
        [wide, narrow],
        flops=6_000_000_000,
        moved=2_000_000,
    )(offsets, dense)
    outer_blocks = swap(pick(1, "pick_outer", middle_blocks), "grp")
    before, merged = call(
        middle_kernel,
        "middle",
        (shaped(PEERS, ROWS // 2, 2 * HD), shaped(ROWS, 2 * HD, dtype=F32)),
        [SMEM, VMEM, VMEM, VMEM],
        [wide],
        flops=2_000_000_000,
        moved=2_000_000,
    )(offsets, state, middle_query, middle_blocks)
    combined = call(
        outer_kernel,
        "outer",
        shaped(PEERS, ROWS // 2, 2 * HD),
        [SMEM, VMEM, VMEM, VMEM, VMEM],
        aliases={4: 0},
    )(offsets, merged, outer_query, outer_blocks, before)
    home = swap(combined, "set")
    return call(project_kernel, "project", shaped(ROWS, 768), [VMEM, VMEM])(home, w_out)


def solution(mesh):
    spread = P(("grp", "blk", "set"), None)
    return jax.shard_map(
        per_device,
        mesh=mesh,
        in_specs=(spread, spread, spread, P(("grp", "blk", "set")), P(), P()),
        out_specs=spread,
        check_vma=False,
    )
```

```python
import functools
import math

import jax
import jax.numpy as jnp
from jax import lax
from jax.experimental import pallas as pl
from jax.experimental.pallas import tpu as pltpu
from jax.sharding import PartitionSpec as P

HEADS = 6
HD = 64
PEERS = 8
ROWS = 128
FLAG_ROWS = 16
KEY_BLOCK = ROWS + FLAG_ROWS
FIRST_BLOCK = KEY_BLOCK + ROWS // 2
EXP_SCALE = math.log2(math.e) / math.sqrt(HD)
FAR = -1e30
F32 = jnp.float32
BF16 = jnp.bfloat16

VMEM = pl.BlockSpec(memory_space=pltpu.VMEM)
HBM = pl.BlockSpec(memory_space=pltpu.HBM)


def lanes(shape):
    return lax.broadcasted_iota(jnp.int32, shape, len(shape) - 1)


def rows(shape):
    return lax.broadcasted_iota(jnp.int32, shape, len(shape) - 2)


def my_head():
    return jnp.minimum(lax.axis_index("set"), HEADS - 1)


def shifts(offsets_ref):
    both = offsets_ref[...].astype(F32)
    both = jnp.where(lanes(both.shape) == my_head(), both, F32(0.0))
    middle = jnp.sum(both[0:1, :]).astype(jnp.int32)
    outer = jnp.sum(both[1:2, :]).astype(jnp.int32)
    return middle, (outer - middle) // 8


def scores(query, block_ref, index, self_mask):
    raw = lax.dot_general(
        query, block_ref[index, 0:ROWS, :], (((1,), (1,)), ((), ())), preferred_element_type=F32
    )
    flags = block_ref[index, ROWS:KEY_BLOCK, :].astype(F32)[0:1, :]
    bias = jnp.where(flags > 0.5, F32(0.0), F32(FAR))
    if self_mask is not None:
        bias = jnp.where(self_mask, F32(0.0), bias)
    return raw + bias


def level(query, block_ref, self_masks):
    parts = [scores(query, block_ref, c, self_masks[c]) for c in range(PEERS)]
    best = functools.reduce(jnp.maximum, parts)
    top = jnp.max(best, axis=1, keepdims=True)
    sums = None
    mixture = None
    for c in range(PEERS):
        weight = jnp.exp2((parts[c] - top) * F32(EXP_SCALE))
        sums = weight if sums is None else sums + weight
        add = jnp.dot(weight.astype(BF16), block_ref[c, 0:ROWS, :], preferred_element_type=F32)
        mixture = add if mixture is None else mixture + add
    total = jnp.sum(sums, axis=1, keepdims=True)
    lane = lanes(mixture.shape)
    return jnp.where(lane < 32, top, jnp.where(lane < 64, total, mixture))


def merge(one, two):
    top_one, top_two = one[:, 0:1], two[:, 0:1]
    top = jnp.maximum(top_one, top_two)
    scale_one = jnp.exp2((top_one - top) * F32(EXP_SCALE))
    scale_two = jnp.exp2((top_two - top) * F32(EXP_SCALE))
    both = one * scale_one + two * scale_two
    return jnp.where(lanes(both.shape) < 32, top, both)


def divided(state):
    return state / state[:, 32:33]


def pack_kernel(query_hbm, key_hbm, value_hbm, valid_hbm, out_ref, query_ref, key_ref, value_ref, valid_ref, sems):
    pairs = (
        (valid_hbm, valid_ref),
        (key_hbm, key_ref),
        (value_hbm, value_ref),
        (query_hbm, query_ref),
    )
    copies = [pltpu.make_async_copy(a, b, sems.at[i]) for i, (a, b) in enumerate(pairs)]
    for copy in copies:
        copy.start()
    for h in range(HEADS, PEERS):
        out_ref[h] = jnp.zeros((FIRST_BLOCK, 2 * HD), BF16)
    for copy in copies:
        copy.wait()
    flags = jnp.broadcast_to(valid_ref[...].astype(F32), (FLAG_ROWS, ROWS)).astype(BF16)
    half = ROWS // 2
    for h in range(HEADS):
        at = slice(h * HD, (h + 1) * HD)
        out_ref[h, 0:ROWS, 0:HD] = key_ref[:, at]
        out_ref[h, 0:ROWS, HD : 2 * HD] = value_ref[:, at]
        out_ref[h, ROWS:KEY_BLOCK, :] = flags
        out_ref[h, KEY_BLOCK:FIRST_BLOCK, 0:HD] = query_ref[0:half, at]
        out_ref[h, KEY_BLOCK:FIRST_BLOCK, HD : 2 * HD] = query_ref[half:ROWS, at]


def pick_kernel(which, offsets_ref, blocks_ref, out_ref):
    shift = shifts(offsets_ref)[which]
    count = ROWS // 8
    shape = (count, ROWS)
    selector = (lanes(shape) == shift + 8 * rows(shape)).astype(F32).astype(BF16)
    flag_rows = jnp.zeros((PEERS, ROWS), F32)
    for c in range(PEERS):
        picked = jnp.dot(selector, blocks_ref[c, 0:ROWS, :], preferred_element_type=F32).astype(BF16)
        for d in range(PEERS):
            out_ref[d, c * count : (c + 1) * count, :] = picked
        flags = blocks_ref[c, ROWS:KEY_BLOCK, :].astype(F32)[0:PEERS, :]
        flag_rows = jnp.where(rows((PEERS, ROWS)) == c, flags, flag_rows)
    square = (ROWS, ROWS)
    chosen = rows(square) == shift + 8 * (lanes(square) % count)
    spread = jnp.dot(
        flag_rows.astype(BF16), chosen.astype(F32).astype(BF16), preferred_element_type=F32
    )
    own = rows((PEERS, ROWS)) == lanes((PEERS, ROWS)) // count
    flags = jnp.sum(jnp.where(own, spread, F32(0.0)), axis=0, keepdims=True)
    flags = jnp.broadcast_to(flags, (FLAG_ROWS, ROWS)).astype(BF16)
    for d in range(PEERS):
        out_ref[d, ROWS:KEY_BLOCK, :] = flags


def first_kernel(offsets_ref, blocks_ref, state_ref, middle_ref, outer_ref, wide, narrow):
    middle, stride = shifts(offsets_ref)
    half = ROWS // 2
    low = lanes((half, 2 * HD)) < HD
    diagonal = rows((ROWS, ROWS)) == lanes((ROWS, ROWS))
    for j in range(PEERS):
        pair = blocks_ref[j, KEY_BLOCK:FIRST_BLOCK, :].astype(F32)
        wide[j * ROWS : j * ROWS + half, :] = jnp.where(low, pair, F32(0.0))
        wide[j * ROWS + half : (j + 1) * ROWS, :] = jnp.where(
            low, pltpu.roll(pair, HD, 1), F32(0.0)
        )
        query = wide[j * ROWS : (j + 1) * ROWS, :].astype(BF16)
        masks = [diagonal if c == j else None for c in range(PEERS)]
        state_ref[j * ROWS : (j + 1) * ROWS, :] = level(query, blocks_ref, masks)
    picked = wide[pl.ds(middle, ROWS, stride=8), :]
    middle_ref[...] = picked.astype(BF16)
    narrow[...] = picked
    outer_ref[...] = narrow[pl.ds(stride, ROWS // 8, stride=8), :].astype(BF16)


def middle_kernel(offsets_ref, state_ref, query_ref, blocks_ref, out_ref, merged_ref, wide):
    middle, _ = shifts(offsets_ref)
    mine = lax.axis_index("blk")
    diagonal = rows((ROWS, ROWS)) == lanes((ROWS, ROWS))
    masks = [diagonal & (mine == c) for c in range(PEERS)]
    found = level(query_ref[...], blocks_ref, masks)
    both = merge(state_ref[pl.ds(middle, ROWS, stride=8), :], found)
    merged_ref[...] = both
    wide[...] = state_ref[...]
    wide[pl.ds(middle, ROWS, stride=8), :] = both
    half = ROWS // 2
    low = lanes((half, 2 * HD)) < HD
    for j in range(PEERS):
        one = divided(wide[j * ROWS : j * ROWS + half, :])
        two = divided(wide[j * ROWS + half : (j + 1) * ROWS, :])
        out_ref[j] = jnp.where(low, pltpu.roll(one, HD, 1), two).astype(BF16)


def outer_kernel(offsets_ref, merged_ref, query_ref, blocks_ref, before_ref, out_ref):
    middle, stride = shifts(offsets_ref)
    block, group = lax.axis_index("blk"), lax.axis_index("grp")
    count = ROWS // 8
    shape = (count, ROWS)
    diagonal = lanes(shape) == block * count + rows(shape)
    masks = [diagonal & (group == c) for c in range(PEERS)]
    found = level(query_ref[...], blocks_ref, masks)
    both = divided(merge(merged_ref[pl.ds(stride, count, stride=8), :], found))
    turned = pltpu.roll(both, HD, 1)
    tile = 16
    token = middle + 8 * stride
    start = pl.multiple_of((token // tile) * tile, tile)
    here = rows((tile, 2 * HD)) == token - start
    low = lanes((1, 2 * HD)) < HD
    for j in range(PEERS):
        row = jnp.where(low, turned[2 * j : 2 * j + 1, :], both[2 * j + 1 : 2 * j + 2, :])
        kept = before_ref[j, pl.ds(start, tile), :].astype(F32)
        out_ref[j, pl.ds(start, tile), :] = jnp.where(here, row, kept).astype(BF16)


def project_kernel(blocks_ref, weight_ref, out_ref):
    half = ROWS // 2
    low = lanes((half, 2 * HD)) < HD
    tops, bottoms = [], []
    for h in range(0, HEADS, 2):
        one, two = blocks_ref[h].astype(F32), blocks_ref[h + 1].astype(F32)
        tops.append(jnp.where(low, one, pltpu.roll(two, HD, 1)).astype(BF16))
        bottoms.append(jnp.where(low, pltpu.roll(one, HD, 1), two).astype(BF16))
    combined = jnp.concatenate(
        [jnp.concatenate(tops, axis=1), jnp.concatenate(bottoms, axis=1)], axis=0
    )
    out_ref[...] = jnp.dot(combined, weight_ref[...], preferred_element_type=F32).astype(BF16)


def call(kernel, name, out_shape, in_specs, scratch=(), flops=0, moved=0, aliases=None):
    outs = jax.tree.map(lambda _: VMEM, out_shape)
    return pl.pallas_call(
        kernel,
        name=name,
        out_shape=out_shape,
        in_specs=in_specs,
        out_specs=outs,
        scratch_shapes=list(scratch),
        input_output_aliases=aliases or {},
        compiler_params=pltpu.CompilerParams(vmem_limit_bytes=40 * 2**20),
        cost_estimate=pl.CostEstimate(flops=flops, bytes_accessed=moved, transcendentals=0),
    )


def shaped(*shape, dtype=BF16):
    return jax.ShapeDtypeStruct(shape, dtype)


def per_device(queries, keys, values, valid, offsets, w_out):
    wide = pltpu.VMEM((PEERS * ROWS, 2 * HD), F32)
    narrow = pltpu.VMEM((ROWS, 2 * HD), F32)
    swap = functools.partial(lax.all_to_all, split_axis=0, concat_axis=0, tiled=True)

    whole = pltpu.VMEM((ROWS, HEADS * HD), BF16)
    given = (queries, keys, values, valid.reshape(1, ROWS))
    packed = call(
        pack_kernel,
        "pack",
        shaped(PEERS, FIRST_BLOCK, 2 * HD),
        [HBM] * 4,
        [whole, whole, whole, pltpu.VMEM((1, ROWS), jnp.int32), pltpu.SemaphoreType.DMA((4,))],
    )(*(pltpu.with_memory_space_constraint(a, pltpu.HBM) for a in given))
    dense = swap(packed, "set")

    def pick(which, name, blocks):
        return call(
            functools.partial(pick_kernel, which),
            name,
            shaped(PEERS, KEY_BLOCK, 2 * HD),
            [VMEM, VMEM],
        )(offsets, blocks)

    middle_blocks = swap(pick(0, "pick_middle", dense), "blk")
    state, middle_query, outer_query = call(
        first_kernel,
        "first",
        (shaped(PEERS * ROWS, 2 * HD, dtype=F32), shaped(ROWS, 2 * HD), shaped(ROWS // 8, 2 * HD)),
        [VMEM, VMEM],
        [wide, narrow],
        flops=6_000_000_000,
        moved=2_000_000,
    )(offsets, dense)
    outer_blocks = swap(pick(1, "pick_outer", middle_blocks), "grp")
    before, merged = call(
        middle_kernel,
        "middle",
        (shaped(PEERS, ROWS // 2, 2 * HD), shaped(ROWS, 2 * HD, dtype=F32)),
        [VMEM, VMEM, VMEM, VMEM],
        [wide],
        flops=2_000_000_000,
        moved=2_000_000,
    )(offsets, state, middle_query, middle_blocks)
    combined = call(
        outer_kernel,
        "outer",
        shaped(PEERS, ROWS // 2, 2 * HD),
        [VMEM, VMEM, VMEM, VMEM, VMEM],
        aliases={4: 0},
    )(offsets, merged, outer_query, outer_blocks, before)
    home = swap(combined, "set")
    return call(project_kernel, "project", shaped(ROWS, 768), [VMEM, VMEM])(home, w_out)


def solution(mesh):
    spread = P(("grp", "blk", "set"), None)
    return jax.shard_map(
        per_device,
        mesh=mesh,
        in_specs=(spread, spread, spread, P(("grp", "blk", "set")), P(), P()),
        out_specs=spread,
        check_vma=False,
    )
```

```python
import functools
import math

import jax
import jax.numpy as jnp
from jax import lax
from jax.experimental import pallas as pl
from jax.experimental.pallas import tpu as pltpu
from jax.sharding import PartitionSpec as P

HEADS = 6
HD = 64
PEERS = 8
ROWS = 128
FIRST_BLOCK = ROWS + ROWS // 2
MARK = 1024.0
EXP_SCALE = math.log2(math.e) / math.sqrt(HD)
FAR = -1e30
F32 = jnp.float32
BF16 = jnp.bfloat16

VMEM = pl.BlockSpec(memory_space=pltpu.VMEM)
HBM = pl.BlockSpec(memory_space=pltpu.HBM)


def lanes(shape):
    return lax.broadcasted_iota(jnp.int32, shape, len(shape) - 1)


def rows(shape):
    return lax.broadcasted_iota(jnp.int32, shape, len(shape) - 2)


def my_head():
    return jnp.minimum(lax.axis_index("set"), HEADS - 1)


def shifts(offsets_ref):
    both = offsets_ref[...].astype(F32)
    both = jnp.where(lanes(both.shape) == my_head(), both, F32(0.0))
    middle = jnp.sum(both[0:1, :]).astype(jnp.int32)
    outer = jnp.sum(both[1:2, :]).astype(jnp.int32)
    return middle, (outer - middle) // 8


def marks():
    shape = (16, 2 * HD)
    row, lane = rows(shape), lanes(shape)
    chosen = ((row == 0) & (lane == 0)) | ((row == 1) & (lane >= 1) & (lane <= 3))
    return chosen.astype(F32).astype(BF16)


def against(query, block_ref, index):
    return lax.dot_general(
        query, block_ref[index, 0:ROWS, :], (((1,), (1,)), ((), ())), preferred_element_type=F32
    )


def level(query, block_ref, self_masks, seen=None):
    count = query.shape[0]
    parts = []
    if seen is None:
        query = jnp.concatenate([query, marks()], axis=0)
    for c in range(PEERS):
        part = against(query, block_ref, c)
        seen_part = part[count:, :] if seen is None else seen[c]
        hidden = seen_part[0:1, :] > F32(MARK / 2)
        masked = part[0:count, :] + jnp.where(hidden, F32(FAR), F32(0.0))
        if self_masks[c] is not None:
            masked = jnp.where(self_masks[c] & hidden, seen_part[1:2, :], masked)
        parts.append(masked)
    best = functools.reduce(jnp.maximum, parts)
    top = jnp.max(best, axis=1, keepdims=True)
    sums = None
    mixture = None
    for c in range(PEERS):
        weight = jnp.exp2((parts[c] - top) * F32(EXP_SCALE))
        sums = weight if sums is None else sums + weight
        add = jnp.dot(weight.astype(BF16), block_ref[c, 0:ROWS, :], preferred_element_type=F32)
        mixture = add if mixture is None else mixture + add
    total = jnp.sum(sums, axis=1, keepdims=True)
    lane = lanes(mixture.shape)
    return jnp.where(lane < 32, top, jnp.where(lane < 64, total, mixture))


def merge(one, two):
    top_one, top_two = one[:, 0:1], two[:, 0:1]
    top = jnp.maximum(top_one, top_two)
    scale_one = jnp.exp2((top_one - top) * F32(EXP_SCALE))
    scale_two = jnp.exp2((top_two - top) * F32(EXP_SCALE))
    both = one * scale_one + two * scale_two
    return jnp.where(lanes(both.shape) < 32, top, both)


def divided(state):
    return state / state[:, 32:33]


def pack_kernel(query_hbm, key_hbm, value_hbm, valid_hbm, out_ref, query_ref, key_ref, value_ref, valid_ref, sems):
    pairs = (
        (valid_hbm, valid_ref),
        (key_hbm, key_ref),
        (value_hbm, value_ref),
        (query_hbm, query_ref),
    )
    copies = [pltpu.make_async_copy(a, b, sems.at[i]) for i, (a, b) in enumerate(pairs)]
    for copy in copies:
        copy.start()
    for h in range(HEADS, PEERS):
        out_ref[h] = jnp.zeros((FIRST_BLOCK, 2 * HD), BF16)
    for copy in copies:
        copy.wait()
    square = (ROWS, ROWS)
    valid = jnp.where(rows(square) == lanes(square), valid_ref[...].astype(F32), F32(0.0))
    hidden = jnp.sum(valid, axis=1, keepdims=True) < F32(0.5)
    half = ROWS // 2
    lane = lanes((ROWS, HD))
    for h in range(HEADS):
        at = slice(h * HD, (h + 1) * HD)
        key = key_ref[:, at].astype(F32)
        own = jnp.sum(query_ref[:, at].astype(F32) * key, axis=1, keepdims=True)
        high = own.astype(BF16).astype(F32)
        middle = (own - high).astype(BF16).astype(F32)
        rest = own - high - middle
        code = jnp.where(lane == 0, F32(MARK), jnp.where(lane == 1, high, F32(0.0)))
        code = jnp.where(lane == 2, middle, jnp.where(lane == 3, rest, code))
        out_ref[h, 0:ROWS, 0:HD] = jnp.where(hidden, code, key).astype(BF16)
        out_ref[h, 0:ROWS, HD : 2 * HD] = value_ref[:, at]
        out_ref[h, ROWS:FIRST_BLOCK, 0:HD] = query_ref[0:half, at]
        out_ref[h, ROWS:FIRST_BLOCK, HD : 2 * HD] = query_ref[half:ROWS, at]


def pick_kernel(which, offsets_ref, blocks_ref, out_ref):
    shift = shifts(offsets_ref)[which]
    count = ROWS // 8
    shape = (count, ROWS)
    selector = (lanes(shape) == shift + 8 * rows(shape)).astype(F32).astype(BF16)
    for c in range(PEERS):
        picked = jnp.dot(selector, blocks_ref[c, 0:ROWS, :], preferred_element_type=F32).astype(BF16)
        for d in range(PEERS):
            out_ref[d, c * count : (c + 1) * count, :] = picked


def first_kernel(offsets_ref, blocks_ref, state_ref, middle_ref, outer_ref, wide, narrow):
    middle, stride = shifts(offsets_ref)
    half = ROWS // 2
    low = lanes((half, 2 * HD)) < HD
    diagonal = rows((ROWS, ROWS)) == lanes((ROWS, ROWS))
    reader = marks()
    seen = [against(reader, blocks_ref, c) for c in range(PEERS)]
    for j in range(PEERS):
        pair = blocks_ref[j, ROWS:FIRST_BLOCK, :].astype(F32)
        wide[j * ROWS : j * ROWS + half, :] = jnp.where(low, pair, F32(0.0))
        wide[j * ROWS + half : (j + 1) * ROWS, :] = jnp.where(
            low, pltpu.roll(pair, HD, 1), F32(0.0)
        )
        query = wide[j * ROWS : (j + 1) * ROWS, :].astype(BF16)
        masks = [diagonal if c == j else None for c in range(PEERS)]
        state_ref[j * ROWS : (j + 1) * ROWS, :] = level(query, blocks_ref, masks, seen)
    picked = wide[pl.ds(middle, ROWS, stride=8), :]
    middle_ref[...] = picked.astype(BF16)
    narrow[...] = picked
    outer_ref[...] = narrow[pl.ds(stride, ROWS // 8, stride=8), :].astype(BF16)


def middle_kernel(offsets_ref, state_ref, query_ref, blocks_ref, out_ref, merged_ref, wide):
    middle, _ = shifts(offsets_ref)
    mine = lax.axis_index("blk")
    diagonal = rows((ROWS, ROWS)) == lanes((ROWS, ROWS))
    masks = [diagonal & (mine == c) for c in range(PEERS)]
    found = level(query_ref[...], blocks_ref, masks)
    both = merge(state_ref[pl.ds(middle, ROWS, stride=8), :], found)
    merged_ref[...] = both
    wide[...] = state_ref[...]
    wide[pl.ds(middle, ROWS, stride=8), :] = both
    half = ROWS // 2
    low = lanes((half, 2 * HD)) < HD
    for j in range(PEERS):
        one = divided(wide[j * ROWS : j * ROWS + half, :])
        two = divided(wide[j * ROWS + half : (j + 1) * ROWS, :])
        out_ref[j] = jnp.where(low, pltpu.roll(one, HD, 1), two).astype(BF16)


def outer_kernel(offsets_ref, merged_ref, query_ref, blocks_ref, before_ref, out_ref):
    middle, stride = shifts(offsets_ref)
    block, group = lax.axis_index("blk"), lax.axis_index("grp")
    count = ROWS // 8
    shape = (count, ROWS)
    diagonal = lanes(shape) == block * count + rows(shape)
    masks = [diagonal & (group == c) for c in range(PEERS)]
    found = level(query_ref[...], blocks_ref, masks)
    both = divided(merge(merged_ref[pl.ds(stride, count, stride=8), :], found))
    turned = pltpu.roll(both, HD, 1)
    tile = 16
    token = middle + 8 * stride
    start = pl.multiple_of((token // tile) * tile, tile)
    here = rows((tile, 2 * HD)) == token - start
    low = lanes((1, 2 * HD)) < HD
    for j in range(PEERS):
        row = jnp.where(low, turned[2 * j : 2 * j + 1, :], both[2 * j + 1 : 2 * j + 2, :])
        kept = before_ref[j, pl.ds(start, tile), :].astype(F32)
        out_ref[j, pl.ds(start, tile), :] = jnp.where(here, row, kept).astype(BF16)


def project_kernel(blocks_ref, weight_ref, out_ref):
    half = ROWS // 2
    low = lanes((half, 2 * HD)) < HD
    tops, bottoms = [], []
    for h in range(0, HEADS, 2):
        one, two = blocks_ref[h].astype(F32), blocks_ref[h + 1].astype(F32)
        tops.append(jnp.where(low, one, pltpu.roll(two, HD, 1)).astype(BF16))
        bottoms.append(jnp.where(low, pltpu.roll(one, HD, 1), two).astype(BF16))
    combined = jnp.concatenate(
        [jnp.concatenate(tops, axis=1), jnp.concatenate(bottoms, axis=1)], axis=0
    )
    out_ref[...] = jnp.dot(combined, weight_ref[...], preferred_element_type=F32).astype(BF16)


def call(kernel, name, out_shape, in_specs, scratch=(), flops=0, moved=0, aliases=None):
    outs = jax.tree.map(lambda _: VMEM, out_shape)
    return pl.pallas_call(
        kernel,
        name=name,
        out_shape=out_shape,
        in_specs=in_specs,
        out_specs=outs,
        scratch_shapes=list(scratch),
        input_output_aliases=aliases or {},
        compiler_params=pltpu.CompilerParams(vmem_limit_bytes=40 * 2**20),
        cost_estimate=pl.CostEstimate(flops=flops, bytes_accessed=moved, transcendentals=0),
    )


def shaped(*shape, dtype=BF16):
    return jax.ShapeDtypeStruct(shape, dtype)


def per_device(queries, keys, values, valid, offsets, w_out):
    wide = pltpu.VMEM((PEERS * ROWS, 2 * HD), F32)
    narrow = pltpu.VMEM((ROWS, 2 * HD), F32)
    swap = functools.partial(lax.all_to_all, split_axis=0, concat_axis=0, tiled=True)

    whole = pltpu.VMEM((ROWS, HEADS * HD), BF16)
    given = (queries, keys, values, valid.reshape(1, ROWS))
    packed = call(
        pack_kernel,
        "pack",
        shaped(PEERS, FIRST_BLOCK, 2 * HD),
        [HBM] * 4,
        [whole, whole, whole, pltpu.VMEM((1, ROWS), jnp.int32), pltpu.SemaphoreType.DMA((4,))],
    )(*(pltpu.with_memory_space_constraint(a, pltpu.HBM) for a in given))
    dense = swap(packed, "set")

    def pick(which, name, blocks):
        return call(
            functools.partial(pick_kernel, which),
            name,
            shaped(PEERS, ROWS, 2 * HD),
            [VMEM, VMEM],
        )(offsets, blocks)

    middle_blocks = swap(pick(0, "pick_middle", dense), "blk")
    state, middle_query, outer_query = call(
        first_kernel,
        "first",
        (shaped(PEERS * ROWS, 2 * HD, dtype=F32), shaped(ROWS, 2 * HD), shaped(ROWS // 8, 2 * HD)),
        [VMEM, VMEM],
        [wide, narrow],
        flops=6_000_000_000,
        moved=2_000_000,
    )(offsets, dense)
    outer_blocks = swap(pick(1, "pick_outer", middle_blocks), "grp")
    before, merged = call(
        middle_kernel,
        "middle",
        (shaped(PEERS, ROWS // 2, 2 * HD), shaped(ROWS, 2 * HD, dtype=F32)),
        [VMEM, VMEM, VMEM, VMEM],
        [wide],
        flops=2_000_000_000,
        moved=2_000_000,
    )(offsets, state, middle_query, middle_blocks)
    combined = call(
        outer_kernel,
        "outer",
        shaped(PEERS, ROWS // 2, 2 * HD),
        [VMEM, VMEM, VMEM, VMEM, VMEM],
        aliases={4: 0},
    )(offsets, merged, outer_query, outer_blocks, before)
    home = swap(combined, "set")
    return call(project_kernel, "project", shaped(ROWS, 768), [VMEM, VMEM])(home, w_out)


def solution(mesh):
    spread = P(("grp", "blk", "set"), None)
    return jax.shard_map(
        per_device,
        mesh=mesh,
        in_specs=(spread, spread, spread, P(("grp", "blk", "set")), P(), P()),
        out_specs=spread,
        check_vma=False,
    )
```

```python
import functools
import math

import jax
import jax.numpy as jnp
from jax import lax
from jax.experimental import pallas as pl
from jax.experimental.pallas import tpu as pltpu
from jax.sharding import PartitionSpec as P

HEADS = 6
HD = 64
PEERS = 8
ROWS = 128
FIRST_BLOCK = ROWS + ROWS // 2
MARK = 1024.0
EXP_SCALE = math.log2(math.e) / math.sqrt(HD)
FAR = -1e30
THIRD = 256
F32 = jnp.float32
BF16 = jnp.bfloat16

VMEM = pl.BlockSpec(memory_space=pltpu.VMEM)
HBM = pl.BlockSpec(memory_space=pltpu.HBM)


def lanes(shape):
    return lax.broadcasted_iota(jnp.int32, shape, len(shape) - 1)


def rows(shape):
    return lax.broadcasted_iota(jnp.int32, shape, len(shape) - 2)


def my_head():
    return jnp.minimum(lax.axis_index("set"), HEADS - 1)


def shifts(offsets_ref):
    both = offsets_ref[...].astype(F32)
    both = jnp.where(lanes(both.shape) == my_head(), both, F32(0.0))
    middle = jnp.sum(both[0:1, :]).astype(jnp.int32)
    outer = jnp.sum(both[1:2, :]).astype(jnp.int32)
    return middle, (outer - middle) // 8


def marks():
    shape = (16, 2 * HD)
    row, lane = rows(shape), lanes(shape)
    chosen = ((row == 0) & (lane == 0)) | ((row == 1) & (lane >= 1) & (lane <= 3))
    return chosen.astype(F32).astype(BF16)


def against(query, block_ref, index):
    return lax.dot_general(
        query, block_ref[index, 0:ROWS, :], (((1,), (1,)), ((), ())), preferred_element_type=F32
    )


def level(query, block_ref, self_masks, seen=None):
    count = query.shape[0]
    parts = []
    if seen is None:
        query = jnp.concatenate([query, marks()], axis=0)
    for c in range(PEERS):
        part = against(query, block_ref, c)
        seen_part = part[count:, :] if seen is None else seen[c]
        hidden = seen_part[0:1, :] > F32(MARK / 2)
        masked = part[0:count, :] + jnp.where(hidden, F32(FAR), F32(0.0))
        if self_masks[c] is not None:
            masked = jnp.where(self_masks[c] & hidden, seen_part[1:2, :], masked)
        parts.append(masked)
    best = functools.reduce(jnp.maximum, parts)
    top = jnp.max(best, axis=1, keepdims=True)
    sums = None
    mixture = None
    for c in range(PEERS):
        weight = jnp.exp2((parts[c] - top) * F32(EXP_SCALE))
        sums = weight if sums is None else sums + weight
        add = jnp.dot(weight.astype(BF16), block_ref[c, 0:ROWS, :], preferred_element_type=F32)
        mixture = add if mixture is None else mixture + add
    total = jnp.sum(sums, axis=1, keepdims=True)
    lane = lanes(mixture.shape)
    return jnp.where(lane < 32, top, jnp.where(lane < 64, total, mixture))


def merge(one, two):
    top_one, top_two = one[:, 0:1], two[:, 0:1]
    top = jnp.maximum(top_one, top_two)
    scale_one = jnp.exp2((top_one - top) * F32(EXP_SCALE))
    scale_two = jnp.exp2((top_two - top) * F32(EXP_SCALE))
    both = one * scale_one + two * scale_two
    return jnp.where(lanes(both.shape) < 32, top, both)


def divided(state):
    return state / state[:, 32:33]


def product_of(one, two):
    return jnp.dot(one, two, preferred_element_type=F32)


def pack_kernel(query_hbm, key_hbm, value_hbm, valid_hbm, out_ref, query_ref, key_ref, value_ref, valid_ref, sems):
    pairs = (
        (valid_hbm, valid_ref),
        (key_hbm, key_ref),
        (value_hbm, value_ref),
        (query_hbm, query_ref),
    )
    copies = [pltpu.make_async_copy(a, b, sems.at[i]) for i, (a, b) in enumerate(pairs)]
    for copy in copies:
        copy.start()
    for h in range(HEADS, PEERS):
        out_ref[h] = jnp.zeros((FIRST_BLOCK, 2 * HD), BF16)
    for copy in copies:
        copy.wait()
    square = (ROWS, 2 * HD)
    row, lane = rows(square), lanes(square)
    valid = jnp.where(row == lane, valid_ref[...].astype(F32), F32(0.0)).astype(BF16)
    hidden = product_of(valid, jnp.ones(square, BF16)) < F32(0.5)
    same_head = ((row // HD) == (lane // HD)).astype(F32).astype(BF16)
    column = lane % HD
    half = ROWS // 2
    for h in range(0, HEADS, 2):
        at = slice(h * HD, (h + 2) * HD)
        key = key_ref[:, at].astype(F32)
        product = query_ref[:, at].astype(F32) * key
        upper = product.astype(BF16)
        lower = (product - upper.astype(F32)).astype(BF16)
        own = product_of(upper, same_head) + product_of(lower, same_head)
        high = own.astype(BF16).astype(F32)
        middle = (own - high).astype(BF16).astype(F32)
        rest = own - high - middle
        code = jnp.where(column == 0, F32(MARK), jnp.where(column == 1, high, F32(0.0)))
        code = jnp.where(column == 2, middle, jnp.where(column == 3, rest, code))
        coded = jnp.where(hidden, code, key).astype(BF16)
        for part in range(2):
            inner = slice(part * HD, (part + 1) * HD)
            at = slice((h + part) * HD, (h + part + 1) * HD)
            out_ref[h + part, 0:ROWS, 0:HD] = coded[:, inner]
            out_ref[h + part, 0:ROWS, HD : 2 * HD] = value_ref[:, at]
            out_ref[h + part, ROWS:FIRST_BLOCK, 0:HD] = query_ref[0:half, at]
            out_ref[h + part, ROWS:FIRST_BLOCK, HD : 2 * HD] = query_ref[half:ROWS, at]


def selector_of(shift):
    shape = (ROWS // 8, ROWS)
    return (lanes(shape) == shift + 8 * rows(shape)).astype(F32).astype(BF16)


def pick_middle_kernel(offsets_ref, blocks_ref, out_ref):
    selector = selector_of(shifts(offsets_ref)[0])
    count = ROWS // 8
    for c in range(PEERS):
        picked = product_of(selector, blocks_ref[c, 0:ROWS, :]).astype(BF16)
        for d in range(PEERS):
            out_ref[d, c * count : (c + 1) * count, :] = picked


def pick_outer_kernel(offsets_ref, blocks_ref, out_hbm, picked_ref, sems):
    selector = selector_of(shifts(offsets_ref)[1])
    count = ROWS // 8
    for c in range(PEERS):
        picked = product_of(selector, blocks_ref[c, 0:ROWS, :]).astype(BF16)
        picked_ref[c * count : (c + 1) * count, :] = picked
    copies = [pltpu.make_async_copy(picked_ref, out_hbm.at[d], sems.at[d]) for d in range(PEERS)]
    for copy in copies:
        copy.start()
    for copy in copies:
        copy.wait()


def first_kernel(offsets_ref, blocks_ref, state_ref, middle_ref, outer_ref, wide, narrow):
    middle, stride = shifts(offsets_ref)
    half = ROWS // 2
    low = lanes((half, 2 * HD)) < HD
    diagonal = rows((ROWS, ROWS)) == lanes((ROWS, ROWS))
    reader = marks()
    seen = [against(reader, blocks_ref, c) for c in range(PEERS)]
    for j in range(PEERS):
        pair = blocks_ref[j, ROWS:FIRST_BLOCK, :].astype(F32)
        wide[j * ROWS : j * ROWS + half, :] = jnp.where(low, pair, F32(0.0))
        wide[j * ROWS + half : (j + 1) * ROWS, :] = jnp.where(
            low, pltpu.roll(pair, HD, 1), F32(0.0)
        )
        query = wide[j * ROWS : (j + 1) * ROWS, :].astype(BF16)
        masks = [diagonal if c == j else None for c in range(PEERS)]
        state_ref[j * ROWS : (j + 1) * ROWS, :] = level(query, blocks_ref, masks, seen)
    picked = wide[pl.ds(middle, ROWS, stride=8), :]
    middle_ref[...] = picked.astype(BF16)
    narrow[...] = picked
    outer_ref[...] = narrow[pl.ds(stride, ROWS // 8, stride=8), :].astype(BF16)


def middle_kernel(offsets_ref, state_ref, query_ref, blocks_ref, out_ref, merged_ref, wide):
    middle, _ = shifts(offsets_ref)
    mine = lax.axis_index("blk")
    diagonal = rows((ROWS, ROWS)) == lanes((ROWS, ROWS))
    masks = [diagonal & (mine == c) for c in range(PEERS)]
    found = level(query_ref[...], blocks_ref, masks)
    both = merge(state_ref[pl.ds(middle, ROWS, stride=8), :], found)
    merged_ref[...] = both
    wide[...] = state_ref[...]
    wide[pl.ds(middle, ROWS, stride=8), :] = both
    half = ROWS // 2
    low = lanes((half, 2 * HD)) < HD
    for j in range(PEERS):
        one = divided(wide[j * ROWS : j * ROWS + half, :])
        two = divided(wide[j * ROWS + half : (j + 1) * ROWS, :])
        out_ref[j] = jnp.where(low, pltpu.roll(one, HD, 1), two).astype(BF16)


def outer_kernel(offsets_ref, merged_ref, query_ref, blocks_ref, before_ref, out_ref):
    middle, stride = shifts(offsets_ref)
    block, group = lax.axis_index("blk"), lax.axis_index("grp")
    count = ROWS // 8
    shape = (count, ROWS)
    diagonal = lanes(shape) == block * count + rows(shape)
    masks = [diagonal & (group == c) for c in range(PEERS)]
    found = level(query_ref[...], blocks_ref, masks)
    both = divided(merge(merged_ref[pl.ds(stride, count, stride=8), :], found))
    turned = pltpu.roll(both, HD, 1)
    tile = 16
    token = middle + 8 * stride
    start = pl.multiple_of((token // tile) * tile, tile)
    here = rows((tile, 2 * HD)) == token - start
    low = lanes((1, 2 * HD)) < HD
    for j in range(PEERS):
        row = jnp.where(low, turned[2 * j : 2 * j + 1, :], both[2 * j + 1 : 2 * j + 2, :])
        kept = before_ref[j, pl.ds(start, tile), :].astype(F32)
        out_ref[j, pl.ds(start, tile), :] = jnp.where(here, row, kept).astype(BF16)


def project_kernel(blocks_ref, weight_ref, out_hbm, out_ref, sems):
    half = ROWS // 2
    low = lanes((half, 2 * HD)) < HD
    tops, bottoms = [], []
    for h in range(0, HEADS, 2):
        one, two = blocks_ref[h].astype(F32), blocks_ref[h + 1].astype(F32)
        tops.append(jnp.where(low, one, pltpu.roll(two, HD, 1)).astype(BF16))
        bottoms.append(jnp.where(low, pltpu.roll(one, HD, 1), two).astype(BF16))
    combined = jnp.concatenate(
        [jnp.concatenate(tops, axis=1), jnp.concatenate(bottoms, axis=1)], axis=0
    )
    copies = []
    for n in range(out_ref.shape[1] // THIRD):
        at = slice(n * THIRD, (n + 1) * THIRD)
        out_ref[:, at] = product_of(combined, weight_ref[:, at]).astype(BF16)
        copies.append(pltpu.make_async_copy(out_ref.at[:, at], out_hbm.at[:, at], sems.at[n]))
        copies[-1].start()
    for copy in copies:
        copy.wait()


def call(kernel, name, out_shape, in_specs, scratch=(), flops=0, moved=0, aliases=None, out_spec=VMEM):
    outs = jax.tree.map(lambda _: out_spec, out_shape)
    return pl.pallas_call(
        kernel,
        name=name,
        out_shape=out_shape,
        in_specs=in_specs,
        out_specs=outs,
        scratch_shapes=list(scratch),
        input_output_aliases=aliases or {},
        compiler_params=pltpu.CompilerParams(vmem_limit_bytes=40 * 2**20),
        cost_estimate=pl.CostEstimate(flops=flops, bytes_accessed=moved, transcendentals=0),
    )


def shaped(*shape, dtype=BF16):
    return jax.ShapeDtypeStruct(shape, dtype)


def per_device(queries, keys, values, valid, offsets, w_out):
    wide = pltpu.VMEM((PEERS * ROWS, 2 * HD), F32)
    narrow = pltpu.VMEM((ROWS, 2 * HD), F32)
    swap = functools.partial(lax.all_to_all, split_axis=0, concat_axis=0, tiled=True)

    whole = pltpu.VMEM((ROWS, HEADS * HD), BF16)
    given = (queries, keys, values, valid.reshape(1, ROWS))
    packed = call(
        pack_kernel,
        "pack",
        shaped(PEERS, FIRST_BLOCK, 2 * HD),
        [HBM] * 4,
        [whole, whole, whole, pltpu.VMEM((1, ROWS), jnp.int32), pltpu.SemaphoreType.DMA((4,))],
    )(*(pltpu.with_memory_space_constraint(a, pltpu.HBM) for a in given))
    dense = swap(packed, "set")

    middle_send = call(
        pick_middle_kernel, "pick_middle", shaped(PEERS, ROWS, 2 * HD), [VMEM, VMEM]
    )(offsets, dense)
    middle_blocks = swap(middle_send, "blk")
    state, middle_query, outer_query = call(
        first_kernel,
        "first",
        (shaped(PEERS * ROWS, 2 * HD, dtype=F32), shaped(ROWS, 2 * HD), shaped(ROWS // 8, 2 * HD)),
        [VMEM, VMEM],
        [wide, narrow],
        flops=6_000_000_000,
        moved=2_000_000,
    )(offsets, dense)
    outer_send = call(
        pick_outer_kernel,
        "pick_outer",
        shaped(PEERS, ROWS, 2 * HD),
        [VMEM, VMEM],
        [pltpu.VMEM((ROWS, 2 * HD), BF16), pltpu.SemaphoreType.DMA((PEERS,))],
        out_spec=HBM,
    )(offsets, middle_blocks)
    outer_blocks = swap(outer_send, "grp")
    before, merged = call(
        middle_kernel,
        "middle",
        (shaped(PEERS, ROWS // 2, 2 * HD), shaped(ROWS, 2 * HD, dtype=F32)),
        [VMEM, VMEM, VMEM, VMEM],
        [wide],
        flops=2_000_000_000,
        moved=2_000_000,
    )(offsets, state, middle_query, middle_blocks)
    combined = call(
        outer_kernel,
        "outer",
        shaped(PEERS, ROWS // 2, 2 * HD),
        [VMEM, VMEM, VMEM, VMEM, VMEM],
        aliases={4: 0},
    )(offsets, merged, outer_query, outer_blocks, before)
    home = swap(combined, "set")
    width = w_out.shape[1]
    return call(
        project_kernel,
        "project",
        shaped(ROWS, width),
        [VMEM, VMEM],
        [pltpu.VMEM((ROWS, width), BF16), pltpu.SemaphoreType.DMA((width // THIRD,))],
        out_spec=HBM,
    )(home, w_out)


def solution(mesh):
    spread = P(("grp", "blk", "set"), None)
    return jax.shard_map(
        per_device,
        mesh=mesh,
        in_specs=(spread, spread, spread, P(("grp", "blk", "set")), P(), P()),
        out_specs=spread,
        check_vma=False,
    )
```

```python
import functools
import math

import jax
import jax.numpy as jnp
from jax import lax
from jax.experimental import pallas as pl
from jax.experimental.pallas import tpu as pltpu
from jax.sharding import PartitionSpec as P

HEADS = 6
HD = 64
PEERS = 8
NEAR = 4
HALF_HEADS = HEADS // 2
ROWS = 128
FIRST_BLOCK = ROWS + ROWS // 2
MARK = 1024.0
EXP_SCALE = math.log2(math.e) / math.sqrt(HD)
FAR = -1e30
THIRD = 256
F32 = jnp.float32
BF16 = jnp.bfloat16

VMEM = pl.BlockSpec(memory_space=pltpu.VMEM)
HBM = pl.BlockSpec(memory_space=pltpu.HBM)


def lanes(shape):
    return lax.broadcasted_iota(jnp.int32, shape, len(shape) - 1)


def rows(shape):
    return lax.broadcasted_iota(jnp.int32, shape, len(shape) - 2)


def my_half():
    return lax.div(lax.axis_index("set"), NEAR)


def head_at(half):
    column = lax.rem(lax.axis_index("set"), NEAR)
    return half * HALF_HEADS + jnp.minimum(column, HALF_HEADS - 1)


def shifts(offsets_ref, head=None):
    head = head_at(my_half()) if head is None else head
    both = offsets_ref[...].astype(F32)
    both = jnp.where(lanes(both.shape) == head, both, F32(0.0))
    middle = jnp.sum(both[0:1, :]).astype(jnp.int32)
    outer = jnp.sum(both[1:2, :]).astype(jnp.int32)
    return middle, (outer - middle) // 8


def place_of(half):
    return pl.multiple_of(jnp.where(half == my_half(), 0, FIRST_BLOCK), FIRST_BLOCK)


def marks():
    shape = (16, 2 * HD)
    row, lane = rows(shape), lanes(shape)
    chosen = ((row == 0) & (lane == 0)) | ((row == 1) & (lane >= 1) & (lane <= 3))
    return chosen.astype(F32).astype(BF16)


def against(query, block_ref, index):
    return lax.dot_general(
        query, block_ref[index, 0:ROWS, :], (((1,), (1,)), ((), ())), preferred_element_type=F32
    )


def level(query, block_ref, self_masks, seen=None):
    count = query.shape[0]
    parts = []
    if seen is None:
        query = jnp.concatenate([query, marks()], axis=0)
    for c in range(PEERS):
        part = against(query, block_ref, c)
        seen_part = part[count:, :] if seen is None else seen[c]
        hidden = seen_part[0:1, :] > F32(MARK / 2)
        masked = part[0:count, :] + jnp.where(hidden, F32(FAR), F32(0.0))
        if self_masks[c] is not None:
            masked = jnp.where(self_masks[c] & hidden, seen_part[1:2, :], masked)
        parts.append(masked)
    best = functools.reduce(jnp.maximum, parts)
    top = jnp.max(best, axis=1, keepdims=True)
    sums = None
    mixture = None
    for c in range(PEERS):
        weight = jnp.exp2((parts[c] - top) * F32(EXP_SCALE))
        sums = weight if sums is None else sums + weight
        add = jnp.dot(weight.astype(BF16), block_ref[c, 0:ROWS, :], preferred_element_type=F32)
        mixture = add if mixture is None else mixture + add
    total = jnp.sum(sums, axis=1, keepdims=True)
    lane = lanes(mixture.shape)
    return jnp.where(lane < 32, top, jnp.where(lane < 64, total, mixture))


def merge(one, two):
    top_one, top_two = one[:, 0:1], two[:, 0:1]
    top = jnp.maximum(top_one, top_two)
    scale_one = jnp.exp2((top_one - top) * F32(EXP_SCALE))
    scale_two = jnp.exp2((top_two - top) * F32(EXP_SCALE))
    both = one * scale_one + two * scale_two
    return jnp.where(lanes(both.shape) < 32, top, both)


def divided(state):
    return state / state[:, 32:33]


def product_of(one, two):
    return jnp.dot(one, two, preferred_element_type=F32)


def pack_kernel(query_hbm, key_hbm, value_hbm, valid_hbm, out_ref, query_ref, key_ref, value_ref, valid_ref, sems):
    pairs = (
        (valid_hbm, valid_ref),
        (key_hbm, key_ref),
        (value_hbm, value_ref),
        (query_hbm, query_ref),
    )
    copies = [pltpu.make_async_copy(a, b, sems.at[i]) for i, (a, b) in enumerate(pairs)]
    for copy in copies:
        copy.start()
    for c in range(HALF_HEADS, NEAR):
        out_ref[c] = jnp.zeros((2 * FIRST_BLOCK, 2 * HD), BF16)
    for copy in copies:
        copy.wait()
    square = (ROWS, 2 * HD)
    row, lane = rows(square), lanes(square)
    valid = jnp.where(row == lane, valid_ref[...].astype(F32), F32(0.0)).astype(BF16)
    hidden = product_of(valid, jnp.ones(square, BF16)) < F32(0.5)
    same_head = ((row // HD) == (lane // HD)).astype(F32).astype(BF16)
    column = lane % HD
    half = ROWS // 2
    for h in range(0, HEADS, 2):
        at = slice(h * HD, (h + 2) * HD)
        key = key_ref[:, at].astype(F32)
        product = query_ref[:, at].astype(F32) * key
        upper = product.astype(BF16)
        lower = (product - upper.astype(F32)).astype(BF16)
        own = product_of(upper, same_head) + product_of(lower, same_head)
        high = own.astype(BF16).astype(F32)
        middle = (own - high).astype(BF16).astype(F32)
        rest = own - high - middle
        code = jnp.where(column == 0, F32(MARK), jnp.where(column == 1, high, F32(0.0)))
        code = jnp.where(column == 2, middle, jnp.where(column == 3, rest, code))
        coded = jnp.where(hidden, code, key).astype(BF16)
        for part in range(2):
            head = h + part
            inner = slice(part * HD, (part + 1) * HD)
            at = slice(head * HD, (head + 1) * HD)
            to = head % HALF_HEADS
            start = place_of(head // HALF_HEADS)
            whole, ends = pl.ds(start, ROWS), pl.ds(start + ROWS, half)
            out_ref[to, whole, 0:HD] = coded[:, inner]
            out_ref[to, whole, HD : 2 * HD] = value_ref[:, at]
            out_ref[to, ends, 0:HD] = query_ref[0:half, at]
            out_ref[to, ends, HD : 2 * HD] = query_ref[half:ROWS, at]


def selector_of(shift):
    shape = (ROWS // 8, ROWS)
    return (lanes(shape) == shift + 8 * rows(shape)).astype(F32).astype(BF16)


def pick_middle_kernel(offsets_ref, blocks_ref, out_ref, cross_ref):
    count = ROWS // 8
    for half in range(2):
        selector = selector_of(shifts(offsets_ref, head_at(half))[0])
        start = place_of(half)
        for c in range(NEAR):
            picked = product_of(selector, blocks_ref[c, pl.ds(start, ROWS), :]).astype(BF16)
            for d in range(PEERS):
                out_ref[2 * d + half, c * count : (c + 1) * count, :] = picked
    for c in range(NEAR):
        cross_ref[c] = blocks_ref[c, FIRST_BLOCK : 2 * FIRST_BLOCK, :]


def pick_outer_kernel(offsets_ref, blocks_ref, out_hbm, picked_ref, sems):
    selector = selector_of(shifts(offsets_ref)[1])
    count = ROWS // 8
    for c in range(PEERS):
        picked = product_of(selector, blocks_ref[c, 0:ROWS, :]).astype(BF16)
        picked_ref[c * count : (c + 1) * count, :] = picked
    copies = [pltpu.make_async_copy(picked_ref, out_hbm.at[d], sems.at[d]) for d in range(PEERS)]
    for copy in copies:
        copy.start()
    for copy in copies:
        copy.wait()


def first_kernel(
    offsets_ref, near_ref, far_ref, state_ref, middle_ref, outer_ref, blocks_ref, wide, narrow
):
    middle, stride = shifts(offsets_ref)
    mine = my_half()
    for c in range(NEAR):
        blocks_ref[mine * NEAR + c] = near_ref[c, 0:FIRST_BLOCK, :]
        blocks_ref[(1 - mine) * NEAR + c] = far_ref[c]
    half = ROWS // 2
    low = lanes((half, 2 * HD)) < HD
    diagonal = rows((ROWS, ROWS)) == lanes((ROWS, ROWS))
    reader = marks()
    seen = [against(reader, blocks_ref, c) for c in range(PEERS)]
    for j in range(PEERS):
        pair = blocks_ref[j, ROWS:FIRST_BLOCK, :].astype(F32)
        wide[j * ROWS : j * ROWS + half, :] = jnp.where(low, pair, F32(0.0))
        wide[j * ROWS + half : (j + 1) * ROWS, :] = jnp.where(
            low, pltpu.roll(pair, HD, 1), F32(0.0)
        )
        query = wide[j * ROWS : (j + 1) * ROWS, :].astype(BF16)
        masks = [diagonal if c == j else None for c in range(PEERS)]
        state_ref[j * ROWS : (j + 1) * ROWS, :] = level(query, blocks_ref, masks, seen)
    picked = wide[pl.ds(middle, ROWS, stride=8), :]
    middle_ref[...] = picked.astype(BF16)
    narrow[...] = picked
    outer_ref[...] = narrow[pl.ds(stride, ROWS // 8, stride=8), :].astype(BF16)


def middle_kernel(offsets_ref, state_ref, query_ref, blocks_ref, out_ref, merged_ref, wide):
    middle, _ = shifts(offsets_ref)
    mine = lax.axis_index("blk")
    diagonal = rows((ROWS, ROWS)) == lanes((ROWS, ROWS))
    masks = [diagonal & (mine == c) for c in range(PEERS)]
    found = level(query_ref[...], blocks_ref, masks)
    both = merge(state_ref[pl.ds(middle, ROWS, stride=8), :], found)
    merged_ref[...] = both
    wide[...] = state_ref[...]
    wide[pl.ds(middle, ROWS, stride=8), :] = both
    half = ROWS // 2
    low = lanes((half, 2 * HD)) < HD
    for j in range(PEERS):
        one = divided(wide[j * ROWS : j * ROWS + half, :])
        two = divided(wide[j * ROWS + half : (j + 1) * ROWS, :])
        out_ref[j] = jnp.where(low, pltpu.roll(one, HD, 1), two).astype(BF16)


def outer_kernel(offsets_ref, merged_ref, query_ref, blocks_ref, before_ref, out_ref):
    middle, stride = shifts(offsets_ref)
    block, group = lax.axis_index("blk"), lax.axis_index("grp")
    count = ROWS // 8
    shape = (count, ROWS)
    diagonal = lanes(shape) == block * count + rows(shape)
    masks = [diagonal & (group == c) for c in range(PEERS)]
    found = level(query_ref[...], blocks_ref, masks)
    both = divided(merge(merged_ref[pl.ds(stride, count, stride=8), :], found))
    turned = pltpu.roll(both, HD, 1)
    tile = 16
    token = middle + 8 * stride
    start = pl.multiple_of((token // tile) * tile, tile)
    here = rows((tile, 2 * HD)) == token - start
    low = lanes((1, 2 * HD)) < HD
    for j in range(PEERS):
        row = jnp.where(low, turned[2 * j : 2 * j + 1, :], both[2 * j + 1 : 2 * j + 2, :])
        kept = before_ref[j, pl.ds(start, tile), :].astype(F32)
        out_ref[j, pl.ds(start, tile), :] = jnp.where(here, row, kept).astype(BF16)


def project_kernel(blocks_ref, weight_ref, out_hbm, out_ref, sems):
    half = ROWS // 2
    low = lanes((half, 2 * HD)) < HD
    tops, bottoms = [], []
    places = [h // HALF_HEADS * NEAR + h % HALF_HEADS for h in range(HEADS)]
    for h in range(0, HEADS, 2):
        one, two = blocks_ref[places[h]].astype(F32), blocks_ref[places[h + 1]].astype(F32)
        tops.append(jnp.where(low, one, pltpu.roll(two, HD, 1)).astype(BF16))
        bottoms.append(jnp.where(low, pltpu.roll(one, HD, 1), two).astype(BF16))
    combined = jnp.concatenate(
        [jnp.concatenate(tops, axis=1), jnp.concatenate(bottoms, axis=1)], axis=0
    )
    copies = []
    for n in range(out_ref.shape[1] // THIRD):
        at = slice(n * THIRD, (n + 1) * THIRD)
        out_ref[:, at] = product_of(combined, weight_ref[:, at]).astype(BF16)
        copies.append(pltpu.make_async_copy(out_ref.at[:, at], out_hbm.at[:, at], sems.at[n]))
        copies[-1].start()
    for copy in copies:
        copy.wait()


def call(kernel, name, out_shape, in_specs, scratch=(), flops=0, moved=0, aliases=None, out_spec=VMEM):
    outs = jax.tree.map(lambda _: out_spec, out_shape)
    return pl.pallas_call(
        kernel,
        name=name,
        out_shape=out_shape,
        in_specs=in_specs,
        out_specs=outs,
        scratch_shapes=list(scratch),
        input_output_aliases=aliases or {},
        compiler_params=pltpu.CompilerParams(vmem_limit_bytes=40 * 2**20),
        cost_estimate=pl.CostEstimate(flops=flops, bytes_accessed=moved, transcendentals=0),
    )


def shaped(*shape, dtype=BF16):
    return jax.ShapeDtypeStruct(shape, dtype)


def per_device(queries, keys, values, valid, offsets, w_out):
    wide = pltpu.VMEM((PEERS * ROWS, 2 * HD), F32)
    narrow = pltpu.VMEM((ROWS, 2 * HD), F32)
    swap = functools.partial(lax.all_to_all, split_axis=0, concat_axis=0, tiled=True)

    whole = pltpu.VMEM((ROWS, HEADS * HD), BF16)
    given = (queries, keys, values, valid.reshape(1, ROWS))
    packed = call(
        pack_kernel,
        "pack",
        shaped(NEAR, 2 * FIRST_BLOCK, 2 * HD),
        [HBM] * 4,
        [whole, whole, whole, pltpu.VMEM((1, ROWS), jnp.int32), pltpu.SemaphoreType.DMA((4,))],
    )(*(pltpu.with_memory_space_constraint(a, pltpu.HBM) for a in given))
    near_groups = [[z * NEAR + x for x in range(NEAR)] for z in range(2)]
    near = swap(packed, "set", axis_index_groups=near_groups)
    middle_send, cross = call(
        pick_middle_kernel,
        "pick_middle",
        (shaped(2 * PEERS, ROWS // 2, 2 * HD), shaped(NEAR, FIRST_BLOCK, 2 * HD)),
        [VMEM, VMEM],
    )(offsets, near)
    middle_groups = [
        [b * PEERS + z * NEAR + x for b in range(PEERS) for z in range(2)] for x in range(NEAR)
    ]
    middle_blocks = swap(middle_send, ("blk", "set"), axis_index_groups=middle_groups)
    middle_blocks = middle_blocks.reshape(PEERS, ROWS, 2 * HD)
    far = lax.ppermute(cross, "set", [(i, (i + NEAR) % PEERS) for i in range(PEERS)])
    state, middle_query, outer_query = call(
        first_kernel,
        "first",
        (shaped(PEERS * ROWS, 2 * HD, dtype=F32), shaped(ROWS, 2 * HD), shaped(ROWS // 8, 2 * HD)),
        [VMEM, VMEM, VMEM],
        [pltpu.VMEM((PEERS, FIRST_BLOCK, 2 * HD), BF16), wide, narrow],
        flops=6_000_000_000,
        moved=2_000_000,
    )(offsets, near, far)
    outer_send = call(
        pick_outer_kernel,
        "pick_outer",
        shaped(PEERS, ROWS, 2 * HD),
        [VMEM, VMEM],
        [pltpu.VMEM((ROWS, 2 * HD), BF16), pltpu.SemaphoreType.DMA((PEERS,))],
        out_spec=HBM,
    )(offsets, middle_blocks)
    outer_blocks = swap(outer_send, "grp")
    before, merged = call(
        middle_kernel,
        "middle",
        (shaped(PEERS, ROWS // 2, 2 * HD), shaped(ROWS, 2 * HD, dtype=F32)),
        [VMEM, VMEM, VMEM, VMEM],
        [wide],
        flops=2_000_000_000,
        moved=2_000_000,
    )(offsets, state, middle_query, middle_blocks)
    combined = call(
        outer_kernel,
        "outer",
        shaped(PEERS, ROWS // 2, 2 * HD),
        [VMEM, VMEM, VMEM, VMEM, VMEM],
        aliases={4: 0},
    )(offsets, merged, outer_query, outer_blocks, before)
    home = swap(combined, "set")
    width = w_out.shape[1]
    return call(
        project_kernel,
        "project",
        shaped(ROWS, width),
        [VMEM, VMEM],
        [pltpu.VMEM((ROWS, width), BF16), pltpu.SemaphoreType.DMA((width // THIRD,))],
        out_spec=HBM,
    )(home, w_out)


def solution(mesh):
    spread = P(("grp", "blk", "set"), None)
    return jax.shard_map(
        per_device,
        mesh=mesh,
        in_specs=(spread, spread, spread, P(("grp", "blk", "set")), P(), P()),
        out_specs=spread,
        check_vma=False,
    )
```

```python
import functools
import math

import jax
import jax.numpy as jnp
from jax import lax
from jax.experimental import pallas as pl
from jax.experimental.pallas import tpu as pltpu
from jax.sharding import PartitionSpec as P

HEADS = 6
HD = 64
PEERS = 8
NEAR = 4
HALF_HEADS = HEADS // 2
ROWS = 128
FIRST_BLOCK = ROWS + ROWS // 2
MARK = 1024.0
EXP_SCALE = math.log2(math.e) / math.sqrt(HD)
FAR = -1e30
THIRD = 256
F32 = jnp.float32
BF16 = jnp.bfloat16

VMEM = pl.BlockSpec(memory_space=pltpu.VMEM)
HBM = pl.BlockSpec(memory_space=pltpu.HBM)


def lanes(shape):
    return lax.broadcasted_iota(jnp.int32, shape, len(shape) - 1)


def rows(shape):
    return lax.broadcasted_iota(jnp.int32, shape, len(shape) - 2)


def my_half():
    return lax.div(lax.axis_index("set"), NEAR)


def head_at(half):
    column = lax.rem(lax.axis_index("set"), NEAR)
    return half * HALF_HEADS + jnp.minimum(column, HALF_HEADS - 1)


def shifts(offsets_ref, head=None):
    head = head_at(my_half()) if head is None else head
    both = offsets_ref[...].astype(F32)
    both = jnp.where(lanes(both.shape) == head, both, F32(0.0))
    middle = jnp.sum(both[0:1, :]).astype(jnp.int32)
    outer = jnp.sum(both[1:2, :]).astype(jnp.int32)
    return middle, (outer - middle) // 8


def place_of(half):
    return pl.multiple_of(jnp.where(half == my_half(), 0, FIRST_BLOCK), FIRST_BLOCK)


def marks():
    shape = (16, 2 * HD)
    row, lane = rows(shape), lanes(shape)
    chosen = ((row == 0) & (lane == 0)) | ((row == 1) & (lane >= 1) & (lane <= 3))
    return chosen.astype(F32).astype(BF16)


def against(query, block_ref, index):
    return lax.dot_general(
        query, block_ref[index, 0:ROWS, :], (((1,), (1,)), ((), ())), preferred_element_type=F32
    )


def level(query, block_ref, self_masks, seen=None):
    count = query.shape[0]
    parts = []
    if seen is None:
        query = jnp.concatenate([query, marks()], axis=0)
    for c in range(PEERS):
        part = against(query, block_ref, c)
        seen_part = part[count:, :] if seen is None else seen[c]
        hidden = seen_part[0:1, :] > F32(MARK / 2)
        masked = part[0:count, :] + jnp.where(hidden, F32(FAR), F32(0.0))
        if self_masks[c] is not None:
            masked = jnp.where(self_masks[c] & hidden, seen_part[1:2, :], masked)
        parts.append(masked)
    best = functools.reduce(jnp.maximum, parts)
    top = jnp.max(best, axis=1, keepdims=True)
    sums = None
    mixture = None
    for c in range(PEERS):
        weight = jnp.exp2((parts[c] - top) * F32(EXP_SCALE))
        sums = weight if sums is None else sums + weight
        add = jnp.dot(weight.astype(BF16), block_ref[c, 0:ROWS, :], preferred_element_type=F32)
        mixture = add if mixture is None else mixture + add
    total = jnp.sum(sums, axis=1, keepdims=True)
    lane = lanes(mixture.shape)
    return jnp.where(lane < 32, top, jnp.where(lane < 64, total, mixture))


def merge(one, two):
    top_one, top_two = one[:, 0:1], two[:, 0:1]
    top = jnp.maximum(top_one, top_two)
    scale_one = jnp.exp2((top_one - top) * F32(EXP_SCALE))
    scale_two = jnp.exp2((top_two - top) * F32(EXP_SCALE))
    both = one * scale_one + two * scale_two
    return jnp.where(lanes(both.shape) < 32, top, both)


def divided(state):
    return state / state[:, 32:33]


def product_of(one, two):
    return jnp.dot(one, two, preferred_element_type=F32)


def pack_kernel(query_hbm, key_hbm, value_hbm, valid_hbm, out_ref, query_ref, key_ref, value_ref, valid_ref, sems):
    pairs = (
        (valid_hbm, valid_ref),
        (key_hbm, key_ref),
        (value_hbm, value_ref),
        (query_hbm, query_ref),
    )
    copies = [pltpu.make_async_copy(a, b, sems.at[i]) for i, (a, b) in enumerate(pairs)]
    for copy in copies:
        copy.start()
    for c in range(HALF_HEADS, NEAR):
        out_ref[c] = jnp.zeros((2 * FIRST_BLOCK, 2 * HD), BF16)
    for copy in copies:
        copy.wait()
    square = (ROWS, 2 * HD)
    row, lane = rows(square), lanes(square)
    valid = jnp.where(row == lane, valid_ref[...].astype(F32), F32(0.0)).astype(BF16)
    hidden = product_of(valid, jnp.ones(square, BF16)) < F32(0.5)
    same_head = ((row // HD) == (lane // HD)).astype(F32).astype(BF16)
    column = lane % HD
    half = ROWS // 2
    for h in range(0, HEADS, 2):
        at = slice(h * HD, (h + 2) * HD)
        key = key_ref[:, at].astype(F32)
        product = query_ref[:, at].astype(F32) * key
        upper = product.astype(BF16)
        lower = (product - upper.astype(F32)).astype(BF16)
        own = product_of(upper, same_head) + product_of(lower, same_head)
        high = own.astype(BF16).astype(F32)
        middle = (own - high).astype(BF16).astype(F32)
        rest = own - high - middle
        code = jnp.where(column == 0, F32(MARK), jnp.where(column == 1, high, F32(0.0)))
        code = jnp.where(column == 2, middle, jnp.where(column == 3, rest, code))
        coded = jnp.where(hidden, code, key).astype(BF16)
        for part in range(2):
            head = h + part
            inner = slice(part * HD, (part + 1) * HD)
            at = slice(head * HD, (head + 1) * HD)
            to = head % HALF_HEADS
            start = place_of(head // HALF_HEADS)
            whole, ends = pl.ds(start, ROWS), pl.ds(start + ROWS, half)
            out_ref[to, whole, 0:HD] = coded[:, inner]
            out_ref[to, whole, HD : 2 * HD] = value_ref[:, at]
            out_ref[to, ends, 0:HD] = query_ref[0:half, at]
            out_ref[to, ends, HD : 2 * HD] = query_ref[half:ROWS, at]


def selector_of(shift):
    shape = (ROWS // 8, ROWS)
    return (lanes(shape) == shift + 8 * rows(shape)).astype(F32).astype(BF16)


def pick_middle_kernel(offsets_ref, blocks_ref, own_ref, partner_ref):
    count = ROWS // 8
    for out_ref, half, start in (
        (own_ref, my_half(), 0),
        (partner_ref, 1 - my_half(), FIRST_BLOCK),
    ):
        selector = selector_of(shifts(offsets_ref, head_at(half))[0])
        for c in range(NEAR):
            rows_of = blocks_ref[c, start : start + ROWS, :]
            out_ref[c * count : (c + 1) * count, :] = product_of(selector, rows_of).astype(BF16)


def join_kernel(own_ref, partner_ref, blocks_ref, out_ref, cross_ref):
    count = ROWS // 2
    mine = my_half()
    own, other = own_ref[...].astype(F32), partner_ref[...].astype(F32)
    first = jnp.where(mine == 0, own, other).astype(BF16)
    second = jnp.where(mine == 0, other, own).astype(BF16)
    for d in range(PEERS):
        out_ref[d, 0:count, :] = first
        out_ref[d, count:ROWS, :] = second
    for c in range(NEAR):
        cross_ref[c] = blocks_ref[c, FIRST_BLOCK : 2 * FIRST_BLOCK, :]


def pick_outer_kernel(offsets_ref, blocks_ref, out_hbm, picked_ref, sems):
    selector = selector_of(shifts(offsets_ref)[1])
    count = ROWS // 8
    for c in range(PEERS):
        picked = product_of(selector, blocks_ref[c, 0:ROWS, :]).astype(BF16)
        picked_ref[c * count : (c + 1) * count, :] = picked
    copies = [pltpu.make_async_copy(picked_ref, out_hbm.at[d], sems.at[d]) for d in range(PEERS)]
    for copy in copies:
        copy.start()
    for copy in copies:
        copy.wait()


def first_kernel(
    offsets_ref, near_ref, far_ref, state_ref, middle_ref, outer_ref, blocks_ref, wide, narrow
):
    middle, stride = shifts(offsets_ref)
    mine = my_half()
    for c in range(NEAR):
        blocks_ref[mine * NEAR + c] = near_ref[c, 0:FIRST_BLOCK, :]
        blocks_ref[(1 - mine) * NEAR + c] = far_ref[c]
    half = ROWS // 2
    low = lanes((half, 2 * HD)) < HD
    diagonal = rows((ROWS, ROWS)) == lanes((ROWS, ROWS))
    reader = marks()
    seen = [against(reader, blocks_ref, c) for c in range(PEERS)]
    for j in range(PEERS):
        pair = blocks_ref[j, ROWS:FIRST_BLOCK, :].astype(F32)
        wide[j * ROWS : j * ROWS + half, :] = jnp.where(low, pair, F32(0.0))
        wide[j * ROWS + half : (j + 1) * ROWS, :] = jnp.where(
            low, pltpu.roll(pair, HD, 1), F32(0.0)
        )
        query = wide[j * ROWS : (j + 1) * ROWS, :].astype(BF16)
        masks = [diagonal if c == j else None for c in range(PEERS)]
        state_ref[j * ROWS : (j + 1) * ROWS, :] = level(query, blocks_ref, masks, seen)
    picked = wide[pl.ds(middle, ROWS, stride=8), :]
    middle_ref[...] = picked.astype(BF16)
    narrow[...] = picked
    outer_ref[...] = narrow[pl.ds(stride, ROWS // 8, stride=8), :].astype(BF16)


def middle_kernel(offsets_ref, state_ref, query_ref, blocks_ref, out_ref, merged_ref, wide):
    middle, _ = shifts(offsets_ref)
    mine = lax.axis_index("blk")
    diagonal = rows((ROWS, ROWS)) == lanes((ROWS, ROWS))
    masks = [diagonal & (mine == c) for c in range(PEERS)]
    found = level(query_ref[...], blocks_ref, masks)
    both = merge(state_ref[pl.ds(middle, ROWS, stride=8), :], found)
    merged_ref[...] = both
    wide[...] = state_ref[...]
    wide[pl.ds(middle, ROWS, stride=8), :] = both
    half = ROWS // 2
    low = lanes((half, 2 * HD)) < HD
    for j in range(PEERS):
        one = divided(wide[j * ROWS : j * ROWS + half, :])
        two = divided(wide[j * ROWS + half : (j + 1) * ROWS, :])
        out_ref[j] = jnp.where(low, pltpu.roll(one, HD, 1), two).astype(BF16)


def outer_kernel(offsets_ref, merged_ref, query_ref, blocks_ref, before_ref, out_ref):
    middle, stride = shifts(offsets_ref)
    block, group = lax.axis_index("blk"), lax.axis_index("grp")
    count = ROWS // 8
    shape = (count, ROWS)
    diagonal = lanes(shape) == block * count + rows(shape)
    masks = [diagonal & (group == c) for c in range(PEERS)]
    found = level(query_ref[...], blocks_ref, masks)
    both = divided(merge(merged_ref[pl.ds(stride, count, stride=8), :], found))
    turned = pltpu.roll(both, HD, 1)
    tile = 16
    token = middle + 8 * stride
    start = pl.multiple_of((token // tile) * tile, tile)
    here = rows((tile, 2 * HD)) == token - start
    low = lanes((1, 2 * HD)) < HD
    for j in range(PEERS):
        row = jnp.where(low, turned[2 * j : 2 * j + 1, :], both[2 * j + 1 : 2 * j + 2, :])
        kept = before_ref[j, pl.ds(start, tile), :].astype(F32)
        out_ref[j, pl.ds(start, tile), :] = jnp.where(here, row, kept).astype(BF16)


def project_kernel(blocks_ref, weight_ref, out_hbm, out_ref, sems):
    half = ROWS // 2
    low = lanes((half, 2 * HD)) < HD
    tops, bottoms = [], []
    places = [h // HALF_HEADS * NEAR + h % HALF_HEADS for h in range(HEADS)]
    for h in range(0, HEADS, 2):
        one, two = blocks_ref[places[h]].astype(F32), blocks_ref[places[h + 1]].astype(F32)
        tops.append(jnp.where(low, one, pltpu.roll(two, HD, 1)).astype(BF16))
        bottoms.append(jnp.where(low, pltpu.roll(one, HD, 1), two).astype(BF16))
    combined = jnp.concatenate(
        [jnp.concatenate(tops, axis=1), jnp.concatenate(bottoms, axis=1)], axis=0
    )
    copies = []
    for n in range(out_ref.shape[1] // THIRD):
        at = slice(n * THIRD, (n + 1) * THIRD)
        out_ref[:, at] = product_of(combined, weight_ref[:, at]).astype(BF16)
        copies.append(pltpu.make_async_copy(out_ref.at[:, at], out_hbm.at[:, at], sems.at[n]))
        copies[-1].start()
    for copy in copies:
        copy.wait()


def call(kernel, name, out_shape, in_specs, scratch=(), flops=0, moved=0, aliases=None, out_spec=VMEM):
    outs = jax.tree.map(lambda _: out_spec, out_shape)
    return pl.pallas_call(
        kernel,
        name=name,
        out_shape=out_shape,
        in_specs=in_specs,
        out_specs=outs,
        scratch_shapes=list(scratch),
        input_output_aliases=aliases or {},
        compiler_params=pltpu.CompilerParams(vmem_limit_bytes=40 * 2**20),
        cost_estimate=pl.CostEstimate(flops=flops, bytes_accessed=moved, transcendentals=0),
    )


def shaped(*shape, dtype=BF16):
    return jax.ShapeDtypeStruct(shape, dtype)


def per_device(queries, keys, values, valid, offsets, w_out):
    wide = pltpu.VMEM((PEERS * ROWS, 2 * HD), F32)
    narrow = pltpu.VMEM((ROWS, 2 * HD), F32)
    swap = functools.partial(lax.all_to_all, split_axis=0, concat_axis=0, tiled=True)

    whole = pltpu.VMEM((ROWS, HEADS * HD), BF16)
    given = (queries, keys, values, valid.reshape(1, ROWS))
    packed = call(
        pack_kernel,
        "pack",
        shaped(NEAR, 2 * FIRST_BLOCK, 2 * HD),
        [HBM] * 4,
        [whole, whole, whole, pltpu.VMEM((1, ROWS), jnp.int32), pltpu.SemaphoreType.DMA((4,))],
    )(*(pltpu.with_memory_space_constraint(a, pltpu.HBM) for a in given))
    near_groups = [[z * NEAR + x for x in range(NEAR)] for z in range(2)]
    near = swap(packed, "set", axis_index_groups=near_groups)
    partners = [(i, (i + NEAR) % PEERS) for i in range(PEERS)]
    half_rows = shaped(ROWS // 2, 2 * HD)
    own_rows, partner_rows = call(
        pick_middle_kernel, "pick_middle", (half_rows, half_rows), [VMEM, VMEM]
    )(offsets, near)
    middle_send, cross = call(
        join_kernel,
        "join",
        (shaped(PEERS, ROWS, 2 * HD), shaped(NEAR, FIRST_BLOCK, 2 * HD)),
        [VMEM, VMEM, VMEM],
    )(own_rows, lax.ppermute(partner_rows, "set", partners), near)
    middle_blocks = swap(middle_send, "blk")
    far = lax.ppermute(cross, "set", partners)
    state, middle_query, outer_query = call(
        first_kernel,
        "first",
        (shaped(PEERS * ROWS, 2 * HD, dtype=F32), shaped(ROWS, 2 * HD), shaped(ROWS // 8, 2 * HD)),
        [VMEM, VMEM, VMEM],
        [pltpu.VMEM((PEERS, FIRST_BLOCK, 2 * HD), BF16), wide, narrow],
        flops=6_000_000_000,
        moved=2_000_000,
    )(offsets, near, far)
    outer_send = call(
        pick_outer_kernel,
        "pick_outer",
        shaped(PEERS, ROWS, 2 * HD),
        [VMEM, VMEM],
        [pltpu.VMEM((ROWS, 2 * HD), BF16), pltpu.SemaphoreType.DMA((PEERS,))],
        out_spec=HBM,
    )(offsets, middle_blocks)
    outer_blocks = swap(outer_send, "grp")
    before, merged = call(
        middle_kernel,
        "middle",
        (shaped(PEERS, ROWS // 2, 2 * HD), shaped(ROWS, 2 * HD, dtype=F32)),
        [VMEM, VMEM, VMEM, VMEM],
        [wide],
        flops=2_000_000_000,
        moved=2_000_000,
    )(offsets, state, middle_query, middle_blocks)
    combined = call(
        outer_kernel,
        "outer",
        shaped(PEERS, ROWS // 2, 2 * HD),
        [VMEM, VMEM, VMEM, VMEM, VMEM],
        aliases={4: 0},
    )(offsets, merged, outer_query, outer_blocks, before)
    home = swap(combined, "set")
    width = w_out.shape[1]
    return call(
        project_kernel,
        "project",
        shaped(ROWS, width),
        [VMEM, VMEM],
        [pltpu.VMEM((ROWS, width), BF16), pltpu.SemaphoreType.DMA((width // THIRD,))],
        out_spec=HBM,
    )(home, w_out)


def solution(mesh):
    spread = P(("grp", "blk", "set"), None)
    return jax.shard_map(
        per_device,
        mesh=mesh,
        in_specs=(spread, spread, spread, P(("grp", "blk", "set")), P(), P()),
        out_specs=spread,
        check_vma=False,
    )
```

```python
import functools
import math

import jax
import jax.numpy as jnp
from jax import lax
from jax.experimental import pallas as pl
from jax.experimental.pallas import tpu as pltpu
from jax.sharding import PartitionSpec as P

HEADS = 6
HD = 64
PEERS = 8
NEAR = 4
HALF_HEADS = HEADS // 2
NEAR_TURN = 3
BLOCK_TURN = 4
HALF_TURN = 1
GROUP_TURN = 4
ROWS = 128
FIRST_BLOCK = ROWS + ROWS // 2
MARK = 1024.0
EXP_SCALE = math.log2(math.e) / math.sqrt(HD)
FAR = -1e30
THIRD = 256
F32 = jnp.float32
BF16 = jnp.bfloat16

VMEM = pl.BlockSpec(memory_space=pltpu.VMEM)
HBM = pl.BlockSpec(memory_space=pltpu.HBM)


def lanes(shape):
    return lax.broadcasted_iota(jnp.int32, shape, len(shape) - 1)


def rows(shape):
    return lax.broadcasted_iota(jnp.int32, shape, len(shape) - 2)


def my_half():
    return lax.div(lax.axis_index("set"), NEAR)


def head_at(half):
    column = lax.rem(lax.axis_index("set"), NEAR)
    return half * HALF_HEADS + jnp.minimum(column, HALF_HEADS - 1)


def shifts(offsets_ref, head=None):
    head = head_at(my_half()) if head is None else head
    both = offsets_ref[...].astype(F32)
    both = jnp.where(lanes(both.shape) == head, both, F32(0.0))
    middle = jnp.sum(both[0:1, :]).astype(jnp.int32)
    outer = jnp.sum(both[1:2, :]).astype(jnp.int32)
    return middle, (outer - middle) // 8


def place_of(half):
    return pl.multiple_of(jnp.where(half == my_half(), 0, FIRST_BLOCK), FIRST_BLOCK)


def marks():
    shape = (16, 2 * HD)
    row, lane = rows(shape), lanes(shape)
    chosen = ((row == 0) & (lane == 0)) | ((row == 1) & (lane >= 1) & (lane <= 3))
    return chosen.astype(F32).astype(BF16)


def against(query, block_ref, index):
    return lax.dot_general(
        query, block_ref[index, 0:ROWS, :], (((1,), (1,)), ((), ())), preferred_element_type=F32
    )


def level(query, block_ref, self_masks, seen=None):
    count = query.shape[0]
    parts = []
    if seen is None:
        query = jnp.concatenate([query, marks()], axis=0)
    for c in range(PEERS):
        part = against(query, block_ref, c)
        seen_part = part[count:, :] if seen is None else seen[c]
        hidden = seen_part[0:1, :] > F32(MARK / 2)
        masked = part[0:count, :] + jnp.where(hidden, F32(FAR), F32(0.0))
        if self_masks[c] is not None:
            masked = jnp.where(self_masks[c] & hidden, seen_part[1:2, :], masked)
        parts.append(masked)
    best = functools.reduce(jnp.maximum, parts)
    top = jnp.max(best, axis=1, keepdims=True)
    sums = None
    mixture = None
    for c in range(PEERS):
        weight = jnp.exp2((parts[c] - top) * F32(EXP_SCALE))
        sums = weight if sums is None else sums + weight
        add = jnp.dot(weight.astype(BF16), block_ref[c, 0:ROWS, :], preferred_element_type=F32)
        mixture = add if mixture is None else mixture + add
    total = jnp.sum(sums, axis=1, keepdims=True)
    lane = lanes(mixture.shape)
    return jnp.where(lane < 32, top, jnp.where(lane < 64, total, mixture))


def merge(one, two):
    top_one, top_two = one[:, 0:1], two[:, 0:1]
    top = jnp.maximum(top_one, top_two)
    scale_one = jnp.exp2((top_one - top) * F32(EXP_SCALE))
    scale_two = jnp.exp2((top_two - top) * F32(EXP_SCALE))
    both = one * scale_one + two * scale_two
    return jnp.where(lanes(both.shape) < 32, top, both)


def divided(state):
    return state / state[:, 32:33]


def product_of(one, two):
    return jnp.dot(one, two, preferred_element_type=F32)


def pack_kernel(query_hbm, key_hbm, value_hbm, valid_hbm, out_ref, query_ref, key_ref, value_ref, valid_ref, sems):
    pairs = (
        (valid_hbm, valid_ref),
        (key_hbm, key_ref),
        (value_hbm, value_ref),
        (query_hbm, query_ref),
    )
    copies = [pltpu.make_async_copy(a, b, sems.at[i]) for i, (a, b) in enumerate(pairs)]
    for copy in copies:
        copy.start()
    for c in range(HALF_HEADS, NEAR):
        out_ref[c ^ NEAR_TURN] = jnp.zeros((2 * FIRST_BLOCK, 2 * HD), BF16)
    for copy in copies:
        copy.wait()
    square = (ROWS, 2 * HD)
    row, lane = rows(square), lanes(square)
    valid = jnp.where(row == lane, valid_ref[...].astype(F32), F32(0.0)).astype(BF16)
    hidden = product_of(valid, jnp.ones(square, BF16)) < F32(0.5)
    same_head = ((row // HD) == (lane // HD)).astype(F32).astype(BF16)
    column = lane % HD
    half = ROWS // 2
    for h in range(0, HEADS, 2):
        at = slice(h * HD, (h + 2) * HD)
        key = key_ref[:, at].astype(F32)
        product = query_ref[:, at].astype(F32) * key
        upper = product.astype(BF16)
        lower = (product - upper.astype(F32)).astype(BF16)
        own = product_of(upper, same_head) + product_of(lower, same_head)
        high = own.astype(BF16).astype(F32)
        middle = (own - high).astype(BF16).astype(F32)
        rest = own - high - middle
        code = jnp.where(column == 0, F32(MARK), jnp.where(column == 1, high, F32(0.0)))
        code = jnp.where(column == 2, middle, jnp.where(column == 3, rest, code))
        coded = jnp.where(hidden, code, key).astype(BF16)
        for part in range(2):
            head = h + part
            inner = slice(part * HD, (part + 1) * HD)
            at = slice(head * HD, (head + 1) * HD)
            to = (head % HALF_HEADS) ^ NEAR_TURN
            start = place_of(head // HALF_HEADS)
            whole, ends = pl.ds(start, ROWS), pl.ds(start + ROWS, half)
            out_ref[to, whole, 0:HD] = coded[:, inner]
            out_ref[to, whole, HD : 2 * HD] = value_ref[:, at]
            out_ref[to, ends, 0:HD] = query_ref[0:half, at]
            out_ref[to, ends, HD : 2 * HD] = query_ref[half:ROWS, at]


def turned(row):
    return (row + HALF_TURN * ROWS // 2) % ROWS


def selector_of(shift, place=lambda row: row):
    shape = (ROWS // 8, ROWS)
    return (lanes(shape) == place(shift + 8 * rows(shape))).astype(F32).astype(BF16)


def pick_middle_kernel(offsets_ref, blocks_ref, out_ref, cross_ref):
    count = ROWS // 8
    for half in range(2):
        selector = selector_of(shifts(offsets_ref, head_at(half))[0])
        start = place_of(half)
        for c in range(NEAR):
            rows_of = blocks_ref[c ^ NEAR_TURN, pl.ds(start, ROWS), :]
            picked = product_of(selector, rows_of).astype(BF16)
            for d in range(PEERS):
                place = 2 * d + (half ^ HALF_TURN)
                out_ref[place, c * count : (c + 1) * count, :] = picked
    for c in range(NEAR):
        cross_ref[c] = blocks_ref[c ^ NEAR_TURN, FIRST_BLOCK : 2 * FIRST_BLOCK, :]


def pick_outer_kernel(offsets_ref, blocks_ref, out_hbm, picked_ref, sems):
    selector = selector_of(shifts(offsets_ref)[1], turned)
    count = ROWS // 8
    for c in range(PEERS):
        picked = product_of(selector, blocks_ref[c ^ BLOCK_TURN, 0:ROWS, :]).astype(BF16)
        picked_ref[c * count : (c + 1) * count, :] = picked
    copies = [pltpu.make_async_copy(picked_ref, out_hbm.at[d], sems.at[d]) for d in range(PEERS)]
    for copy in copies:
        copy.start()
    for copy in copies:
        copy.wait()


def first_kernel(
    offsets_ref, near_ref, far_ref, state_ref, middle_ref, outer_ref, blocks_ref, wide, narrow
):
    middle, stride = shifts(offsets_ref)
    mine = my_half()
    for c in range(NEAR):
        blocks_ref[mine * NEAR + c] = near_ref[c ^ NEAR_TURN, 0:FIRST_BLOCK, :]
        blocks_ref[(1 - mine) * NEAR + c] = far_ref[c]
    half = ROWS // 2
    low = lanes((half, 2 * HD)) < HD
    diagonal = rows((ROWS, ROWS)) == lanes((ROWS, ROWS))
    reader = marks()
    seen = [against(reader, blocks_ref, c) for c in range(PEERS)]
    for j in range(PEERS):
        pair = blocks_ref[j, ROWS:FIRST_BLOCK, :].astype(F32)
        wide[j * ROWS : j * ROWS + half, :] = jnp.where(low, pair, F32(0.0))
        wide[j * ROWS + half : (j + 1) * ROWS, :] = jnp.where(
            low, pltpu.roll(pair, HD, 1), F32(0.0)
        )
        query = wide[j * ROWS : (j + 1) * ROWS, :].astype(BF16)
        masks = [diagonal if c == j else None for c in range(PEERS)]
        state_ref[j * ROWS : (j + 1) * ROWS, :] = level(query, blocks_ref, masks, seen)
    picked = wide[pl.ds(middle, ROWS, stride=8), :]
    middle_ref[...] = picked.astype(BF16)
    narrow[...] = picked
    outer_ref[...] = narrow[pl.ds(stride, ROWS // 8, stride=8), :].astype(BF16)


def middle_kernel(offsets_ref, state_ref, query_ref, blocks_ref, out_ref, merged_ref, wide):
    middle, _ = shifts(offsets_ref)
    mine = lax.axis_index("blk")
    diagonal = turned(rows((ROWS, ROWS))) == lanes((ROWS, ROWS))
    masks = [diagonal & (mine == c ^ BLOCK_TURN) for c in range(PEERS)]
    found = level(query_ref[...], blocks_ref, masks)
    both = merge(state_ref[pl.ds(middle, ROWS, stride=8), :], found)
    merged_ref[...] = both
    wide[...] = state_ref[...]
    wide[pl.ds(middle, ROWS, stride=8), :] = both
    half = ROWS // 2
    low = lanes((half, 2 * HD)) < HD
    for j in range(PEERS):
        one = divided(wide[j * ROWS : j * ROWS + half, :])
        two = divided(wide[j * ROWS + half : (j + 1) * ROWS, :])
        out_ref[j] = jnp.where(low, pltpu.roll(one, HD, 1), two).astype(BF16)


def outer_kernel(offsets_ref, merged_ref, query_ref, blocks_ref, before_ref, out_ref):
    middle, stride = shifts(offsets_ref)
    block, group = lax.axis_index("blk"), lax.axis_index("grp")
    count = ROWS // 8
    shape = (count, ROWS)
    diagonal = lanes(shape) == block * count + rows(shape)
    masks = [diagonal & (group == c ^ GROUP_TURN) for c in range(PEERS)]
    found = level(query_ref[...], blocks_ref, masks)
    both = divided(merge(merged_ref[pl.ds(stride, count, stride=8), :], found))
    rolled = pltpu.roll(both, HD, 1)
    tile = 16
    token = middle + 8 * stride
    start = pl.multiple_of((token // tile) * tile, tile)
    here = rows((tile, 2 * HD)) == token - start
    low = lanes((1, 2 * HD)) < HD
    for j in range(PEERS):
        row = jnp.where(low, rolled[2 * j : 2 * j + 1, :], both[2 * j + 1 : 2 * j + 2, :])
        kept = before_ref[j, pl.ds(start, tile), :].astype(F32)
        out_ref[j, pl.ds(start, tile), :] = jnp.where(here, row, kept).astype(BF16)


def project_kernel(blocks_ref, weight_ref, out_hbm, out_ref, sems):
    half = ROWS // 2
    low = lanes((half, 2 * HD)) < HD
    tops, bottoms = [], []
    places = [h // HALF_HEADS * NEAR + h % HALF_HEADS for h in range(HEADS)]
    for h in range(0, HEADS, 2):
        one, two = blocks_ref[places[h]].astype(F32), blocks_ref[places[h + 1]].astype(F32)
        tops.append(jnp.where(low, one, pltpu.roll(two, HD, 1)).astype(BF16))
        bottoms.append(jnp.where(low, pltpu.roll(one, HD, 1), two).astype(BF16))
    combined = jnp.concatenate(
        [jnp.concatenate(tops, axis=1), jnp.concatenate(bottoms, axis=1)], axis=0
    )
    copies = []
    for n in range(out_ref.shape[1] // THIRD):
        at = slice(n * THIRD, (n + 1) * THIRD)
        out_ref[:, at] = product_of(combined, weight_ref[:, at]).astype(BF16)
        copies.append(pltpu.make_async_copy(out_ref.at[:, at], out_hbm.at[:, at], sems.at[n]))
        copies[-1].start()
    for copy in copies:
        copy.wait()


def call(kernel, name, out_shape, in_specs, scratch=(), flops=0, moved=0, aliases=None, out_spec=VMEM):
    outs = jax.tree.map(lambda _: out_spec, out_shape)
    return pl.pallas_call(
        kernel,
        name=name,
        out_shape=out_shape,
        in_specs=in_specs,
        out_specs=outs,
        scratch_shapes=list(scratch),
        input_output_aliases=aliases or {},
        compiler_params=pltpu.CompilerParams(vmem_limit_bytes=40 * 2**20),
        cost_estimate=pl.CostEstimate(flops=flops, bytes_accessed=moved, transcendentals=0),
    )


def shaped(*shape, dtype=BF16):
    return jax.ShapeDtypeStruct(shape, dtype)


def per_device(queries, keys, values, valid, offsets, w_out):
    wide = pltpu.VMEM((PEERS * ROWS, 2 * HD), F32)
    narrow = pltpu.VMEM((ROWS, 2 * HD), F32)
    swap = functools.partial(lax.all_to_all, split_axis=0, concat_axis=0, tiled=True)

    whole = pltpu.VMEM((ROWS, HEADS * HD), BF16)
    given = (queries, keys, values, valid.reshape(1, ROWS))
    packed = call(
        pack_kernel,
        "pack",
        shaped(NEAR, 2 * FIRST_BLOCK, 2 * HD),
        [HBM] * 4,
        [whole, whole, whole, pltpu.VMEM((1, ROWS), jnp.int32), pltpu.SemaphoreType.DMA((4,))],
    )(*(pltpu.with_memory_space_constraint(a, pltpu.HBM) for a in given))
    near_groups = [[z * NEAR + (x ^ NEAR_TURN) for x in range(NEAR)] for z in range(2)]
    near = swap(packed, "set", axis_index_groups=near_groups)
    middle_send, cross = call(
        pick_middle_kernel,
        "pick_middle",
        (shaped(2 * PEERS, ROWS // 2, 2 * HD), shaped(NEAR, FIRST_BLOCK, 2 * HD)),
        [VMEM, VMEM],
    )(offsets, near)
    middle_groups = [
        [
            (b ^ BLOCK_TURN) * PEERS + (z ^ HALF_TURN) * NEAR + x
            for b in range(PEERS)
            for z in range(2)
        ]
        for x in range(NEAR)
    ]
    middle_blocks = swap(middle_send, ("blk", "set"), axis_index_groups=middle_groups)
    middle_blocks = middle_blocks.reshape(PEERS, ROWS, 2 * HD)
    far = lax.ppermute(cross, "set", [(i, (i + NEAR) % PEERS) for i in range(PEERS)])
    state, middle_query, outer_query = call(
        first_kernel,
        "first",
        (shaped(PEERS * ROWS, 2 * HD, dtype=F32), shaped(ROWS, 2 * HD), shaped(ROWS // 8, 2 * HD)),
        [VMEM, VMEM, VMEM],
        [pltpu.VMEM((PEERS, FIRST_BLOCK, 2 * HD), BF16), wide, narrow],
        flops=6_000_000_000,
        moved=2_000_000,
    )(offsets, near, far)
    outer_send = call(
        pick_outer_kernel,
        "pick_outer",
        shaped(PEERS, ROWS, 2 * HD),
        [VMEM, VMEM],
        [pltpu.VMEM((ROWS, 2 * HD), BF16), pltpu.SemaphoreType.DMA((PEERS,))],
        out_spec=HBM,
    )(offsets, middle_blocks)
    outer_groups = [[g ^ GROUP_TURN for g in range(PEERS)]]
    outer_blocks = swap(outer_send, "grp", axis_index_groups=outer_groups)
    before, merged = call(
        middle_kernel,
        "middle",
        (shaped(PEERS, ROWS // 2, 2 * HD), shaped(ROWS, 2 * HD, dtype=F32)),
        [VMEM, VMEM, VMEM, VMEM],
        [wide],
        flops=2_000_000_000,
        moved=2_000_000,
    )(offsets, state, middle_query, middle_blocks)
    combined = call(
        outer_kernel,
        "outer",
        shaped(PEERS, ROWS // 2, 2 * HD),
        [VMEM, VMEM, VMEM, VMEM, VMEM],
        aliases={4: 0},
    )(offsets, merged, outer_query, outer_blocks, before)
    home = swap(combined, "set")
    width = w_out.shape[1]
    return call(
        project_kernel,
        "project",
        shaped(ROWS, width),
        [VMEM, VMEM],
        [pltpu.VMEM((ROWS, width), BF16), pltpu.SemaphoreType.DMA((width // THIRD,))],
        out_spec=HBM,
    )(home, w_out)


def solution(mesh):
    spread = P(("grp", "blk", "set"), None)
    return jax.shard_map(
        per_device,
        mesh=mesh,
        in_specs=(spread, spread, spread, P(("grp", "blk", "set")), P(), P()),
        out_specs=spread,
        check_vma=False,
    )
```

```python
import functools
import math

import jax
import jax.numpy as jnp
from jax import lax
from jax.experimental import pallas as pl
from jax.experimental.pallas import tpu as pltpu
from jax.sharding import PartitionSpec as P

HEADS = 6
HD = 64
PEERS = 8
NEAR = 4
HALF_HEADS = HEADS // 2
NEAR_TURN = 3
BLOCK_TURN = 4
HALF_TURN = 1
GROUP_TURN = 4
HOME_TURN = 7
ROWS = 128
FIRST_BLOCK = ROWS + ROWS // 2
MARK = 1024.0
EXP_SCALE = math.log2(math.e) / math.sqrt(HD)
FAR = -1e30
THIRD = 256
F32 = jnp.float32
BF16 = jnp.bfloat16

VMEM = pl.BlockSpec(memory_space=pltpu.VMEM)
HBM = pl.BlockSpec(memory_space=pltpu.HBM)


def lanes(shape):
    return lax.broadcasted_iota(jnp.int32, shape, len(shape) - 1)


def rows(shape):
    return lax.broadcasted_iota(jnp.int32, shape, len(shape) - 2)


def my_half():
    return lax.div(lax.axis_index("set"), NEAR)


def head_at(half):
    column = lax.rem(lax.axis_index("set"), NEAR)
    return half * HALF_HEADS + jnp.minimum(column, HALF_HEADS - 1)


def shifts(offsets_ref, head=None):
    head = head_at(my_half()) if head is None else head
    both = offsets_ref[...].astype(F32)
    both = jnp.where(lanes(both.shape) == head, both, F32(0.0))
    middle = jnp.sum(both[0:1, :]).astype(jnp.int32)
    outer = jnp.sum(both[1:2, :]).astype(jnp.int32)
    return middle, (outer - middle) // 8


def place_of(half):
    return pl.multiple_of(jnp.where(half == my_half(), 0, FIRST_BLOCK), FIRST_BLOCK)


def marks():
    shape = (16, 2 * HD)
    row, lane = rows(shape), lanes(shape)
    chosen = ((row == 0) & (lane == 0)) | ((row == 1) & (lane >= 1) & (lane <= 3))
    return chosen.astype(F32).astype(BF16)


def against(query, block_ref, index):
    return lax.dot_general(
        query, block_ref[index, 0:ROWS, :], (((1,), (1,)), ((), ())), preferred_element_type=F32
    )


def level(query, block_ref, self_masks, seen=None):
    count = query.shape[0]
    parts = []
    if seen is None:
        query = jnp.concatenate([query, marks()], axis=0)
    for c in range(PEERS):
        part = against(query, block_ref, c)
        seen_part = part[count:, :] if seen is None else seen[c]
        hidden = seen_part[0:1, :] > F32(MARK / 2)
        masked = part[0:count, :] + jnp.where(hidden, F32(FAR), F32(0.0))
        if self_masks[c] is not None:
            masked = jnp.where(self_masks[c] & hidden, seen_part[1:2, :], masked)
        parts.append(masked)
    best = functools.reduce(jnp.maximum, parts)
    top = jnp.max(best, axis=1, keepdims=True)
    sums = None
    mixture = None
    for c in range(PEERS):
        weight = jnp.exp2((parts[c] - top) * F32(EXP_SCALE))
        sums = weight if sums is None else sums + weight
        add = jnp.dot(weight.astype(BF16), block_ref[c, 0:ROWS, :], preferred_element_type=F32)
        mixture = add if mixture is None else mixture + add
    total = jnp.sum(sums, axis=1, keepdims=True)
    lane = lanes(mixture.shape)
    return jnp.where(lane < 32, top, jnp.where(lane < 64, total, mixture))


def merge(one, two):
    top_one, top_two = one[:, 0:1], two[:, 0:1]
    top = jnp.maximum(top_one, top_two)
    scale_one = jnp.exp2((top_one - top) * F32(EXP_SCALE))
    scale_two = jnp.exp2((top_two - top) * F32(EXP_SCALE))
    both = one * scale_one + two * scale_two
    return jnp.where(lanes(both.shape) < 32, top, both)


def divided(state):
    return state / state[:, 32:33]


def product_of(one, two):
    return jnp.dot(one, two, preferred_element_type=F32)


def pack_kernel(query_hbm, key_hbm, value_hbm, valid_hbm, out_ref, query_ref, key_ref, value_ref, valid_ref, sems):
    pairs = (
        (valid_hbm, valid_ref),
        (key_hbm, key_ref),
        (value_hbm, value_ref),
        (query_hbm, query_ref),
    )
    copies = [pltpu.make_async_copy(a, b, sems.at[i]) for i, (a, b) in enumerate(pairs)]
    for copy in copies:
        copy.start()
    for c in range(HALF_HEADS, NEAR):
        out_ref[c ^ NEAR_TURN] = jnp.zeros((2 * FIRST_BLOCK, 2 * HD), BF16)
    for copy in copies:
        copy.wait()
    square = (ROWS, 2 * HD)
    row, lane = rows(square), lanes(square)
    valid = jnp.where(row == lane, valid_ref[...].astype(F32), F32(0.0)).astype(BF16)
    hidden = product_of(valid, jnp.ones(square, BF16)) < F32(0.5)
    same_head = ((row // HD) == (lane // HD)).astype(F32).astype(BF16)
    column = lane % HD
    half = ROWS // 2
    for h in range(0, HEADS, 2):
        at = slice(h * HD, (h + 2) * HD)
        key = key_ref[:, at].astype(F32)
        product = query_ref[:, at].astype(F32) * key
        upper = product.astype(BF16)
        lower = (product - upper.astype(F32)).astype(BF16)
        own = product_of(upper, same_head) + product_of(lower, same_head)
        high = own.astype(BF16).astype(F32)
        middle = (own - high).astype(BF16).astype(F32)
        rest = own - high - middle
        code = jnp.where(column == 0, F32(MARK), jnp.where(column == 1, high, F32(0.0)))
        code = jnp.where(column == 2, middle, jnp.where(column == 3, rest, code))
        coded = jnp.where(hidden, code, key).astype(BF16)
        for part in range(2):
            head = h + part
            inner = slice(part * HD, (part + 1) * HD)
            at = slice(head * HD, (head + 1) * HD)
            to = (head % HALF_HEADS) ^ NEAR_TURN
            start = place_of(head // HALF_HEADS)
            whole, ends = pl.ds(start, ROWS), pl.ds(start + ROWS, half)
            out_ref[to, whole, 0:HD] = coded[:, inner]
            out_ref[to, whole, HD : 2 * HD] = value_ref[:, at]
            out_ref[to, ends, 0:HD] = query_ref[0:half, at]
            out_ref[to, ends, HD : 2 * HD] = query_ref[half:ROWS, at]


def turned(row):
    return (row + HALF_TURN * ROWS // 2) % ROWS


def selector_of(shift, place=lambda row: row):
    shape = (ROWS // 8, ROWS)
    return (lanes(shape) == place(shift + 8 * rows(shape))).astype(F32).astype(BF16)


def pick_middle_kernel(offsets_ref, blocks_ref, out_ref, cross_ref):
    count = ROWS // 8
    for half in range(2):
        selector = selector_of(shifts(offsets_ref, head_at(half))[0])
        start = place_of(half)
        for c in range(NEAR):
            rows_of = blocks_ref[c ^ NEAR_TURN, pl.ds(start, ROWS), :]
            picked = product_of(selector, rows_of).astype(BF16)
            for d in range(PEERS):
                place = 2 * d + (half ^ HALF_TURN)
                out_ref[place, c * count : (c + 1) * count, :] = picked
    for c in range(NEAR):
        cross_ref[c] = blocks_ref[c ^ NEAR_TURN, FIRST_BLOCK : 2 * FIRST_BLOCK, :]


def pick_outer_kernel(offsets_ref, blocks_ref, out_hbm, picked_ref, sems):
    selector = selector_of(shifts(offsets_ref)[1], turned)
    count = ROWS // 8
    for c in range(PEERS):
        picked = product_of(selector, blocks_ref[c ^ BLOCK_TURN, 0:ROWS, :]).astype(BF16)
        picked_ref[c * count : (c + 1) * count, :] = picked
    copies = [pltpu.make_async_copy(picked_ref, out_hbm.at[d], sems.at[d]) for d in range(PEERS)]
    for copy in copies:
        copy.start()
    for copy in copies:
        copy.wait()


def first_kernel(
    offsets_ref, near_ref, far_ref, state_ref, middle_ref, outer_ref, blocks_ref, wide, narrow
):
    middle, stride = shifts(offsets_ref)
    mine = my_half()
    for c in range(NEAR):
        blocks_ref[mine * NEAR + c] = near_ref[c ^ NEAR_TURN, 0:FIRST_BLOCK, :]
        blocks_ref[(1 - mine) * NEAR + c] = far_ref[c]
    half = ROWS // 2
    low = lanes((half, 2 * HD)) < HD
    diagonal = rows((ROWS, ROWS)) == lanes((ROWS, ROWS))
    reader = marks()
    seen = [against(reader, blocks_ref, c) for c in range(PEERS)]
    for j in range(PEERS):
        pair = blocks_ref[j, ROWS:FIRST_BLOCK, :].astype(F32)
        wide[j * ROWS : j * ROWS + half, :] = jnp.where(low, pair, F32(0.0))
        wide[j * ROWS + half : (j + 1) * ROWS, :] = jnp.where(
            low, pltpu.roll(pair, HD, 1), F32(0.0)
        )
        query = wide[j * ROWS : (j + 1) * ROWS, :].astype(BF16)
        masks = [diagonal if c == j else None for c in range(PEERS)]
        state_ref[j * ROWS : (j + 1) * ROWS, :] = level(query, blocks_ref, masks, seen)
    picked = wide[pl.ds(middle, ROWS, stride=8), :]
    middle_ref[...] = picked.astype(BF16)
    narrow[...] = picked
    outer_ref[...] = narrow[pl.ds(stride, ROWS // 8, stride=8), :].astype(BF16)


def middle_kernel(offsets_ref, state_ref, query_ref, blocks_ref, out_ref, merged_ref, wide):
    middle, _ = shifts(offsets_ref)
    mine = lax.axis_index("blk")
    diagonal = turned(rows((ROWS, ROWS))) == lanes((ROWS, ROWS))
    masks = [diagonal & (mine == c ^ BLOCK_TURN) for c in range(PEERS)]
    found = level(query_ref[...], blocks_ref, masks)
    both = merge(state_ref[pl.ds(middle, ROWS, stride=8), :], found)
    merged_ref[...] = both
    wide[...] = state_ref[...]
    wide[pl.ds(middle, ROWS, stride=8), :] = both
    half = ROWS // 2
    low = lanes((half, 2 * HD)) < HD
    for j in range(PEERS):
        one = divided(wide[j * ROWS : j * ROWS + half, :])
        two = divided(wide[j * ROWS + half : (j + 1) * ROWS, :])
        out_ref[j ^ HOME_TURN] = jnp.where(low, pltpu.roll(one, HD, 1), two).astype(BF16)


def outer_kernel(offsets_ref, merged_ref, query_ref, blocks_ref, before_ref, out_ref):
    middle, stride = shifts(offsets_ref)
    block, group = lax.axis_index("blk"), lax.axis_index("grp")
    count = ROWS // 8
    shape = (count, ROWS)
    diagonal = lanes(shape) == block * count + rows(shape)
    masks = [diagonal & (group == c ^ GROUP_TURN) for c in range(PEERS)]
    found = level(query_ref[...], blocks_ref, masks)
    both = divided(merge(merged_ref[pl.ds(stride, count, stride=8), :], found))
    rolled = pltpu.roll(both, HD, 1)
    tile = 16
    token = middle + 8 * stride
    start = pl.multiple_of((token // tile) * tile, tile)
    here = rows((tile, 2 * HD)) == token - start
    low = lanes((1, 2 * HD)) < HD
    for j in range(PEERS):
        row = jnp.where(low, rolled[2 * j : 2 * j + 1, :], both[2 * j + 1 : 2 * j + 2, :])
        place = j ^ HOME_TURN
        kept = before_ref[place, pl.ds(start, tile), :].astype(F32)
        out_ref[place, pl.ds(start, tile), :] = jnp.where(here, row, kept).astype(BF16)


def project_kernel(blocks_ref, weight_ref, out_hbm, out_ref, sems):
    half = ROWS // 2
    low = lanes((half, 2 * HD)) < HD
    tops, bottoms = [], []
    places = [(h // HALF_HEADS * NEAR + h % HALF_HEADS) ^ HOME_TURN for h in range(HEADS)]
    for h in range(0, HEADS, 2):
        one, two = blocks_ref[places[h]].astype(F32), blocks_ref[places[h + 1]].astype(F32)
        tops.append(jnp.where(low, one, pltpu.roll(two, HD, 1)).astype(BF16))
        bottoms.append(jnp.where(low, pltpu.roll(one, HD, 1), two).astype(BF16))
    combined = jnp.concatenate(
        [jnp.concatenate(tops, axis=1), jnp.concatenate(bottoms, axis=1)], axis=0
    )
    copies = []
    for n in range(out_ref.shape[1] // THIRD):
        at = slice(n * THIRD, (n + 1) * THIRD)
        out_ref[:, at] = product_of(combined, weight_ref[:, at]).astype(BF16)
        copies.append(pltpu.make_async_copy(out_ref.at[:, at], out_hbm.at[:, at], sems.at[n]))
        copies[-1].start()
    for copy in copies:
        copy.wait()


def call(kernel, name, out_shape, in_specs, scratch=(), flops=0, moved=0, aliases=None, out_spec=VMEM):
    outs = jax.tree.map(lambda _: out_spec, out_shape)
    return pl.pallas_call(
        kernel,
        name=name,
        out_shape=out_shape,
        in_specs=in_specs,
        out_specs=outs,
        scratch_shapes=list(scratch),
        input_output_aliases=aliases or {},
        compiler_params=pltpu.CompilerParams(vmem_limit_bytes=40 * 2**20),
        cost_estimate=pl.CostEstimate(flops=flops, bytes_accessed=moved, transcendentals=0),
    )


def shaped(*shape, dtype=BF16):
    return jax.ShapeDtypeStruct(shape, dtype)


def per_device(queries, keys, values, valid, offsets, w_out):
    wide = pltpu.VMEM((PEERS * ROWS, 2 * HD), F32)
    narrow = pltpu.VMEM((ROWS, 2 * HD), F32)
    swap = functools.partial(lax.all_to_all, split_axis=0, concat_axis=0, tiled=True)

    whole = pltpu.VMEM((ROWS, HEADS * HD), BF16)
    given = (queries, keys, values, valid.reshape(1, ROWS))
    packed = call(
        pack_kernel,
        "pack",
        shaped(NEAR, 2 * FIRST_BLOCK, 2 * HD),
        [HBM] * 4,
        [whole, whole, whole, pltpu.VMEM((1, ROWS), jnp.int32), pltpu.SemaphoreType.DMA((4,))],
    )(*(pltpu.with_memory_space_constraint(a, pltpu.HBM) for a in given))
    near_groups = [[z * NEAR + (x ^ NEAR_TURN) for x in range(NEAR)] for z in range(2)]
    near = swap(packed, "set", axis_index_groups=near_groups)
    middle_send, cross = call(
        pick_middle_kernel,
        "pick_middle",
        (shaped(2 * PEERS, ROWS // 2, 2 * HD), shaped(NEAR, FIRST_BLOCK, 2 * HD)),
        [VMEM, VMEM],
    )(offsets, near)
    middle_groups = [
        [
            (b ^ BLOCK_TURN) * PEERS + (z ^ HALF_TURN) * NEAR + x
            for b in range(PEERS)
            for z in range(2)
        ]
        for x in range(NEAR)
    ]
    middle_blocks = swap(middle_send, ("blk", "set"), axis_index_groups=middle_groups)
    middle_blocks = middle_blocks.reshape(PEERS, ROWS, 2 * HD)
    far = lax.ppermute(cross, "set", [(i, (i + NEAR) % PEERS) for i in range(PEERS)])
    state, middle_query, outer_query = call(
        first_kernel,
        "first",
        (shaped(PEERS * ROWS, 2 * HD, dtype=F32), shaped(ROWS, 2 * HD), shaped(ROWS // 8, 2 * HD)),
        [VMEM, VMEM, VMEM],
        [pltpu.VMEM((PEERS, FIRST_BLOCK, 2 * HD), BF16), wide, narrow],
        flops=6_000_000_000,
        moved=2_000_000,
    )(offsets, near, far)
    outer_send = call(
        pick_outer_kernel,
        "pick_outer",
        shaped(PEERS, ROWS, 2 * HD),
        [VMEM, VMEM],
        [pltpu.VMEM((ROWS, 2 * HD), BF16), pltpu.SemaphoreType.DMA((PEERS,))],
        out_spec=HBM,
    )(offsets, middle_blocks)
    outer_groups = [[g ^ GROUP_TURN for g in range(PEERS)]]
    outer_blocks = swap(outer_send, "grp", axis_index_groups=outer_groups)
    before, merged = call(
        middle_kernel,
        "middle",
        (shaped(PEERS, ROWS // 2, 2 * HD), shaped(ROWS, 2 * HD, dtype=F32)),
        [VMEM, VMEM, VMEM, VMEM],
        [wide],
        flops=2_000_000_000,
        moved=2_000_000,
    )(offsets, state, middle_query, middle_blocks)
    combined = call(
        outer_kernel,
        "outer",
        shaped(PEERS, ROWS // 2, 2 * HD),
        [VMEM, VMEM, VMEM, VMEM, VMEM],
        aliases={4: 0},
    )(offsets, merged, outer_query, outer_blocks, before)
    home = swap(combined, "set", axis_index_groups=[[s ^ HOME_TURN for s in range(PEERS)]])
    width = w_out.shape[1]
    return call(
        project_kernel,
        "project",
        shaped(ROWS, width),
        [VMEM, VMEM],
        [pltpu.VMEM((ROWS, width), BF16), pltpu.SemaphoreType.DMA((width // THIRD,))],
        out_spec=HBM,
    )(home, w_out)


def solution(mesh):
    spread = P(("grp", "blk", "set"), None)
    return jax.shard_map(
        per_device,
        mesh=mesh,
        in_specs=(spread, spread, spread, P(("grp", "blk", "set")), P(), P()),
        out_specs=spread,
        check_vma=False,
    )
```

```python
import functools
import math

import jax
import jax.numpy as jnp
from jax import lax
from jax.experimental import pallas as pl
from jax.experimental.pallas import tpu as pltpu
from jax.sharding import PartitionSpec as P

HEADS = 6
HD = 64
PEERS = 8
NEAR = 4
HALF_HEADS = HEADS // 2
NEAR_TURN = 3
BLOCK_TURN = 4
HALF_TURN = 1
GROUP_ORDER = (4, 2, 6, 0, 5, 3, 7, 1)
HOME_TURN = 7
ROWS = 128
FIRST_BLOCK = ROWS + ROWS // 2
MARK = 1024.0
EXP_SCALE = math.log2(math.e) / math.sqrt(HD)
FAR = -1e30
THIRD = 256
F32 = jnp.float32
BF16 = jnp.bfloat16

VMEM = pl.BlockSpec(memory_space=pltpu.VMEM)
HBM = pl.BlockSpec(memory_space=pltpu.HBM)


def lanes(shape):
    return lax.broadcasted_iota(jnp.int32, shape, len(shape) - 1)


def rows(shape):
    return lax.broadcasted_iota(jnp.int32, shape, len(shape) - 2)


def my_half():
    return lax.div(lax.axis_index("set"), NEAR)


def head_at(half):
    column = lax.rem(lax.axis_index("set"), NEAR)
    return half * HALF_HEADS + jnp.minimum(column, HALF_HEADS - 1)


def shifts(offsets_ref, head=None):
    head = head_at(my_half()) if head is None else head
    both = offsets_ref[...].astype(F32)
    both = jnp.where(lanes(both.shape) == head, both, F32(0.0))
    middle = jnp.sum(both[0:1, :]).astype(jnp.int32)
    outer = jnp.sum(both[1:2, :]).astype(jnp.int32)
    return middle, (outer - middle) // 8


def place_of(half):
    return pl.multiple_of(jnp.where(half == my_half(), 0, FIRST_BLOCK), FIRST_BLOCK)


def marks():
    shape = (16, 2 * HD)
    row, lane = rows(shape), lanes(shape)
    chosen = ((row == 0) & (lane == 0)) | ((row == 1) & (lane >= 1) & (lane <= 3))
    return chosen.astype(F32).astype(BF16)


def against(query, block_ref, index):
    return lax.dot_general(
        query, block_ref[index, 0:ROWS, :], (((1,), (1,)), ((), ())), preferred_element_type=F32
    )


def level(query, block_ref, self_masks, seen=None):
    count = query.shape[0]
    parts = []
    if seen is None:
        query = jnp.concatenate([query, marks()], axis=0)
    for c in range(PEERS):
        part = against(query, block_ref, c)
        seen_part = part[count:, :] if seen is None else seen[c]
        hidden = seen_part[0:1, :] > F32(MARK / 2)
        masked = part[0:count, :] + jnp.where(hidden, F32(FAR), F32(0.0))
        if self_masks[c] is not None:
            masked = jnp.where(self_masks[c] & hidden, seen_part[1:2, :], masked)
        parts.append(masked)
    best = functools.reduce(jnp.maximum, parts)
    top = jnp.max(best, axis=1, keepdims=True)
    sums = None
    mixture = None
    for c in range(PEERS):
        weight = jnp.exp2((parts[c] - top) * F32(EXP_SCALE))
        sums = weight if sums is None else sums + weight
        add = jnp.dot(weight.astype(BF16), block_ref[c, 0:ROWS, :], preferred_element_type=F32)
        mixture = add if mixture is None else mixture + add
    total = jnp.sum(sums, axis=1, keepdims=True)
    lane = lanes(mixture.shape)
    return jnp.where(lane < 32, top, jnp.where(lane < 64, total, mixture))


def merge(one, two):
    top_one, top_two = one[:, 0:1], two[:, 0:1]
    top = jnp.maximum(top_one, top_two)
    scale_one = jnp.exp2((top_one - top) * F32(EXP_SCALE))
    scale_two = jnp.exp2((top_two - top) * F32(EXP_SCALE))
    both = one * scale_one + two * scale_two
    return jnp.where(lanes(both.shape) < 32, top, both)


def divided(state):
    return state / state[:, 32:33]


def product_of(one, two):
    return jnp.dot(one, two, preferred_element_type=F32)


def pack_kernel(query_hbm, key_hbm, value_hbm, valid_hbm, out_ref, query_ref, key_ref, value_ref, valid_ref, sems):
    pairs = (
        (valid_hbm, valid_ref),
        (key_hbm, key_ref),
        (value_hbm, value_ref),
        (query_hbm, query_ref),
    )
    copies = [pltpu.make_async_copy(a, b, sems.at[i]) for i, (a, b) in enumerate(pairs)]
    for copy in copies:
        copy.start()
    for c in range(HALF_HEADS, NEAR):
        out_ref[c ^ NEAR_TURN] = jnp.zeros((2 * FIRST_BLOCK, 2 * HD), BF16)
    for copy in copies:
        copy.wait()
    square = (ROWS, 2 * HD)
    row, lane = rows(square), lanes(square)
    valid = jnp.where(row == lane, valid_ref[...].astype(F32), F32(0.0)).astype(BF16)
    hidden = product_of(valid, jnp.ones(square, BF16)) < F32(0.5)
    same_head = ((row // HD) == (lane // HD)).astype(F32).astype(BF16)
    column = lane % HD
    half = ROWS // 2
    for h in range(0, HEADS, 2):
        at = slice(h * HD, (h + 2) * HD)
        key = key_ref[:, at].astype(F32)
        product = query_ref[:, at].astype(F32) * key
        upper = product.astype(BF16)
        lower = (product - upper.astype(F32)).astype(BF16)
        own = product_of(upper, same_head) + product_of(lower, same_head)
        high = own.astype(BF16).astype(F32)
        middle = (own - high).astype(BF16).astype(F32)
        rest = own - high - middle
        code = jnp.where(column == 0, F32(MARK), jnp.where(column == 1, high, F32(0.0)))
        code = jnp.where(column == 2, middle, jnp.where(column == 3, rest, code))
        coded = jnp.where(hidden, code, key).astype(BF16)
        for part in range(2):
            head = h + part
            inner = slice(part * HD, (part + 1) * HD)
            at = slice(head * HD, (head + 1) * HD)
            to = (head % HALF_HEADS) ^ NEAR_TURN
            start = place_of(head // HALF_HEADS)
            whole, ends = pl.ds(start, ROWS), pl.ds(start + ROWS, half)
            out_ref[to, whole, 0:HD] = coded[:, inner]
            out_ref[to, whole, HD : 2 * HD] = value_ref[:, at]
            out_ref[to, ends, 0:HD] = query_ref[0:half, at]
            out_ref[to, ends, HD : 2 * HD] = query_ref[half:ROWS, at]


def selector_of(shift):
    shape = (ROWS // 8, ROWS)
    return (lanes(shape) == shift + 8 * rows(shape)).astype(F32).astype(BF16)


def pick_middle_kernel(offsets_ref, blocks_ref, out_ref, cross_ref):
    count = ROWS // 8
    for half in range(2):
        selector = selector_of(shifts(offsets_ref, head_at(half))[0])
        start = place_of(half)
        for c in range(NEAR):
            rows_of = blocks_ref[c ^ NEAR_TURN, pl.ds(start, ROWS), :]
            picked = product_of(selector, rows_of).astype(BF16)
            for d in range(PEERS):
                place = (half ^ HALF_TURN) * PEERS + d
                out_ref[place, c * count : (c + 1) * count, :] = picked
    for c in range(NEAR):
        cross_ref[c] = blocks_ref[c ^ NEAR_TURN, FIRST_BLOCK : 2 * FIRST_BLOCK, :]


def pick_outer_kernel(offsets_ref, blocks_ref, out_hbm, picked_ref, sems):
    selector = selector_of(shifts(offsets_ref)[1])
    count = ROWS // 8
    for c in range(PEERS):
        picked = product_of(selector, blocks_ref[c, 0:ROWS, :]).astype(BF16)
        picked_ref[c * count : (c + 1) * count, :] = picked
    copies = [pltpu.make_async_copy(picked_ref, out_hbm.at[d], sems.at[d]) for d in range(PEERS)]
    for copy in copies:
        copy.start()
    for copy in copies:
        copy.wait()


def first_kernel(
    offsets_ref, near_ref, far_ref, state_ref, middle_ref, outer_ref, blocks_ref, wide, narrow
):
    middle, stride = shifts(offsets_ref)
    mine = my_half()
    for c in range(NEAR):
        blocks_ref[mine * NEAR + c] = near_ref[c ^ NEAR_TURN, 0:FIRST_BLOCK, :]
        blocks_ref[(1 - mine) * NEAR + c] = far_ref[c]
    half = ROWS // 2
    low = lanes((half, 2 * HD)) < HD
    diagonal = rows((ROWS, ROWS)) == lanes((ROWS, ROWS))
    reader = marks()
    seen = [against(reader, blocks_ref, c) for c in range(PEERS)]
    for j in range(PEERS):
        pair = blocks_ref[j, ROWS:FIRST_BLOCK, :].astype(F32)
        wide[j * ROWS : j * ROWS + half, :] = jnp.where(low, pair, F32(0.0))
        wide[j * ROWS + half : (j + 1) * ROWS, :] = jnp.where(
            low, pltpu.roll(pair, HD, 1), F32(0.0)
        )
        query = wide[j * ROWS : (j + 1) * ROWS, :].astype(BF16)
        masks = [diagonal if c == j else None for c in range(PEERS)]
        state_ref[j * ROWS : (j + 1) * ROWS, :] = level(query, blocks_ref, masks, seen)
    picked = wide[pl.ds(middle, ROWS, stride=8), :]
    middle_ref[...] = picked.astype(BF16)
    narrow[...] = picked
    outer_ref[...] = narrow[pl.ds(stride, ROWS // 8, stride=8), :].astype(BF16)


def middle_kernel(offsets_ref, state_ref, query_ref, blocks_ref, out_ref, merged_ref, wide):
    middle, _ = shifts(offsets_ref)
    mine = lax.axis_index("blk") ^ BLOCK_TURN
    row, lane = rows((ROWS, ROWS)), lanes((ROWS, ROWS))
    count = ROWS // 2
    diagonal = lane == row % count + count * lax.rem(mine, 2)
    masks = [
        diagonal & (row // count == (c // 4) ^ HALF_TURN) & (lax.div(mine, 2) == c % 4)
        for c in range(PEERS)
    ]
    found = level(query_ref[...], blocks_ref, masks)
    both = merge(state_ref[pl.ds(middle, ROWS, stride=8), :], found)
    merged_ref[...] = both
    wide[...] = state_ref[...]
    wide[pl.ds(middle, ROWS, stride=8), :] = both
    half = ROWS // 2
    low = lanes((half, 2 * HD)) < HD
    for j in range(PEERS):
        one = divided(wide[j * ROWS : j * ROWS + half, :])
        two = divided(wide[j * ROWS + half : (j + 1) * ROWS, :])
        out_ref[j ^ HOME_TURN] = jnp.where(low, pltpu.roll(one, HD, 1), two).astype(BF16)


def outer_kernel(offsets_ref, merged_ref, query_ref, blocks_ref, before_ref, out_ref):
    middle, stride = shifts(offsets_ref)
    block, group = lax.axis_index("blk") ^ BLOCK_TURN, lax.axis_index("grp")
    count = ROWS // 8
    shape = (count, ROWS)
    row = rows(shape)
    place = ((row // 8) ^ HALF_TURN) * (ROWS // 2) + block * 8 + row % 8
    diagonal = lanes(shape) == place
    masks = [diagonal & (group == g) for g in GROUP_ORDER]
    found = level(query_ref[...], blocks_ref, masks)
    both = divided(merge(merged_ref[pl.ds(stride, count, stride=8), :], found))
    rolled = pltpu.roll(both, HD, 1)
    tile = 16
    token = middle + 8 * stride
    start = pl.multiple_of((token // tile) * tile, tile)
    here = rows((tile, 2 * HD)) == token - start
    low = lanes((1, 2 * HD)) < HD
    for j in range(PEERS):
        row = jnp.where(low, rolled[2 * j : 2 * j + 1, :], both[2 * j + 1 : 2 * j + 2, :])
        place = j ^ HOME_TURN
        kept = before_ref[place, pl.ds(start, tile), :].astype(F32)
        out_ref[place, pl.ds(start, tile), :] = jnp.where(here, row, kept).astype(BF16)


def project_kernel(blocks_ref, weight_ref, out_hbm, out_ref, sems):
    half = ROWS // 2
    low = lanes((half, 2 * HD)) < HD
    tops, bottoms = [], []
    places = [(h // HALF_HEADS * NEAR + h % HALF_HEADS) ^ HOME_TURN for h in range(HEADS)]
    for h in range(0, HEADS, 2):
        one, two = blocks_ref[places[h]].astype(F32), blocks_ref[places[h + 1]].astype(F32)
        tops.append(jnp.where(low, one, pltpu.roll(two, HD, 1)).astype(BF16))
        bottoms.append(jnp.where(low, pltpu.roll(one, HD, 1), two).astype(BF16))
    combined = jnp.concatenate(
        [jnp.concatenate(tops, axis=1), jnp.concatenate(bottoms, axis=1)], axis=0
    )
    copies = []
    for n in range(out_ref.shape[1] // THIRD):
        at = slice(n * THIRD, (n + 1) * THIRD)
        out_ref[:, at] = product_of(combined, weight_ref[:, at]).astype(BF16)
        copies.append(pltpu.make_async_copy(out_ref.at[:, at], out_hbm.at[:, at], sems.at[n]))
        copies[-1].start()
    for copy in copies:
        copy.wait()


def call(kernel, name, out_shape, in_specs, scratch=(), flops=0, moved=0, aliases=None, out_spec=VMEM):
    outs = jax.tree.map(lambda _: out_spec, out_shape)
    return pl.pallas_call(
        kernel,
        name=name,
        out_shape=out_shape,
        in_specs=in_specs,
        out_specs=outs,
        scratch_shapes=list(scratch),
        input_output_aliases=aliases or {},
        compiler_params=pltpu.CompilerParams(vmem_limit_bytes=40 * 2**20),
        cost_estimate=pl.CostEstimate(flops=flops, bytes_accessed=moved, transcendentals=0),
    )


def shaped(*shape, dtype=BF16):
    return jax.ShapeDtypeStruct(shape, dtype)


def per_device(queries, keys, values, valid, offsets, w_out):
    wide = pltpu.VMEM((PEERS * ROWS, 2 * HD), F32)
    narrow = pltpu.VMEM((ROWS, 2 * HD), F32)
    swap = functools.partial(lax.all_to_all, split_axis=0, concat_axis=0, tiled=True)

    whole = pltpu.VMEM((ROWS, HEADS * HD), BF16)
    given = (queries, keys, values, valid.reshape(1, ROWS))
    packed = call(
        pack_kernel,
        "pack",
        shaped(NEAR, 2 * FIRST_BLOCK, 2 * HD),
        [HBM] * 4,
        [whole, whole, whole, pltpu.VMEM((1, ROWS), jnp.int32), pltpu.SemaphoreType.DMA((4,))],
    )(*(pltpu.with_memory_space_constraint(a, pltpu.HBM) for a in given))
    near_groups = [[z * NEAR + (x ^ NEAR_TURN) for x in range(NEAR)] for z in range(2)]
    near = swap(packed, "set", axis_index_groups=near_groups)
    middle_send, cross = call(
        pick_middle_kernel,
        "pick_middle",
        (shaped(2 * PEERS, ROWS // 2, 2 * HD), shaped(NEAR, FIRST_BLOCK, 2 * HD)),
        [VMEM, VMEM],
    )(offsets, near)
    middle_groups = [
        [
            (b ^ BLOCK_TURN) * PEERS + (z ^ HALF_TURN) * NEAR + x
            for z in range(2)
            for b in range(PEERS)
        ]
        for x in range(NEAR)
    ]
    middle_blocks = swap(middle_send, ("blk", "set"), axis_index_groups=middle_groups)
    middle_blocks = middle_blocks.reshape(PEERS, ROWS, 2 * HD)
    far = lax.ppermute(cross, "set", [(i, (i + NEAR) % PEERS) for i in range(PEERS)])
    state, middle_query, outer_query = call(
        first_kernel,
        "first",
        (shaped(PEERS * ROWS, 2 * HD, dtype=F32), shaped(ROWS, 2 * HD), shaped(ROWS // 8, 2 * HD)),
        [VMEM, VMEM, VMEM],
        [pltpu.VMEM((PEERS, FIRST_BLOCK, 2 * HD), BF16), wide, narrow],
        flops=6_000_000_000,
        moved=2_000_000,
    )(offsets, near, far)
    outer_send = call(
        pick_outer_kernel,
        "pick_outer",
        shaped(PEERS, ROWS, 2 * HD),
        [VMEM, VMEM],
        [pltpu.VMEM((ROWS, 2 * HD), BF16), pltpu.SemaphoreType.DMA((PEERS,))],
        out_spec=HBM,
    )(offsets, middle_blocks)
    outer_blocks = swap(outer_send, "grp", axis_index_groups=[list(GROUP_ORDER)])
    before, merged = call(
        middle_kernel,
        "middle",
        (shaped(PEERS, ROWS // 2, 2 * HD), shaped(ROWS, 2 * HD, dtype=F32)),
        [VMEM, VMEM, VMEM, VMEM],
        [wide],
        flops=2_000_000_000,
        moved=2_000_000,
    )(offsets, state, middle_query, middle_blocks)
    combined = call(
        outer_kernel,
        "outer",
        shaped(PEERS, ROWS // 2, 2 * HD),
        [VMEM, VMEM, VMEM, VMEM, VMEM],
        aliases={4: 0},
    )(offsets, merged, outer_query, outer_blocks, before)
    home = swap(combined, "set", axis_index_groups=[[s ^ HOME_TURN for s in range(PEERS)]])
    width = w_out.shape[1]
    return call(
        project_kernel,
        "project",
        shaped(ROWS, width),
        [VMEM, VMEM],
        [pltpu.VMEM((ROWS, width), BF16), pltpu.SemaphoreType.DMA((width // THIRD,))],
        out_spec=HBM,
    )(home, w_out)


def solution(mesh):
    spread = P(("grp", "blk", "set"), None)
    return jax.shard_map(
        per_device,
        mesh=mesh,
        in_specs=(spread, spread, spread, P(("grp", "blk", "set")), P(), P()),
        out_specs=spread,
        check_vma=False,
    )
```

```python
import functools
import math

import jax
import jax.numpy as jnp
from jax import lax
from jax.experimental import pallas as pl
from jax.experimental.pallas import tpu as pltpu
from jax.sharding import PartitionSpec as P

HEADS = 6
HD = 64
PEERS = 8
NEAR = 4
HALF_HEADS = HEADS // 2
NEAR_TURN = 3
BLOCK_TURN = 4
HALF_TURN = 1
GROUP_ORDER = (4, 2, 6, 0, 5, 3, 7, 1)
HOME_TURN = 7
ROWS = 128
FIRST_BLOCK = ROWS + ROWS // 2
MARK = 1024.0
EXP_SCALE = math.log2(math.e) / math.sqrt(HD)
FAR = -1e30
THIRD = 256
F32 = jnp.float32
BF16 = jnp.bfloat16

VMEM = pl.BlockSpec(memory_space=pltpu.VMEM)
HBM = pl.BlockSpec(memory_space=pltpu.HBM)


def lanes(shape):
    return lax.broadcasted_iota(jnp.int32, shape, len(shape) - 1)


def rows(shape):
    return lax.broadcasted_iota(jnp.int32, shape, len(shape) - 2)


def my_half():
    return lax.div(lax.axis_index("set"), NEAR)


def head_at(half):
    column = lax.rem(lax.axis_index("set"), NEAR)
    return half * HALF_HEADS + jnp.minimum(column, HALF_HEADS - 1)


def shifts(offsets_ref, head=None):
    head = head_at(my_half()) if head is None else head
    both = offsets_ref[...].astype(F32)
    both = jnp.where(lanes(both.shape) == head, both, F32(0.0))
    middle = jnp.sum(both[0:1, :]).astype(jnp.int32)
    outer = jnp.sum(both[1:2, :]).astype(jnp.int32)
    return middle, (outer - middle) // 8


def place_of(half):
    return pl.multiple_of(jnp.where(half == my_half(), 0, FIRST_BLOCK), FIRST_BLOCK)


def marks():
    shape = (16, 2 * HD)
    row, lane = rows(shape), lanes(shape)
    chosen = ((row == 0) & (lane == 0)) | ((row == 1) & (lane >= 1) & (lane <= 3))
    return chosen.astype(F32).astype(BF16)


def product_of(one, two):
    return jnp.dot(one, two, preferred_element_type=F32)


def against(query, keys_ref):
    return lax.dot_general(
        query, keys_ref[...], (((1,), (1,)), ((), ())), preferred_element_type=F32
    )


def level(query, keys_ref, self_masks, seen=None):
    count = query.shape[0]
    if seen is None:
        found = against(jnp.concatenate([query, marks()], axis=0), keys_ref)
        seen = found[count:, :]
    else:
        found = against(query, keys_ref)
    parts = []
    for c in range(PEERS):
        at = slice(c * ROWS, (c + 1) * ROWS)
        hidden = seen[0:1, at] > F32(MARK / 2)
        masked = found[0:count, at] + jnp.where(hidden, F32(FAR), F32(0.0))
        if self_masks[c] is not None:
            masked = jnp.where(self_masks[c] & hidden, seen[1:2, at], masked)
        parts.append(masked)
    best = functools.reduce(jnp.maximum, parts)
    top = jnp.max(best, axis=1, keepdims=True)
    weights = [jnp.exp2((part - top) * F32(EXP_SCALE)) for part in parts]
    total = jnp.sum(functools.reduce(jnp.add, weights), axis=1, keepdims=True)
    probs = jnp.concatenate([weight.astype(BF16) for weight in weights], axis=1)
    mixture = product_of(probs, keys_ref[...])
    lane = lanes(mixture.shape)
    return jnp.where(lane < 32, top, jnp.where(lane < 64, total, mixture))


def merge(one, two):
    top_one, top_two = one[:, 0:1], two[:, 0:1]
    top = jnp.maximum(top_one, top_two)
    scale_one = jnp.exp2((top_one - top) * F32(EXP_SCALE))
    scale_two = jnp.exp2((top_two - top) * F32(EXP_SCALE))
    both = one * scale_one + two * scale_two
    return jnp.where(lanes(both.shape) < 32, top, both)


def divided(state):
    return state / state[:, 32:33]


def pack_kernel(query_hbm, key_hbm, value_hbm, valid_hbm, out_ref, query_ref, key_ref, value_ref, valid_ref, sems):
    pairs = (
        (valid_hbm, valid_ref),
        (key_hbm, key_ref),
        (value_hbm, value_ref),
        (query_hbm, query_ref),
    )
    copies = [pltpu.make_async_copy(a, b, sems.at[i]) for i, (a, b) in enumerate(pairs)]
    for copy in copies:
        copy.start()
    for c in range(HALF_HEADS, NEAR):
        out_ref[c ^ NEAR_TURN] = jnp.zeros((2 * FIRST_BLOCK, 2 * HD), BF16)
    for copy in copies:
        copy.wait()
    square = (ROWS, 2 * HD)
    row, lane = rows(square), lanes(square)
    valid = jnp.where(row == lane, valid_ref[...].astype(F32), F32(0.0)).astype(BF16)
    hidden = product_of(valid, jnp.ones(square, BF16)) < F32(0.5)
    same_head = ((row // HD) == (lane // HD)).astype(F32).astype(BF16)
    column = lane % HD
    half = ROWS // 2
    for h in range(0, HEADS, 2):
        at = slice(h * HD, (h + 2) * HD)
        key = key_ref[:, at].astype(F32)
        product = query_ref[:, at].astype(F32) * key
        upper = product.astype(BF16)
        lower = (product - upper.astype(F32)).astype(BF16)
        own = product_of(upper, same_head) + product_of(lower, same_head)
        high = own.astype(BF16).astype(F32)
        middle = (own - high).astype(BF16).astype(F32)
        rest = own - high - middle
        code = jnp.where(column == 0, F32(MARK), jnp.where(column == 1, high, F32(0.0)))
        code = jnp.where(column == 2, middle, jnp.where(column == 3, rest, code))
        coded = jnp.where(hidden, code, key).astype(BF16)
        for part in range(2):
            head = h + part
            inner = slice(part * HD, (part + 1) * HD)
            at = slice(head * HD, (head + 1) * HD)
            to = (head % HALF_HEADS) ^ NEAR_TURN
            start = place_of(head // HALF_HEADS)
            whole, ends = pl.ds(start, ROWS), pl.ds(start + ROWS, half)
            out_ref[to, whole, 0:HD] = coded[:, inner]
            out_ref[to, whole, HD : 2 * HD] = value_ref[:, at]
            out_ref[to, ends, 0:HD] = query_ref[0:half, at]
            out_ref[to, ends, HD : 2 * HD] = query_ref[half:ROWS, at]


def selector_of(shift):
    shape = (ROWS // 8, ROWS)
    return (lanes(shape) == shift + 8 * rows(shape)).astype(F32).astype(BF16)


def pick_middle_kernel(offsets_ref, blocks_ref, out_ref, cross_ref):
    count = ROWS // 8
    for half in range(2):
        selector = selector_of(shifts(offsets_ref, head_at(half))[0])
        start = place_of(half)
        for c in range(NEAR):
            rows_of = blocks_ref[c ^ NEAR_TURN, pl.ds(start, ROWS), :]
            picked = product_of(selector, rows_of).astype(BF16)
            for d in range(PEERS):
                place = (half ^ HALF_TURN) * PEERS + d
                out_ref[place, c * count : (c + 1) * count, :] = picked
    for c in range(NEAR):
        cross_ref[c] = blocks_ref[c ^ NEAR_TURN, FIRST_BLOCK : 2 * FIRST_BLOCK, :]


def pick_outer_kernel(offsets_ref, blocks_ref, out_hbm, picked_ref, sems):
    selector = selector_of(shifts(offsets_ref)[1])
    count = ROWS // 8
    for c in range(PEERS):
        picked = product_of(selector, blocks_ref[c, 0:ROWS, :]).astype(BF16)
        picked_ref[c * count : (c + 1) * count, :] = picked
    copies = [pltpu.make_async_copy(picked_ref, out_hbm.at[d], sems.at[d]) for d in range(PEERS)]
    for copy in copies:
        copy.start()
    for copy in copies:
        copy.wait()


def first_kernel(
    offsets_ref, near_ref, far_ref, state_ref, middle_ref, outer_ref, keys_ref, pairs_ref, wide, narrow
):
    middle, stride = shifts(offsets_ref)
    mine = my_half()
    for c in range(NEAR):
        for half, ref, place in ((mine, near_ref, c ^ NEAR_TURN), (1 - mine, far_ref, c)):
            block = half * NEAR + c
            start = pl.multiple_of(block * ROWS, ROWS)
            keys_ref[pl.ds(start, ROWS), :] = ref[place, 0:ROWS, :]
            pairs_ref[block] = ref[place, ROWS:FIRST_BLOCK, :]
    half = ROWS // 2
    low = lanes((half, 2 * HD)) < HD
    diagonal = rows((ROWS, ROWS)) == lanes((ROWS, ROWS))
    seen = against(marks(), keys_ref)
    for j in range(PEERS):
        pair = pairs_ref[j].astype(F32)
        wide[j * ROWS : j * ROWS + half, :] = jnp.where(low, pair, F32(0.0))
        wide[j * ROWS + half : (j + 1) * ROWS, :] = jnp.where(
            low, pltpu.roll(pair, HD, 1), F32(0.0)
        )
        query = wide[j * ROWS : (j + 1) * ROWS, :].astype(BF16)
        masks = [diagonal if c == j else None for c in range(PEERS)]
        state_ref[j * ROWS : (j + 1) * ROWS, :] = level(query, keys_ref, masks, seen)
    picked = wide[pl.ds(middle, ROWS, stride=8), :]
    middle_ref[...] = picked.astype(BF16)
    narrow[...] = picked
    outer_ref[...] = narrow[pl.ds(stride, ROWS // 8, stride=8), :].astype(BF16)


def middle_kernel(offsets_ref, state_ref, query_ref, blocks_ref, out_ref, merged_ref, wide):
    middle, _ = shifts(offsets_ref)
    mine = lax.axis_index("blk") ^ BLOCK_TURN
    row, lane = rows((ROWS, ROWS)), lanes((ROWS, ROWS))
    count = ROWS // 2
    diagonal = lane == row % count + count * lax.rem(mine, 2)
    masks = [
        diagonal & (row // count == (c // 4) ^ HALF_TURN) & (lax.div(mine, 2) == c % 4)
        for c in range(PEERS)
    ]
    found = level(query_ref[...], blocks_ref, masks)
    both = merge(state_ref[pl.ds(middle, ROWS, stride=8), :], found)
    merged_ref[...] = both
    wide[...] = state_ref[...]
    wide[pl.ds(middle, ROWS, stride=8), :] = both
    half = ROWS // 2
    low = lanes((half, 2 * HD)) < HD
    for j in range(PEERS):
        one = divided(wide[j * ROWS : j * ROWS + half, :])
        two = divided(wide[j * ROWS + half : (j + 1) * ROWS, :])
        out_ref[j ^ HOME_TURN] = jnp.where(low, pltpu.roll(one, HD, 1), two).astype(BF16)


def outer_kernel(offsets_ref, merged_ref, query_ref, blocks_ref, before_ref, out_ref):
    middle, stride = shifts(offsets_ref)
    block, group = lax.axis_index("blk") ^ BLOCK_TURN, lax.axis_index("grp")
    count = ROWS // 8
    shape = (count, ROWS)
    row = rows(shape)
    place = ((row // 8) ^ HALF_TURN) * (ROWS // 2) + block * 8 + row % 8
    diagonal = lanes(shape) == place
    masks = [diagonal & (group == g) for g in GROUP_ORDER]
    found = level(query_ref[...], blocks_ref, masks)
    both = divided(merge(merged_ref[pl.ds(stride, count, stride=8), :], found))
    rolled = pltpu.roll(both, HD, 1)
    tile = 16
    token = middle + 8 * stride
    start = pl.multiple_of((token // tile) * tile, tile)
    here = rows((tile, 2 * HD)) == token - start
    low = lanes((1, 2 * HD)) < HD
    for j in range(PEERS):
        row = jnp.where(low, rolled[2 * j : 2 * j + 1, :], both[2 * j + 1 : 2 * j + 2, :])
        place = j ^ HOME_TURN
        kept = before_ref[place, pl.ds(start, tile), :].astype(F32)
        out_ref[place, pl.ds(start, tile), :] = jnp.where(here, row, kept).astype(BF16)


def project_kernel(blocks_ref, weight_ref, out_hbm, out_ref, sems):
    half = ROWS // 2
    low = lanes((half, 2 * HD)) < HD
    tops, bottoms = [], []
    places = [(h // HALF_HEADS * NEAR + h % HALF_HEADS) ^ HOME_TURN for h in range(HEADS)]
    for h in range(0, HEADS, 2):
        one, two = blocks_ref[places[h]].astype(F32), blocks_ref[places[h + 1]].astype(F32)
        tops.append(jnp.where(low, one, pltpu.roll(two, HD, 1)).astype(BF16))
        bottoms.append(jnp.where(low, pltpu.roll(one, HD, 1), two).astype(BF16))
    combined = jnp.concatenate(
        [jnp.concatenate(tops, axis=1), jnp.concatenate(bottoms, axis=1)], axis=0
    )
    copies = []
    for n in range(out_ref.shape[1] // THIRD):
        at = slice(n * THIRD, (n + 1) * THIRD)
        out_ref[:, at] = product_of(combined, weight_ref[:, at]).astype(BF16)
        copies.append(pltpu.make_async_copy(out_ref.at[:, at], out_hbm.at[:, at], sems.at[n]))
        copies[-1].start()
    for copy in copies:
        copy.wait()


def call(kernel, name, out_shape, in_specs, scratch=(), flops=0, moved=0, aliases=None, out_spec=VMEM):
    outs = jax.tree.map(lambda _: out_spec, out_shape)
    return pl.pallas_call(
        kernel,
        name=name,
        out_shape=out_shape,
        in_specs=in_specs,
        out_specs=outs,
        scratch_shapes=list(scratch),
        input_output_aliases=aliases or {},
        compiler_params=pltpu.CompilerParams(vmem_limit_bytes=40 * 2**20),
        cost_estimate=pl.CostEstimate(flops=flops, bytes_accessed=moved, transcendentals=0),
    )


def shaped(*shape, dtype=BF16):
    return jax.ShapeDtypeStruct(shape, dtype)


def per_device(queries, keys, values, valid, offsets, w_out):
    wide = pltpu.VMEM((PEERS * ROWS, 2 * HD), F32)
    narrow = pltpu.VMEM((ROWS, 2 * HD), F32)
    swap = functools.partial(lax.all_to_all, split_axis=0, concat_axis=0, tiled=True)

    whole = pltpu.VMEM((ROWS, HEADS * HD), BF16)
    given = (queries, keys, values, valid.reshape(1, ROWS))
    packed = call(
        pack_kernel,
        "pack",
        shaped(NEAR, 2 * FIRST_BLOCK, 2 * HD),
        [HBM] * 4,
        [whole, whole, whole, pltpu.VMEM((1, ROWS), jnp.int32), pltpu.SemaphoreType.DMA((4,))],
    )(*(pltpu.with_memory_space_constraint(a, pltpu.HBM) for a in given))
    near_groups = [[z * NEAR + (x ^ NEAR_TURN) for x in range(NEAR)] for z in range(2)]
    near = swap(packed, "set", axis_index_groups=near_groups)
    middle_send, cross = call(
        pick_middle_kernel,
        "pick_middle",
        (shaped(2 * PEERS, ROWS // 2, 2 * HD), shaped(NEAR, FIRST_BLOCK, 2 * HD)),
        [VMEM, VMEM],
    )(offsets, near)
    middle_groups = [
        [
            (b ^ BLOCK_TURN) * PEERS + (z ^ HALF_TURN) * NEAR + x
            for z in range(2)
            for b in range(PEERS)
        ]
        for x in range(NEAR)
    ]
    middle_blocks = swap(middle_send, ("blk", "set"), axis_index_groups=middle_groups)
    middle_blocks = middle_blocks.reshape(PEERS, ROWS, 2 * HD)
    far = lax.ppermute(cross, "set", [(i, (i + NEAR) % PEERS) for i in range(PEERS)])
    state, middle_query, outer_query = call(
        first_kernel,
        "first",
        (shaped(PEERS * ROWS, 2 * HD, dtype=F32), shaped(ROWS, 2 * HD), shaped(ROWS // 8, 2 * HD)),
        [VMEM, VMEM, VMEM],
        [
            pltpu.VMEM((PEERS * ROWS, 2 * HD), BF16),
            pltpu.VMEM((PEERS, ROWS // 2, 2 * HD), BF16),
            wide,
            narrow,
        ],
        flops=6_000_000_000,
        moved=2_000_000,
    )(offsets, near, far)
    outer_send = call(
        pick_outer_kernel,
        "pick_outer",
        shaped(PEERS, ROWS, 2 * HD),
        [VMEM, VMEM],
        [pltpu.VMEM((ROWS, 2 * HD), BF16), pltpu.SemaphoreType.DMA((PEERS,))],
        out_spec=HBM,
    )(offsets, middle_blocks)
    outer_blocks = swap(outer_send, "grp", axis_index_groups=[list(GROUP_ORDER)])
    before, merged = call(
        middle_kernel,
        "middle",
        (shaped(PEERS, ROWS // 2, 2 * HD), shaped(ROWS, 2 * HD, dtype=F32)),
        [VMEM, VMEM, VMEM, VMEM],
        [wide],
        flops=2_000_000_000,
        moved=2_000_000,
    )(offsets, state, middle_query, middle_blocks.reshape(PEERS * ROWS, 2 * HD))
    combined = call(
        outer_kernel,
        "outer",
        shaped(PEERS, ROWS // 2, 2 * HD),
        [VMEM, VMEM, VMEM, VMEM, VMEM],
        aliases={4: 0},
    )(offsets, merged, outer_query, outer_blocks.reshape(PEERS * ROWS, 2 * HD), before)
    home = swap(combined, "set", axis_index_groups=[[s ^ HOME_TURN for s in range(PEERS)]])
    width = w_out.shape[1]
    return call(
        project_kernel,
        "project",
        shaped(ROWS, width),
        [VMEM, VMEM],
        [pltpu.VMEM((ROWS, width), BF16), pltpu.SemaphoreType.DMA((width // THIRD,))],
        out_spec=HBM,
    )(home, w_out)


def solution(mesh):
    spread = P(("grp", "blk", "set"), None)
    return jax.shard_map(
        per_device,
        mesh=mesh,
        in_specs=(spread, spread, spread, P(("grp", "blk", "set")), P(), P()),
        out_specs=spread,
        check_vma=False,
    )
```

```python
import functools
import math

import jax
import jax.numpy as jnp
from jax import lax
from jax.experimental import pallas as pl
from jax.experimental.pallas import tpu as pltpu
from jax.sharding import PartitionSpec as P

HEADS = 6
HD = 64
PEERS = 8
NEAR = 4
HALF_HEADS = HEADS // 2
NEAR_TURN = 3
BLOCK_TURN = 4
HALF_TURN = 1
GROUP_ORDER = (6, 4, 2, 0, 7, 5, 3, 1)
HOME_TURN = 7
ROWS = 128
FIRST_BLOCK = ROWS + ROWS // 2
MARK = 1024.0
EXP_SCALE = math.log2(math.e) / math.sqrt(HD)
FAR = -1e30
THIRD = 256
F32 = jnp.float32
BF16 = jnp.bfloat16

VMEM = pl.BlockSpec(memory_space=pltpu.VMEM)
HBM = pl.BlockSpec(memory_space=pltpu.HBM)


def lanes(shape):
    return lax.broadcasted_iota(jnp.int32, shape, len(shape) - 1)


def rows(shape):
    return lax.broadcasted_iota(jnp.int32, shape, len(shape) - 2)


def my_half():
    return lax.div(lax.axis_index("set"), NEAR)


def head_at(half):
    column = lax.rem(lax.axis_index("set"), NEAR)
    return half * HALF_HEADS + jnp.minimum(column, HALF_HEADS - 1)


def shifts(offsets_ref, head=None):
    head = head_at(my_half()) if head is None else head
    both = offsets_ref[...].astype(F32)
    both = jnp.where(lanes(both.shape) == head, both, F32(0.0))
    middle = jnp.sum(both[0:1, :]).astype(jnp.int32)
    outer = jnp.sum(both[1:2, :]).astype(jnp.int32)
    return middle, (outer - middle) // 8


def place_of(half):
    return pl.multiple_of(jnp.where(half == my_half(), 0, FIRST_BLOCK), FIRST_BLOCK)


def marks():
    shape = (16, 2 * HD)
    row, lane = rows(shape), lanes(shape)
    chosen = ((row == 0) & (lane == 0)) | ((row == 1) & (lane >= 1) & (lane <= 3))
    return chosen.astype(F32).astype(BF16)


def product_of(one, two):
    return jnp.dot(one, two, preferred_element_type=F32)


def against(query, keys_ref):
    return lax.dot_general(
        query, keys_ref[...], (((1,), (1,)), ((), ())), preferred_element_type=F32
    )


def level(query, keys_ref, self_masks, seen=None):
    count = query.shape[0]
    if seen is None:
        found = against(jnp.concatenate([query, marks()], axis=0), keys_ref)
        seen = found[count:, :]
    else:
        found = against(query, keys_ref)
    parts = []
    for c in range(PEERS):
        at = slice(c * ROWS, (c + 1) * ROWS)
        hidden = seen[0:1, at] > F32(MARK / 2)
        masked = found[0:count, at] + jnp.where(hidden, F32(FAR), F32(0.0))
        if self_masks[c] is not None:
            masked = jnp.where(self_masks[c] & hidden, seen[1:2, at], masked)
        parts.append(masked)
    best = functools.reduce(jnp.maximum, parts)
    top = jnp.max(best, axis=1, keepdims=True)
    weights = [jnp.exp2((part - top) * F32(EXP_SCALE)) for part in parts]
    total = jnp.sum(functools.reduce(jnp.add, weights), axis=1, keepdims=True)
    probs = jnp.concatenate([weight.astype(BF16) for weight in weights], axis=1)
    mixture = product_of(probs, keys_ref[...])
    lane = lanes(mixture.shape)
    return jnp.where(lane < 32, top, jnp.where(lane < 64, total, mixture))


def merge(one, two):
    top_one, top_two = one[:, 0:1], two[:, 0:1]
    top = jnp.maximum(top_one, top_two)
    scale_one = jnp.exp2((top_one - top) * F32(EXP_SCALE))
    scale_two = jnp.exp2((top_two - top) * F32(EXP_SCALE))
    both = one * scale_one + two * scale_two
    return jnp.where(lanes(both.shape) < 32, top, both)


def divided(state):
    return state / state[:, 32:33]


def pack_kernel(query_hbm, key_hbm, value_hbm, valid_hbm, out_ref, query_ref, key_ref, value_ref, valid_ref, sems):
    pairs = (
        (valid_hbm, valid_ref),
        (key_hbm, key_ref),
        (value_hbm, value_ref),
        (query_hbm, query_ref),
    )
    copies = [pltpu.make_async_copy(a, b, sems.at[i]) for i, (a, b) in enumerate(pairs)]
    for copy in copies:
        copy.start()
    for c in range(HALF_HEADS, NEAR):
        out_ref[c ^ NEAR_TURN] = jnp.zeros((2 * FIRST_BLOCK, 2 * HD), BF16)
    for copy in copies:
        copy.wait()
    square = (ROWS, 2 * HD)
    row, lane = rows(square), lanes(square)
    valid = jnp.where(row == lane, valid_ref[...].astype(F32), F32(0.0)).astype(BF16)
    hidden = product_of(valid, jnp.ones(square, BF16)) < F32(0.5)
    same_head = ((row // HD) == (lane // HD)).astype(F32).astype(BF16)
    column = lane % HD
    half = ROWS // 2
    for h in range(0, HEADS, 2):
        at = slice(h * HD, (h + 2) * HD)
        key = key_ref[:, at].astype(F32)
        product = query_ref[:, at].astype(F32) * key
        upper = product.astype(BF16)
        lower = (product - upper.astype(F32)).astype(BF16)
        own = product_of(upper, same_head) + product_of(lower, same_head)
        high = own.astype(BF16).astype(F32)
        middle = (own - high).astype(BF16).astype(F32)
        rest = own - high - middle
        code = jnp.where(column == 0, F32(MARK), jnp.where(column == 1, high, F32(0.0)))
        code = jnp.where(column == 2, middle, jnp.where(column == 3, rest, code))
        coded = jnp.where(hidden, code, key).astype(BF16)
        for part in range(2):
            head = h + part
            inner = slice(part * HD, (part + 1) * HD)
            at = slice(head * HD, (head + 1) * HD)
            to = (head % HALF_HEADS) ^ NEAR_TURN
            start = place_of(head // HALF_HEADS)
            whole, ends = pl.ds(start, ROWS), pl.ds(start + ROWS, half)
            out_ref[to, whole, 0:HD] = coded[:, inner]
            out_ref[to, whole, HD : 2 * HD] = value_ref[:, at]
            out_ref[to, ends, 0:HD] = query_ref[0:half, at]
            out_ref[to, ends, HD : 2 * HD] = query_ref[half:ROWS, at]


def selector_of(shift):
    shape = (ROWS // 8, ROWS)
    return (lanes(shape) == shift + 8 * rows(shape)).astype(F32).astype(BF16)


def pick_middle_kernel(offsets_ref, blocks_ref, out_ref, cross_ref):
    count = ROWS // 8
    for half in range(2):
        selector = selector_of(shifts(offsets_ref, head_at(half))[0])
        start = place_of(half)
        for c in range(NEAR):
            rows_of = blocks_ref[c ^ NEAR_TURN, pl.ds(start, ROWS), :]
            picked = product_of(selector, rows_of).astype(BF16)
            for d in range(PEERS):
                place = (half ^ HALF_TURN) * PEERS + d
                out_ref[place, c * count : (c + 1) * count, :] = picked
    for c in range(NEAR):
        cross_ref[c] = blocks_ref[c ^ NEAR_TURN, FIRST_BLOCK : 2 * FIRST_BLOCK, :]


def pick_outer_kernel(offsets_ref, blocks_ref, out_hbm, picked_ref, sems):
    selector = selector_of(shifts(offsets_ref)[1])
    count = ROWS // 8
    for c in range(PEERS):
        picked = product_of(selector, blocks_ref[c, 0:ROWS, :]).astype(BF16)
        picked_ref[c * count : (c + 1) * count, :] = picked
    copies = [pltpu.make_async_copy(picked_ref, out_hbm.at[d], sems.at[d]) for d in range(PEERS)]
    for copy in copies:
        copy.start()
    for copy in copies:
        copy.wait()


def first_kernel(
    offsets_ref, near_ref, far_ref, state_ref, middle_ref, outer_ref, keys_ref, pairs_ref, wide, narrow
):
    middle, stride = shifts(offsets_ref)
    mine = my_half()
    for c in range(NEAR):
        for half, ref, place in ((mine, near_ref, c ^ NEAR_TURN), (1 - mine, far_ref, c)):
            block = half * NEAR + c
            start = pl.multiple_of(block * ROWS, ROWS)
            keys_ref[pl.ds(start, ROWS), :] = ref[place, 0:ROWS, :]
            pairs_ref[block] = ref[place, ROWS:FIRST_BLOCK, :]
    half = ROWS // 2
    low = lanes((half, 2 * HD)) < HD
    diagonal = rows((ROWS, ROWS)) == lanes((ROWS, ROWS))
    seen = against(marks(), keys_ref)
    for j in range(PEERS):
        pair = pairs_ref[j].astype(F32)
        wide[j * ROWS : j * ROWS + half, :] = jnp.where(low, pair, F32(0.0))
        wide[j * ROWS + half : (j + 1) * ROWS, :] = jnp.where(
            low, pltpu.roll(pair, HD, 1), F32(0.0)
        )
        query = wide[j * ROWS : (j + 1) * ROWS, :].astype(BF16)
        masks = [diagonal if c == j else None for c in range(PEERS)]
        state_ref[j * ROWS : (j + 1) * ROWS, :] = level(query, keys_ref, masks, seen)
    picked = wide[pl.ds(middle, ROWS, stride=8), :]
    middle_ref[...] = picked.astype(BF16)
    narrow[...] = picked
    outer_ref[...] = narrow[pl.ds(stride, ROWS // 8, stride=8), :].astype(BF16)


def middle_kernel(offsets_ref, state_ref, query_ref, blocks_ref, out_ref, merged_ref, wide):
    middle, _ = shifts(offsets_ref)
    mine = lax.axis_index("blk") ^ BLOCK_TURN
    row, lane = rows((ROWS, ROWS)), lanes((ROWS, ROWS))
    count = ROWS // 2
    diagonal = lane == row % count + count * lax.rem(mine, 2)
    masks = [
        diagonal & (row // count == (c // 4) ^ HALF_TURN) & (lax.div(mine, 2) == c % 4)
        for c in range(PEERS)
    ]
    found = level(query_ref[...], blocks_ref, masks)
    both = merge(state_ref[pl.ds(middle, ROWS, stride=8), :], found)
    merged_ref[...] = both
    wide[...] = state_ref[...]
    wide[pl.ds(middle, ROWS, stride=8), :] = both
    half = ROWS // 2
    low = lanes((half, 2 * HD)) < HD
    for j in range(PEERS):
        one = divided(wide[j * ROWS : j * ROWS + half, :])
        two = divided(wide[j * ROWS + half : (j + 1) * ROWS, :])
        out_ref[j ^ HOME_TURN] = jnp.where(low, pltpu.roll(one, HD, 1), two).astype(BF16)


def outer_kernel(offsets_ref, merged_ref, query_ref, blocks_ref, before_ref, out_ref):
    middle, stride = shifts(offsets_ref)
    block, group = lax.axis_index("blk") ^ BLOCK_TURN, lax.axis_index("grp")
    count = ROWS // 8
    shape = (count, ROWS)
    row = rows(shape)
    place = ((row // 8) ^ HALF_TURN) * (ROWS // 2) + block * 8 + row % 8
    diagonal = lanes(shape) == place
    masks = [diagonal & (group == g) for g in GROUP_ORDER]
    found = level(query_ref[...], blocks_ref, masks)
    both = divided(merge(merged_ref[pl.ds(stride, count, stride=8), :], found))
    rolled = pltpu.roll(both, HD, 1)
    tile = 16
    token = middle + 8 * stride
    start = pl.multiple_of((token // tile) * tile, tile)
    here = rows((tile, 2 * HD)) == token - start
    low = lanes((1, 2 * HD)) < HD
    for j in range(PEERS):
        row = jnp.where(low, rolled[2 * j : 2 * j + 1, :], both[2 * j + 1 : 2 * j + 2, :])
        place = j ^ HOME_TURN
        kept = before_ref[place, pl.ds(start, tile), :].astype(F32)
        out_ref[place, pl.ds(start, tile), :] = jnp.where(here, row, kept).astype(BF16)


def project_kernel(blocks_ref, weight_ref, out_hbm, out_ref, sems):
    half = ROWS // 2
    low = lanes((half, 2 * HD)) < HD
    tops, bottoms = [], []
    places = [(h // HALF_HEADS * NEAR + h % HALF_HEADS) ^ HOME_TURN for h in range(HEADS)]
    for h in range(0, HEADS, 2):
        one, two = blocks_ref[places[h]].astype(F32), blocks_ref[places[h + 1]].astype(F32)
        tops.append(jnp.where(low, one, pltpu.roll(two, HD, 1)).astype(BF16))
        bottoms.append(jnp.where(low, pltpu.roll(one, HD, 1), two).astype(BF16))
    combined = jnp.concatenate(
        [jnp.concatenate(tops, axis=1), jnp.concatenate(bottoms, axis=1)], axis=0
    )
    copies = []
    for n in range(out_ref.shape[1] // THIRD):
        at = slice(n * THIRD, (n + 1) * THIRD)
        out_ref[:, at] = product_of(combined, weight_ref[:, at]).astype(BF16)
        copies.append(pltpu.make_async_copy(out_ref.at[:, at], out_hbm.at[:, at], sems.at[n]))
        copies[-1].start()
    for copy in copies:
        copy.wait()


def call(kernel, name, out_shape, in_specs, scratch=(), flops=0, moved=0, aliases=None, out_spec=VMEM):
    outs = jax.tree.map(lambda _: out_spec, out_shape)
    return pl.pallas_call(
        kernel,
        name=name,
        out_shape=out_shape,
        in_specs=in_specs,
        out_specs=outs,
        scratch_shapes=list(scratch),
        input_output_aliases=aliases or {},
        compiler_params=pltpu.CompilerParams(vmem_limit_bytes=40 * 2**20),
        cost_estimate=pl.CostEstimate(flops=flops, bytes_accessed=moved, transcendentals=0),
    )


def shaped(*shape, dtype=BF16):
    return jax.ShapeDtypeStruct(shape, dtype)


def per_device(queries, keys, values, valid, offsets, w_out):
    wide = pltpu.VMEM((PEERS * ROWS, 2 * HD), F32)
    narrow = pltpu.VMEM((ROWS, 2 * HD), F32)
    swap = functools.partial(lax.all_to_all, split_axis=0, concat_axis=0, tiled=True)

    whole = pltpu.VMEM((ROWS, HEADS * HD), BF16)
    given = (queries, keys, values, valid.reshape(1, ROWS))
    packed = call(
        pack_kernel,
        "pack",
        shaped(NEAR, 2 * FIRST_BLOCK, 2 * HD),
        [HBM] * 4,
        [whole, whole, whole, pltpu.VMEM((1, ROWS), jnp.int32), pltpu.SemaphoreType.DMA((4,))],
    )(*(pltpu.with_memory_space_constraint(a, pltpu.HBM) for a in given))
    near_groups = [[z * NEAR + (x ^ NEAR_TURN) for x in range(NEAR)] for z in range(2)]
    near = swap(packed, "set", axis_index_groups=near_groups)
    middle_send, cross = call(
        pick_middle_kernel,
        "pick_middle",
        (shaped(2 * PEERS, ROWS // 2, 2 * HD), shaped(NEAR, FIRST_BLOCK, 2 * HD)),
        [VMEM, VMEM],
    )(offsets, near)
    middle_groups = [
        [
            (b ^ BLOCK_TURN) * PEERS + (z ^ HALF_TURN) * NEAR + x
            for z in range(2)
            for b in range(PEERS)
        ]
        for x in range(NEAR)
    ]
    middle_blocks = swap(middle_send, ("blk", "set"), axis_index_groups=middle_groups)
    middle_blocks = middle_blocks.reshape(PEERS, ROWS, 2 * HD)
    far = lax.ppermute(cross, "set", [(i, (i + NEAR) % PEERS) for i in range(PEERS)])
    state, middle_query, outer_query = call(
        first_kernel,
        "first",
        (shaped(PEERS * ROWS, 2 * HD, dtype=F32), shaped(ROWS, 2 * HD), shaped(ROWS // 8, 2 * HD)),
        [VMEM, VMEM, VMEM],
        [
            pltpu.VMEM((PEERS * ROWS, 2 * HD), BF16),
            pltpu.VMEM((PEERS, ROWS // 2, 2 * HD), BF16),
            wide,
            narrow,
        ],
        flops=6_000_000_000,
        moved=2_000_000,
    )(offsets, near, far)
    outer_send = call(
        pick_outer_kernel,
        "pick_outer",
        shaped(PEERS, ROWS, 2 * HD),
        [VMEM, VMEM],
        [pltpu.VMEM((ROWS, 2 * HD), BF16), pltpu.SemaphoreType.DMA((PEERS,))],
        out_spec=HBM,
    )(offsets, middle_blocks)
    outer_blocks = swap(outer_send, "grp", axis_index_groups=[list(GROUP_ORDER)])
    before, merged = call(
        middle_kernel,
        "middle",
        (shaped(PEERS, ROWS // 2, 2 * HD), shaped(ROWS, 2 * HD, dtype=F32)),
        [VMEM, VMEM, VMEM, VMEM],
        [wide],
        flops=2_000_000_000,
        moved=2_000_000,
    )(offsets, state, middle_query, middle_blocks.reshape(PEERS * ROWS, 2 * HD))
    combined = call(
        outer_kernel,
        "outer",
        shaped(PEERS, ROWS // 2, 2 * HD),
        [VMEM, VMEM, VMEM, VMEM, VMEM],
        aliases={4: 0},
    )(offsets, merged, outer_query, outer_blocks.reshape(PEERS * ROWS, 2 * HD), before)
    home = swap(combined, "set", axis_index_groups=[[s ^ HOME_TURN for s in range(PEERS)]])
    width = w_out.shape[1]
    return call(
        project_kernel,
        "project",
        shaped(ROWS, width),
        [VMEM, VMEM],
        [pltpu.VMEM((ROWS, width), BF16), pltpu.SemaphoreType.DMA((width // THIRD,))],
        out_spec=HBM,
    )(home, w_out)


def solution(mesh):
    spread = P(("grp", "blk", "set"), None)
    return jax.shard_map(
        per_device,
        mesh=mesh,
        in_specs=(spread, spread, spread, P(("grp", "blk", "set")), P(), P()),
        out_specs=spread,
        check_vma=False,
    )
```

```python
import functools
import math

import jax
import jax.numpy as jnp
from jax import lax
from jax.experimental import pallas as pl
from jax.experimental.pallas import tpu as pltpu
from jax.sharding import PartitionSpec as P

HEADS = 6
HD = 64
PEERS = 8
NEAR = 4
HALF_HEADS = HEADS // 2
NEAR_TURN = 3
BLOCK_TURN = 4
HALF_TURN = 1
GROUP_ORDER = (6, 4, 7, 5, 2, 0, 3, 1)
HOME_TURN = 7
ROWS = 128
FIRST_BLOCK = ROWS + ROWS // 2
MARK = 1024.0
EXP_SCALE = math.log2(math.e) / math.sqrt(HD)
FAR = -1e30
THIRD = 256
F32 = jnp.float32
BF16 = jnp.bfloat16

VMEM = pl.BlockSpec(memory_space=pltpu.VMEM)
HBM = pl.BlockSpec(memory_space=pltpu.HBM)


def lanes(shape):
    return lax.broadcasted_iota(jnp.int32, shape, len(shape) - 1)


def rows(shape):
    return lax.broadcasted_iota(jnp.int32, shape, len(shape) - 2)


def my_half():
    return lax.div(lax.axis_index("set"), NEAR)


def head_at(half):
    column = lax.rem(lax.axis_index("set"), NEAR)
    return half * HALF_HEADS + jnp.minimum(column, HALF_HEADS - 1)


def shifts(offsets_ref, head=None):
    head = head_at(my_half()) if head is None else head
    both = offsets_ref[...].astype(F32)
    both = jnp.where(lanes(both.shape) == head, both, F32(0.0))
    middle = jnp.sum(both[0:1, :]).astype(jnp.int32)
    outer = jnp.sum(both[1:2, :]).astype(jnp.int32)
    return middle, (outer - middle) // 8


def place_of(half):
    return pl.multiple_of(jnp.where(half == my_half(), 0, FIRST_BLOCK), FIRST_BLOCK)


def marks():
    shape = (16, 2 * HD)
    row, lane = rows(shape), lanes(shape)
    chosen = ((row == 0) & (lane == 0)) | ((row == 1) & (lane >= 1) & (lane <= 3))
    return chosen.astype(F32).astype(BF16)


def product_of(one, two):
    return jnp.dot(one, two, preferred_element_type=F32)


def against(query, keys_ref):
    return lax.dot_general(
        query, keys_ref[...], (((1,), (1,)), ((), ())), preferred_element_type=F32
    )


def level(query, keys_ref, self_masks, seen=None):
    count = query.shape[0]
    if seen is None:
        found = against(jnp.concatenate([query, marks()], axis=0), keys_ref)
        seen = found[count:, :]
    else:
        found = against(query, keys_ref)
    parts = []
    for c in range(PEERS):
        at = slice(c * ROWS, (c + 1) * ROWS)
        hidden = seen[0:1, at] > F32(MARK / 2)
        masked = found[0:count, at] + jnp.where(hidden, F32(FAR), F32(0.0))
        if self_masks[c] is not None:
            masked = jnp.where(self_masks[c] & hidden, seen[1:2, at], masked)
        parts.append(masked)
    best = functools.reduce(jnp.maximum, parts)
    top = jnp.max(best, axis=1, keepdims=True)
    weights = [jnp.exp2((part - top) * F32(EXP_SCALE)) for part in parts]
    total = jnp.sum(functools.reduce(jnp.add, weights), axis=1, keepdims=True)
    probs = jnp.concatenate([weight.astype(BF16) for weight in weights], axis=1)
    mixture = product_of(probs, keys_ref[...])
    lane = lanes(mixture.shape)
    return jnp.where(lane < 32, top, jnp.where(lane < 64, total, mixture))


def merge(one, two):
    top_one, top_two = one[:, 0:1], two[:, 0:1]
    top = jnp.maximum(top_one, top_two)
    scale_one = jnp.exp2((top_one - top) * F32(EXP_SCALE))
    scale_two = jnp.exp2((top_two - top) * F32(EXP_SCALE))
    both = one * scale_one + two * scale_two
    return jnp.where(lanes(both.shape) < 32, top, both)


def divided(state):
    return state / state[:, 32:33]


def pack_kernel(query_hbm, key_hbm, value_hbm, valid_hbm, out_ref, query_ref, key_ref, value_ref, valid_ref, sems):
    pairs = (
        (valid_hbm, valid_ref),
        (key_hbm, key_ref),
        (value_hbm, value_ref),
        (query_hbm, query_ref),
    )
    copies = [pltpu.make_async_copy(a, b, sems.at[i]) for i, (a, b) in enumerate(pairs)]
    for copy in copies:
        copy.start()
    for c in range(HALF_HEADS, NEAR):
        out_ref[c ^ NEAR_TURN] = jnp.zeros((2 * FIRST_BLOCK, 2 * HD), BF16)
    for copy in copies:
        copy.wait()
    square = (ROWS, 2 * HD)
    row, lane = rows(square), lanes(square)
    valid = jnp.where(row == lane, valid_ref[...].astype(F32), F32(0.0)).astype(BF16)
    hidden = product_of(valid, jnp.ones(square, BF16)) < F32(0.5)
    same_head = ((row // HD) == (lane // HD)).astype(F32).astype(BF16)
    column = lane % HD
    half = ROWS // 2
    for h in range(0, HEADS, 2):
        at = slice(h * HD, (h + 2) * HD)
        key = key_ref[:, at].astype(F32)
        product = query_ref[:, at].astype(F32) * key
        upper = product.astype(BF16)
        lower = (product - upper.astype(F32)).astype(BF16)
        own = product_of(upper, same_head) + product_of(lower, same_head)
        high = own.astype(BF16).astype(F32)
        middle = (own - high).astype(BF16).astype(F32)
        rest = own - high - middle
        code = jnp.where(column == 0, F32(MARK), jnp.where(column == 1, high, F32(0.0)))
        code = jnp.where(column == 2, middle, jnp.where(column == 3, rest, code))
        coded = jnp.where(hidden, code, key).astype(BF16)
        for part in range(2):
            head = h + part
            inner = slice(part * HD, (part + 1) * HD)
            at = slice(head * HD, (head + 1) * HD)
            to = (head % HALF_HEADS) ^ NEAR_TURN
            start = place_of(head // HALF_HEADS)
            whole, ends = pl.ds(start, ROWS), pl.ds(start + ROWS, half)
            out_ref[to, whole, 0:HD] = coded[:, inner]
            out_ref[to, whole, HD : 2 * HD] = value_ref[:, at]
            out_ref[to, ends, 0:HD] = query_ref[0:half, at]
            out_ref[to, ends, HD : 2 * HD] = query_ref[half:ROWS, at]


def selector_of(shift):
    shape = (ROWS // 8, ROWS)
    return (lanes(shape) == shift + 8 * rows(shape)).astype(F32).astype(BF16)


def pick_middle_kernel(offsets_ref, blocks_ref, out_ref, cross_ref):
    count = ROWS // 8
    for half in range(2):
        selector = selector_of(shifts(offsets_ref, head_at(half))[0])
        start = place_of(half)
        for c in range(NEAR):
            rows_of = blocks_ref[c ^ NEAR_TURN, pl.ds(start, ROWS), :]
            picked = product_of(selector, rows_of).astype(BF16)
            for d in range(PEERS):
                place = (half ^ HALF_TURN) * PEERS + d
                out_ref[place, c * count : (c + 1) * count, :] = picked
    for c in range(NEAR):
        cross_ref[c] = blocks_ref[c ^ NEAR_TURN, FIRST_BLOCK : 2 * FIRST_BLOCK, :]


def pick_outer_kernel(offsets_ref, blocks_ref, out_hbm, picked_ref, sems):
    selector = selector_of(shifts(offsets_ref)[1])
    count = ROWS // 8
    for c in range(PEERS):
        picked = product_of(selector, blocks_ref[c, 0:ROWS, :]).astype(BF16)
        picked_ref[c * count : (c + 1) * count, :] = picked
    copies = [pltpu.make_async_copy(picked_ref, out_hbm.at[d], sems.at[d]) for d in range(PEERS)]
    for copy in copies:
        copy.start()
    for copy in copies:
        copy.wait()


def first_kernel(
    offsets_ref, near_ref, far_ref, state_ref, middle_ref, outer_ref, keys_ref, pairs_ref, wide, narrow
):
    middle, stride = shifts(offsets_ref)
    mine = my_half()
    for c in range(NEAR):
        for half, ref, place in ((mine, near_ref, c ^ NEAR_TURN), (1 - mine, far_ref, c)):
            block = half * NEAR + c
            start = pl.multiple_of(block * ROWS, ROWS)
            keys_ref[pl.ds(start, ROWS), :] = ref[place, 0:ROWS, :]
            pairs_ref[block] = ref[place, ROWS:FIRST_BLOCK, :]
    half = ROWS // 2
    low = lanes((half, 2 * HD)) < HD
    diagonal = rows((ROWS, ROWS)) == lanes((ROWS, ROWS))
    seen = against(marks(), keys_ref)
    for j in range(PEERS):
        pair = pairs_ref[j].astype(F32)
        wide[j * ROWS : j * ROWS + half, :] = jnp.where(low, pair, F32(0.0))
        wide[j * ROWS + half : (j + 1) * ROWS, :] = jnp.where(
            low, pltpu.roll(pair, HD, 1), F32(0.0)
        )
        query = wide[j * ROWS : (j + 1) * ROWS, :].astype(BF16)
        masks = [diagonal if c == j else None for c in range(PEERS)]
        state_ref[j * ROWS : (j + 1) * ROWS, :] = level(query, keys_ref, masks, seen)
    picked = wide[pl.ds(middle, ROWS, stride=8), :]
    middle_ref[...] = picked.astype(BF16)
    narrow[...] = picked
    outer_ref[...] = narrow[pl.ds(stride, ROWS // 8, stride=8), :].astype(BF16)


def middle_kernel(offsets_ref, state_ref, query_ref, blocks_ref, out_ref, merged_ref, wide):
    middle, _ = shifts(offsets_ref)
    mine = lax.axis_index("blk") ^ BLOCK_TURN
    row, lane = rows((ROWS, ROWS)), lanes((ROWS, ROWS))
    count = ROWS // 2
    diagonal = lane == row % count + count * lax.rem(mine, 2)
    masks = [
        diagonal & (row // count == (c // 4) ^ HALF_TURN) & (lax.div(mine, 2) == c % 4)
        for c in range(PEERS)
    ]
    found = level(query_ref[...], blocks_ref, masks)
    both = merge(state_ref[pl.ds(middle, ROWS, stride=8), :], found)
    merged_ref[...] = both
    wide[...] = state_ref[...]
    wide[pl.ds(middle, ROWS, stride=8), :] = both
    half = ROWS // 2
    low = lanes((half, 2 * HD)) < HD
    for j in range(PEERS):
        one = divided(wide[j * ROWS : j * ROWS + half, :])
        two = divided(wide[j * ROWS + half : (j + 1) * ROWS, :])
        out_ref[j ^ HOME_TURN] = jnp.where(low, pltpu.roll(one, HD, 1), two).astype(BF16)


def outer_kernel(offsets_ref, merged_ref, query_ref, blocks_ref, before_ref, out_ref):
    middle, stride = shifts(offsets_ref)
    block, group = lax.axis_index("blk") ^ BLOCK_TURN, lax.axis_index("grp")
    count = ROWS // 8
    shape = (count, ROWS)
    row = rows(shape)
    place = ((row // 8) ^ HALF_TURN) * (ROWS // 2) + block * 8 + row % 8
    diagonal = lanes(shape) == place
    masks = [diagonal & (group == g) for g in GROUP_ORDER]
    found = level(query_ref[...], blocks_ref, masks)
    both = divided(merge(merged_ref[pl.ds(stride, count, stride=8), :], found))
    rolled = pltpu.roll(both, HD, 1)
    tile = 16
    token = middle + 8 * stride
    start = pl.multiple_of((token // tile) * tile, tile)
    here = rows((tile, 2 * HD)) == token - start
    low = lanes((1, 2 * HD)) < HD
    for j in range(PEERS):
        row = jnp.where(low, rolled[2 * j : 2 * j + 1, :], both[2 * j + 1 : 2 * j + 2, :])
        place = j ^ HOME_TURN
        kept = before_ref[place, pl.ds(start, tile), :].astype(F32)
        out_ref[place, pl.ds(start, tile), :] = jnp.where(here, row, kept).astype(BF16)


def project_kernel(blocks_ref, weight_ref, out_hbm, out_ref, sems):
    half = ROWS // 2
    low = lanes((half, 2 * HD)) < HD
    tops, bottoms = [], []
    places = [(h // HALF_HEADS * NEAR + h % HALF_HEADS) ^ HOME_TURN for h in range(HEADS)]
    for h in range(0, HEADS, 2):
        one, two = blocks_ref[places[h]].astype(F32), blocks_ref[places[h + 1]].astype(F32)
        tops.append(jnp.where(low, one, pltpu.roll(two, HD, 1)).astype(BF16))
        bottoms.append(jnp.where(low, pltpu.roll(one, HD, 1), two).astype(BF16))
    combined = jnp.concatenate(
        [jnp.concatenate(tops, axis=1), jnp.concatenate(bottoms, axis=1)], axis=0
    )
    copies = []
    for n in range(out_ref.shape[1] // THIRD):
        at = slice(n * THIRD, (n + 1) * THIRD)
        out_ref[:, at] = product_of(combined, weight_ref[:, at]).astype(BF16)
        copies.append(pltpu.make_async_copy(out_ref.at[:, at], out_hbm.at[:, at], sems.at[n]))
        copies[-1].start()
    for copy in copies:
        copy.wait()


def call(kernel, name, out_shape, in_specs, scratch=(), flops=0, moved=0, aliases=None, out_spec=VMEM):
    outs = jax.tree.map(lambda _: out_spec, out_shape)
    return pl.pallas_call(
        kernel,
        name=name,
        out_shape=out_shape,
        in_specs=in_specs,
        out_specs=outs,
        scratch_shapes=list(scratch),
        input_output_aliases=aliases or {},
        compiler_params=pltpu.CompilerParams(vmem_limit_bytes=40 * 2**20),
        cost_estimate=pl.CostEstimate(flops=flops, bytes_accessed=moved, transcendentals=0),
    )


def shaped(*shape, dtype=BF16):
    return jax.ShapeDtypeStruct(shape, dtype)


def per_device(queries, keys, values, valid, offsets, w_out):
    wide = pltpu.VMEM((PEERS * ROWS, 2 * HD), F32)
    narrow = pltpu.VMEM((ROWS, 2 * HD), F32)
    swap = functools.partial(lax.all_to_all, split_axis=0, concat_axis=0, tiled=True)

    whole = pltpu.VMEM((ROWS, HEADS * HD), BF16)
    given = (queries, keys, values, valid.reshape(1, ROWS))
    packed = call(
        pack_kernel,
        "pack",
        shaped(NEAR, 2 * FIRST_BLOCK, 2 * HD),
        [HBM] * 4,
        [whole, whole, whole, pltpu.VMEM((1, ROWS), jnp.int32), pltpu.SemaphoreType.DMA((4,))],
    )(*(pltpu.with_memory_space_constraint(a, pltpu.HBM) for a in given))
    near_groups = [[z * NEAR + (x ^ NEAR_TURN) for x in range(NEAR)] for z in range(2)]
    near = swap(packed, "set", axis_index_groups=near_groups)
    middle_send, cross = call(
        pick_middle_kernel,
        "pick_middle",
        (shaped(2 * PEERS, ROWS // 2, 2 * HD), shaped(NEAR, FIRST_BLOCK, 2 * HD)),
        [VMEM, VMEM],
    )(offsets, near)
    middle_groups = [
        [
            (b ^ BLOCK_TURN) * PEERS + (z ^ HALF_TURN) * NEAR + x
            for z in range(2)
            for b in range(PEERS)
        ]
        for x in range(NEAR)
    ]
    middle_blocks = swap(middle_send, ("blk", "set"), axis_index_groups=middle_groups)
    middle_blocks = middle_blocks.reshape(PEERS, ROWS, 2 * HD)
    far = lax.ppermute(cross, "set", [(i, (i + NEAR) % PEERS) for i in range(PEERS)])
    state, middle_query, outer_query = call(
        first_kernel,
        "first",
        (shaped(PEERS * ROWS, 2 * HD, dtype=F32), shaped(ROWS, 2 * HD), shaped(ROWS // 8, 2 * HD)),
        [VMEM, VMEM, VMEM],
        [
            pltpu.VMEM((PEERS * ROWS, 2 * HD), BF16),
            pltpu.VMEM((PEERS, ROWS // 2, 2 * HD), BF16),
            wide,
            narrow,
        ],
        flops=6_000_000_000,
        moved=2_000_000,
    )(offsets, near, far)
    outer_send = call(
        pick_outer_kernel,
        "pick_outer",
        shaped(PEERS, ROWS, 2 * HD),
        [VMEM, VMEM],
        [pltpu.VMEM((ROWS, 2 * HD), BF16), pltpu.SemaphoreType.DMA((PEERS,))],
        out_spec=HBM,
    )(offsets, middle_blocks)
    outer_blocks = swap(outer_send, "grp", axis_index_groups=[list(GROUP_ORDER)])
    before, merged = call(
        middle_kernel,
        "middle",
        (shaped(PEERS, ROWS // 2, 2 * HD), shaped(ROWS, 2 * HD, dtype=F32)),
        [VMEM, VMEM, VMEM, VMEM],
        [wide],
        flops=2_000_000_000,
        moved=2_000_000,
    )(offsets, state, middle_query, middle_blocks.reshape(PEERS * ROWS, 2 * HD))
    combined = call(
        outer_kernel,
        "outer",
        shaped(PEERS, ROWS // 2, 2 * HD),
        [VMEM, VMEM, VMEM, VMEM, VMEM],
        aliases={4: 0},
    )(offsets, merged, outer_query, outer_blocks.reshape(PEERS * ROWS, 2 * HD), before)
    home = swap(combined, "set", axis_index_groups=[[s ^ HOME_TURN for s in range(PEERS)]])
    width = w_out.shape[1]
    return call(
        project_kernel,
        "project",
        shaped(ROWS, width),
        [VMEM, VMEM],
        [pltpu.VMEM((ROWS, width), BF16), pltpu.SemaphoreType.DMA((width // THIRD,))],
        out_spec=HBM,
    )(home, w_out)


def solution(mesh):
    spread = P(("grp", "blk", "set"), None)
    return jax.shard_map(
        per_device,
        mesh=mesh,
        in_specs=(spread, spread, spread, P(("grp", "blk", "set")), P(), P()),
        out_specs=spread,
        check_vma=False,
    )
```

```python
import functools
import math

import jax
import jax.numpy as jnp
from jax import lax
from jax.experimental import pallas as pl
from jax.experimental.pallas import tpu as pltpu
from jax.sharding import PartitionSpec as P

HEADS = 6
HD = 64
PEERS = 8
NEAR = 4
HALF_HEADS = HEADS // 2
NEAR_TURN = 3
BLOCK_TURN = 4
HALF_TURN = 1
GROUP_ORDER = (6, 0, 2, 4, 7, 1, 3, 5)
HOME_TURN = 7
ROWS = 128
FIRST_BLOCK = ROWS + ROWS // 2
MARK = 1024.0
EXP_SCALE = math.log2(math.e) / math.sqrt(HD)
FAR = -1e30
THIRD = 256
F32 = jnp.float32
BF16 = jnp.bfloat16

VMEM = pl.BlockSpec(memory_space=pltpu.VMEM)
HBM = pl.BlockSpec(memory_space=pltpu.HBM)


def lanes(shape):
    return lax.broadcasted_iota(jnp.int32, shape, len(shape) - 1)


def rows(shape):
    return lax.broadcasted_iota(jnp.int32, shape, len(shape) - 2)


def my_half():
    return lax.div(lax.axis_index("set"), NEAR)


def head_at(half):
    column = lax.rem(lax.axis_index("set"), NEAR)
    return half * HALF_HEADS + jnp.minimum(column, HALF_HEADS - 1)


def shifts(offsets_ref, head=None):
    head = head_at(my_half()) if head is None else head
    both = offsets_ref[...].astype(F32)
    both = jnp.where(lanes(both.shape) == head, both, F32(0.0))
    middle = jnp.sum(both[0:1, :]).astype(jnp.int32)
    outer = jnp.sum(both[1:2, :]).astype(jnp.int32)
    return middle, (outer - middle) // 8


def place_of(half):
    return pl.multiple_of(jnp.where(half == my_half(), 0, FIRST_BLOCK), FIRST_BLOCK)


def marks():
    shape = (16, 2 * HD)
    row, lane = rows(shape), lanes(shape)
    chosen = ((row == 0) & (lane == 0)) | ((row == 1) & (lane >= 1) & (lane <= 3))
    return chosen.astype(F32).astype(BF16)


def product_of(one, two):
    return jnp.dot(one, two, preferred_element_type=F32)


def against(query, keys_ref):
    return lax.dot_general(
        query, keys_ref[...], (((1,), (1,)), ((), ())), preferred_element_type=F32
    )


def level(query, keys_ref, self_masks, seen=None):
    count = query.shape[0]
    if seen is None:
        found = against(jnp.concatenate([query, marks()], axis=0), keys_ref)
        seen = found[count:, :]
    else:
        found = against(query, keys_ref)
    parts = []
    for c in range(PEERS):
        at = slice(c * ROWS, (c + 1) * ROWS)
        hidden = seen[0:1, at] > F32(MARK / 2)
        masked = found[0:count, at] + jnp.where(hidden, F32(FAR), F32(0.0))
        if self_masks[c] is not None:
            masked = jnp.where(self_masks[c] & hidden, seen[1:2, at], masked)
        parts.append(masked)
    best = functools.reduce(jnp.maximum, parts)
    top = jnp.max(best, axis=1, keepdims=True)
    weights = [jnp.exp2((part - top) * F32(EXP_SCALE)) for part in parts]
    total = jnp.sum(functools.reduce(jnp.add, weights), axis=1, keepdims=True)
    probs = jnp.concatenate([weight.astype(BF16) for weight in weights], axis=1)
    mixture = product_of(probs, keys_ref[...])
    lane = lanes(mixture.shape)
    return jnp.where(lane < 32, top, jnp.where(lane < 64, total, mixture))


def merge(one, two):
    top_one, top_two = one[:, 0:1], two[:, 0:1]
    top = jnp.maximum(top_one, top_two)
    scale_one = jnp.exp2((top_one - top) * F32(EXP_SCALE))
    scale_two = jnp.exp2((top_two - top) * F32(EXP_SCALE))
    both = one * scale_one + two * scale_two
    return jnp.where(lanes(both.shape) < 32, top, both)


def divided(state):
    return state / state[:, 32:33]


def pack_kernel(query_hbm, key_hbm, value_hbm, valid_hbm, out_ref, query_ref, key_ref, value_ref, valid_ref, sems):
    pairs = (
        (valid_hbm, valid_ref),
        (key_hbm, key_ref),
        (value_hbm, value_ref),
        (query_hbm, query_ref),
    )
    copies = [pltpu.make_async_copy(a, b, sems.at[i]) for i, (a, b) in enumerate(pairs)]
    for copy in copies:
        copy.start()
    for c in range(HALF_HEADS, NEAR):
        out_ref[c ^ NEAR_TURN] = jnp.zeros((2 * FIRST_BLOCK, 2 * HD), BF16)
    for copy in copies:
        copy.wait()
    square = (ROWS, 2 * HD)
    row, lane = rows(square), lanes(square)
    valid = jnp.where(row == lane, valid_ref[...].astype(F32), F32(0.0)).astype(BF16)
    hidden = product_of(valid, jnp.ones(square, BF16)) < F32(0.5)
    same_head = ((row // HD) == (lane // HD)).astype(F32).astype(BF16)
    column = lane % HD
    half = ROWS // 2
    for h in range(0, HEADS, 2):
        at = slice(h * HD, (h + 2) * HD)
        key = key_ref[:, at].astype(F32)
        product = query_ref[:, at].astype(F32) * key
        upper = product.astype(BF16)
        lower = (product - upper.astype(F32)).astype(BF16)
        own = product_of(upper, same_head) + product_of(lower, same_head)
        high = own.astype(BF16).astype(F32)
        middle = (own - high).astype(BF16).astype(F32)
        rest = own - high - middle
        code = jnp.where(column == 0, F32(MARK), jnp.where(column == 1, high, F32(0.0)))
        code = jnp.where(column == 2, middle, jnp.where(column == 3, rest, code))
        coded = jnp.where(hidden, code, key).astype(BF16)
        for part in range(2):
            head = h + part
            inner = slice(part * HD, (part + 1) * HD)
            at = slice(head * HD, (head + 1) * HD)
            to = (head % HALF_HEADS) ^ NEAR_TURN
            start = place_of(head // HALF_HEADS)
            whole, ends = pl.ds(start, ROWS), pl.ds(start + ROWS, half)
            out_ref[to, whole, 0:HD] = coded[:, inner]
            out_ref[to, whole, HD : 2 * HD] = value_ref[:, at]
            out_ref[to, ends, 0:HD] = query_ref[0:half, at]
            out_ref[to, ends, HD : 2 * HD] = query_ref[half:ROWS, at]


def selector_of(shift):
    shape = (ROWS // 8, ROWS)
    return (lanes(shape) == shift + 8 * rows(shape)).astype(F32).astype(BF16)


def pick_middle_kernel(offsets_ref, blocks_ref, out_ref, cross_ref):
    count = ROWS // 8
    for half in range(2):
        selector = selector_of(shifts(offsets_ref, head_at(half))[0])
        start = place_of(half)
        for c in range(NEAR):
            rows_of = blocks_ref[c ^ NEAR_TURN, pl.ds(start, ROWS), :]
            picked = product_of(selector, rows_of).astype(BF16)
            for d in range(PEERS):
                place = (half ^ HALF_TURN) * PEERS + d
                out_ref[place, c * count : (c + 1) * count, :] = picked
    for c in range(NEAR):
        cross_ref[c] = blocks_ref[c ^ NEAR_TURN, FIRST_BLOCK : 2 * FIRST_BLOCK, :]


def pick_outer_kernel(offsets_ref, blocks_ref, out_hbm, picked_ref, sems):
    selector = selector_of(shifts(offsets_ref)[1])
    count = ROWS // 8
    for c in range(PEERS):
        picked = product_of(selector, blocks_ref[c, 0:ROWS, :]).astype(BF16)
        picked_ref[c * count : (c + 1) * count, :] = picked
    copies = [pltpu.make_async_copy(picked_ref, out_hbm.at[d], sems.at[d]) for d in range(PEERS)]
    for copy in copies:
        copy.start()
    for copy in copies:
        copy.wait()


def first_kernel(
    offsets_ref, near_ref, far_ref, state_ref, middle_ref, outer_ref, keys_ref, pairs_ref, wide, narrow
):
    middle, stride = shifts(offsets_ref)
    mine = my_half()
    for c in range(NEAR):
        for half, ref, place in ((mine, near_ref, c ^ NEAR_TURN), (1 - mine, far_ref, c)):
            block = half * NEAR + c
            start = pl.multiple_of(block * ROWS, ROWS)
            keys_ref[pl.ds(start, ROWS), :] = ref[place, 0:ROWS, :]
            pairs_ref[block] = ref[place, ROWS:FIRST_BLOCK, :]
    half = ROWS // 2
    low = lanes((half, 2 * HD)) < HD
    diagonal = rows((ROWS, ROWS)) == lanes((ROWS, ROWS))
    seen = against(marks(), keys_ref)
    for j in range(PEERS):
        pair = pairs_ref[j].astype(F32)
        wide[j * ROWS : j * ROWS + half, :] = jnp.where(low, pair, F32(0.0))
        wide[j * ROWS + half : (j + 1) * ROWS, :] = jnp.where(
            low, pltpu.roll(pair, HD, 1), F32(0.0)
        )
        query = wide[j * ROWS : (j + 1) * ROWS, :].astype(BF16)
        masks = [diagonal if c == j else None for c in range(PEERS)]
        state_ref[j * ROWS : (j + 1) * ROWS, :] = level(query, keys_ref, masks, seen)
    picked = wide[pl.ds(middle, ROWS, stride=8), :]
    middle_ref[...] = picked.astype(BF16)
    narrow[...] = picked
    outer_ref[...] = narrow[pl.ds(stride, ROWS // 8, stride=8), :].astype(BF16)


def middle_kernel(offsets_ref, state_ref, query_ref, blocks_ref, out_ref, merged_ref, wide):
    middle, _ = shifts(offsets_ref)
    mine = lax.axis_index("blk") ^ BLOCK_TURN
    row, lane = rows((ROWS, ROWS)), lanes((ROWS, ROWS))
    count = ROWS // 2
    diagonal = lane == row % count + count * lax.rem(mine, 2)
    masks = [
        diagonal & (row // count == (c // 4) ^ HALF_TURN) & (lax.div(mine, 2) == c % 4)
        for c in range(PEERS)
    ]
    found = level(query_ref[...], blocks_ref, masks)
    both = merge(state_ref[pl.ds(middle, ROWS, stride=8), :], found)
    merged_ref[...] = both
    wide[...] = state_ref[...]
    wide[pl.ds(middle, ROWS, stride=8), :] = both
    half = ROWS // 2
    low = lanes((half, 2 * HD)) < HD
    for j in range(PEERS):
        one = divided(wide[j * ROWS : j * ROWS + half, :])
        two = divided(wide[j * ROWS + half : (j + 1) * ROWS, :])
        out_ref[j ^ HOME_TURN] = jnp.where(low, pltpu.roll(one, HD, 1), two).astype(BF16)


def outer_kernel(offsets_ref, merged_ref, query_ref, blocks_ref, before_ref, out_ref):
    middle, stride = shifts(offsets_ref)
    block, group = lax.axis_index("blk") ^ BLOCK_TURN, lax.axis_index("grp")
    count = ROWS // 8
    shape = (count, ROWS)
    row = rows(shape)
    place = ((row // 8) ^ HALF_TURN) * (ROWS // 2) + block * 8 + row % 8
    diagonal = lanes(shape) == place
    masks = [diagonal & (group == g) for g in GROUP_ORDER]
    found = level(query_ref[...], blocks_ref, masks)
    both = divided(merge(merged_ref[pl.ds(stride, count, stride=8), :], found))
    rolled = pltpu.roll(both, HD, 1)
    tile = 16
    token = middle + 8 * stride
    start = pl.multiple_of((token // tile) * tile, tile)
    here = rows((tile, 2 * HD)) == token - start
    low = lanes((1, 2 * HD)) < HD
    for j in range(PEERS):
        row = jnp.where(low, rolled[2 * j : 2 * j + 1, :], both[2 * j + 1 : 2 * j + 2, :])
        place = j ^ HOME_TURN
        kept = before_ref[place, pl.ds(start, tile), :].astype(F32)
        out_ref[place, pl.ds(start, tile), :] = jnp.where(here, row, kept).astype(BF16)


def project_kernel(blocks_ref, weight_ref, out_hbm, out_ref, sems):
    half = ROWS // 2
    low = lanes((half, 2 * HD)) < HD
    tops, bottoms = [], []
    places = [(h // HALF_HEADS * NEAR + h % HALF_HEADS) ^ HOME_TURN for h in range(HEADS)]
    for h in range(0, HEADS, 2):
        one, two = blocks_ref[places[h]].astype(F32), blocks_ref[places[h + 1]].astype(F32)
        tops.append(jnp.where(low, one, pltpu.roll(two, HD, 1)).astype(BF16))
        bottoms.append(jnp.where(low, pltpu.roll(one, HD, 1), two).astype(BF16))
    combined = jnp.concatenate(
        [jnp.concatenate(tops, axis=1), jnp.concatenate(bottoms, axis=1)], axis=0
    )
    copies = []
    for n in range(out_ref.shape[1] // THIRD):
        at = slice(n * THIRD, (n + 1) * THIRD)
        out_ref[:, at] = product_of(combined, weight_ref[:, at]).astype(BF16)
        copies.append(pltpu.make_async_copy(out_ref.at[:, at], out_hbm.at[:, at], sems.at[n]))
        copies[-1].start()
    for copy in copies:
        copy.wait()


def call(kernel, name, out_shape, in_specs, scratch=(), flops=0, moved=0, aliases=None, out_spec=VMEM):
    outs = jax.tree.map(lambda _: out_spec, out_shape)
    return pl.pallas_call(
        kernel,
        name=name,
        out_shape=out_shape,
        in_specs=in_specs,
        out_specs=outs,
        scratch_shapes=list(scratch),
        input_output_aliases=aliases or {},
        compiler_params=pltpu.CompilerParams(vmem_limit_bytes=40 * 2**20),
        cost_estimate=pl.CostEstimate(flops=flops, bytes_accessed=moved, transcendentals=0),
    )


def shaped(*shape, dtype=BF16):
    return jax.ShapeDtypeStruct(shape, dtype)


def per_device(queries, keys, values, valid, offsets, w_out):
    wide = pltpu.VMEM((PEERS * ROWS, 2 * HD), F32)
    narrow = pltpu.VMEM((ROWS, 2 * HD), F32)
    swap = functools.partial(lax.all_to_all, split_axis=0, concat_axis=0, tiled=True)

    whole = pltpu.VMEM((ROWS, HEADS * HD), BF16)
    given = (queries, keys, values, valid.reshape(1, ROWS))
    packed = call(
        pack_kernel,
        "pack",
        shaped(NEAR, 2 * FIRST_BLOCK, 2 * HD),
        [HBM] * 4,
        [whole, whole, whole, pltpu.VMEM((1, ROWS), jnp.int32), pltpu.SemaphoreType.DMA((4,))],
    )(*(pltpu.with_memory_space_constraint(a, pltpu.HBM) for a in given))
    near_groups = [[z * NEAR + (x ^ NEAR_TURN) for x in range(NEAR)] for z in range(2)]
    near = swap(packed, "set", axis_index_groups=near_groups)
    middle_send, cross = call(
        pick_middle_kernel,
        "pick_middle",
        (shaped(2 * PEERS, ROWS // 2, 2 * HD), shaped(NEAR, FIRST_BLOCK, 2 * HD)),
        [VMEM, VMEM],
    )(offsets, near)
    middle_groups = [
        [
            (b ^ BLOCK_TURN) * PEERS + (z ^ HALF_TURN) * NEAR + x
            for z in range(2)
            for b in range(PEERS)
        ]
        for x in range(NEAR)
    ]
    middle_blocks = swap(middle_send, ("blk", "set"), axis_index_groups=middle_groups)
    middle_blocks = middle_blocks.reshape(PEERS, ROWS, 2 * HD)
    far = lax.ppermute(cross, "set", [(i, (i + NEAR) % PEERS) for i in range(PEERS)])
    state, middle_query, outer_query = call(
        first_kernel,
        "first",
        (shaped(PEERS * ROWS, 2 * HD, dtype=F32), shaped(ROWS, 2 * HD), shaped(ROWS // 8, 2 * HD)),
        [VMEM, VMEM, VMEM],
        [
            pltpu.VMEM((PEERS * ROWS, 2 * HD), BF16),
            pltpu.VMEM((PEERS, ROWS // 2, 2 * HD), BF16),
            wide,
            narrow,
        ],
        flops=6_000_000_000,
        moved=2_000_000,
    )(offsets, near, far)
    outer_send = call(
        pick_outer_kernel,
        "pick_outer",
        shaped(PEERS, ROWS, 2 * HD),
        [VMEM, VMEM],
        [pltpu.VMEM((ROWS, 2 * HD), BF16), pltpu.SemaphoreType.DMA((PEERS,))],
        out_spec=HBM,
    )(offsets, middle_blocks)
    outer_blocks = swap(outer_send, "grp", axis_index_groups=[list(GROUP_ORDER)])
    before, merged = call(
        middle_kernel,
        "middle",
        (shaped(PEERS, ROWS // 2, 2 * HD), shaped(ROWS, 2 * HD, dtype=F32)),
        [VMEM, VMEM, VMEM, VMEM],
        [wide],
        flops=2_000_000_000,
        moved=2_000_000,
    )(offsets, state, middle_query, middle_blocks.reshape(PEERS * ROWS, 2 * HD))
    combined = call(
        outer_kernel,
        "outer",
        shaped(PEERS, ROWS // 2, 2 * HD),
        [VMEM, VMEM, VMEM, VMEM, VMEM],
        aliases={4: 0},
    )(offsets, merged, outer_query, outer_blocks.reshape(PEERS * ROWS, 2 * HD), before)
    home = swap(combined, "set", axis_index_groups=[[s ^ HOME_TURN for s in range(PEERS)]])
    width = w_out.shape[1]
    return call(
        project_kernel,
        "project",
        shaped(ROWS, width),
        [VMEM, VMEM],
        [pltpu.VMEM((ROWS, width), BF16), pltpu.SemaphoreType.DMA((width // THIRD,))],
        out_spec=HBM,
    )(home, w_out)


def solution(mesh):
    spread = P(("grp", "blk", "set"), None)
    return jax.shard_map(
        per_device,
        mesh=mesh,
        in_specs=(spread, spread, spread, P(("grp", "blk", "set")), P(), P()),
        out_specs=spread,
        check_vma=False,
    )
```

```python
import functools
import math

import jax
import jax.numpy as jnp
from jax import lax
from jax.experimental import pallas as pl
from jax.experimental.pallas import tpu as pltpu
from jax.sharding import PartitionSpec as P

HEADS = 6
HD = 64
PEERS = 8
NEAR = 4
HALF_HEADS = HEADS // 2
NEAR_TURN = 2
BLOCK_TURN = 4
HALF_TURN = 1
GROUP_ORDER = (6, 4, 2, 0, 7, 5, 3, 1)
HOME_TURN = 7
ROWS = 128
FIRST_BLOCK = ROWS + ROWS // 2
MARK = 1024.0
EXP_SCALE = math.log2(math.e) / math.sqrt(HD)
FAR = -1e30
THIRD = 256
F32 = jnp.float32
BF16 = jnp.bfloat16

VMEM = pl.BlockSpec(memory_space=pltpu.VMEM)
HBM = pl.BlockSpec(memory_space=pltpu.HBM)


def lanes(shape):
    return lax.broadcasted_iota(jnp.int32, shape, len(shape) - 1)


def rows(shape):
    return lax.broadcasted_iota(jnp.int32, shape, len(shape) - 2)


def my_half():
    return lax.div(lax.axis_index("set"), NEAR)


def head_at(half):
    column = lax.rem(lax.axis_index("set"), NEAR)
    return half * HALF_HEADS + jnp.minimum(column, HALF_HEADS - 1)


def shifts(offsets_ref, head=None):
    head = head_at(my_half()) if head is None else head
    both = offsets_ref[...].astype(F32)
    both = jnp.where(lanes(both.shape) == head, both, F32(0.0))
    middle = jnp.sum(both[0:1, :]).astype(jnp.int32)
    outer = jnp.sum(both[1:2, :]).astype(jnp.int32)
    return middle, (outer - middle) // 8


def place_of(half):
    return pl.multiple_of(jnp.where(half == my_half(), 0, FIRST_BLOCK), FIRST_BLOCK)


def marks():
    shape = (16, 2 * HD)
    row, lane = rows(shape), lanes(shape)
    chosen = ((row == 0) & (lane == 0)) | ((row == 1) & (lane >= 1) & (lane <= 3))
    return chosen.astype(F32).astype(BF16)


def product_of(one, two):
    return jnp.dot(one, two, preferred_element_type=F32)


def against(query, keys_ref):
    return lax.dot_general(
        query, keys_ref[...], (((1,), (1,)), ((), ())), preferred_element_type=F32
    )


def level(query, keys_ref, self_masks, seen=None):
    count = query.shape[0]
    if seen is None:
        found = against(jnp.concatenate([query, marks()], axis=0), keys_ref)
        seen = found[count:, :]
    else:
        found = against(query, keys_ref)
    parts = []
    for c in range(PEERS):
        at = slice(c * ROWS, (c + 1) * ROWS)
        hidden = seen[0:1, at] > F32(MARK / 2)
        masked = found[0:count, at] + jnp.where(hidden, F32(FAR), F32(0.0))
        if self_masks[c] is not None:
            masked = jnp.where(self_masks[c] & hidden, seen[1:2, at], masked)
        parts.append(masked)
    best = functools.reduce(jnp.maximum, parts)
    top = jnp.max(best, axis=1, keepdims=True)
    weights = [jnp.exp2((part - top) * F32(EXP_SCALE)) for part in parts]
    total = jnp.sum(functools.reduce(jnp.add, weights), axis=1, keepdims=True)
    probs = jnp.concatenate([weight.astype(BF16) for weight in weights], axis=1)
    mixture = product_of(probs, keys_ref[...])
    lane = lanes(mixture.shape)
    return jnp.where(lane < 32, top, jnp.where(lane < 64, total, mixture))


def merge(one, two):
    top_one, top_two = one[:, 0:1], two[:, 0:1]
    top = jnp.maximum(top_one, top_two)
    scale_one = jnp.exp2((top_one - top) * F32(EXP_SCALE))
    scale_two = jnp.exp2((top_two - top) * F32(EXP_SCALE))
    both = one * scale_one + two * scale_two
    return jnp.where(lanes(both.shape) < 32, top, both)


def divided(state):
    return state / state[:, 32:33]


def pack_kernel(query_hbm, key_hbm, value_hbm, valid_hbm, out_ref, query_ref, key_ref, value_ref, valid_ref, sems):
    pairs = (
        (valid_hbm, valid_ref),
        (key_hbm, key_ref),
        (value_hbm, value_ref),
        (query_hbm, query_ref),
    )
    copies = [pltpu.make_async_copy(a, b, sems.at[i]) for i, (a, b) in enumerate(pairs)]
    for copy in copies:
        copy.start()
    for c in range(HALF_HEADS, NEAR):
        out_ref[c ^ NEAR_TURN] = jnp.zeros((2 * FIRST_BLOCK, 2 * HD), BF16)
    for copy in copies:
        copy.wait()
    square = (ROWS, 2 * HD)
    row, lane = rows(square), lanes(square)
    valid = jnp.where(row == lane, valid_ref[...].astype(F32), F32(0.0)).astype(BF16)
    hidden = product_of(valid, jnp.ones(square, BF16)) < F32(0.5)
    same_head = ((row // HD) == (lane // HD)).astype(F32).astype(BF16)
    column = lane % HD
    half = ROWS // 2
    for h in range(0, HEADS, 2):
        at = slice(h * HD, (h + 2) * HD)
        key = key_ref[:, at].astype(F32)
        product = query_ref[:, at].astype(F32) * key
        upper = product.astype(BF16)
        lower = (product - upper.astype(F32)).astype(BF16)
        own = product_of(upper, same_head) + product_of(lower, same_head)
        high = own.astype(BF16).astype(F32)
        middle = (own - high).astype(BF16).astype(F32)
        rest = own - high - middle
        code = jnp.where(column == 0, F32(MARK), jnp.where(column == 1, high, F32(0.0)))
        code = jnp.where(column == 2, middle, jnp.where(column == 3, rest, code))
        coded = jnp.where(hidden, code, key).astype(BF16)
        for part in range(2):
            head = h + part
            inner = slice(part * HD, (part + 1) * HD)
            at = slice(head * HD, (head + 1) * HD)
            to = (head % HALF_HEADS) ^ NEAR_TURN
            start = place_of(head // HALF_HEADS)
            whole, ends = pl.ds(start, ROWS), pl.ds(start + ROWS, half)
            out_ref[to, whole, 0:HD] = coded[:, inner]
            out_ref[to, whole, HD : 2 * HD] = value_ref[:, at]
            out_ref[to, ends, 0:HD] = query_ref[0:half, at]
            out_ref[to, ends, HD : 2 * HD] = query_ref[half:ROWS, at]


def selector_of(shift):
    shape = (ROWS // 8, ROWS)
    return (lanes(shape) == shift + 8 * rows(shape)).astype(F32).astype(BF16)


def pick_middle_kernel(offsets_ref, blocks_ref, out_ref, cross_ref):
    count = ROWS // 8
    for half in range(2):
        selector = selector_of(shifts(offsets_ref, head_at(half))[0])
        start = place_of(half)
        for c in range(NEAR):
            rows_of = blocks_ref[c ^ NEAR_TURN, pl.ds(start, ROWS), :]
            picked = product_of(selector, rows_of).astype(BF16)
            for d in range(PEERS):
                place = (half ^ HALF_TURN) * PEERS + d
                out_ref[place, c * count : (c + 1) * count, :] = picked
    for c in range(NEAR):
        cross_ref[c] = blocks_ref[c ^ NEAR_TURN, FIRST_BLOCK : 2 * FIRST_BLOCK, :]


def pick_outer_kernel(offsets_ref, blocks_ref, out_hbm, picked_ref, sems):
    selector = selector_of(shifts(offsets_ref)[1])
    count = ROWS // 8
    for c in range(PEERS):
        picked = product_of(selector, blocks_ref[c, 0:ROWS, :]).astype(BF16)
        picked_ref[c * count : (c + 1) * count, :] = picked
    copies = [pltpu.make_async_copy(picked_ref, out_hbm.at[d], sems.at[d]) for d in range(PEERS)]
    for copy in copies:
        copy.start()
    for copy in copies:
        copy.wait()


def first_kernel(
    offsets_ref, near_ref, far_ref, state_ref, middle_ref, outer_ref, keys_ref, pairs_ref, wide, narrow
):
    middle, stride = shifts(offsets_ref)
    mine = my_half()
    for c in range(NEAR):
        for half, ref, place in ((mine, near_ref, c ^ NEAR_TURN), (1 - mine, far_ref, c)):
            block = half * NEAR + c
            start = pl.multiple_of(block * ROWS, ROWS)
            keys_ref[pl.ds(start, ROWS), :] = ref[place, 0:ROWS, :]
            pairs_ref[block] = ref[place, ROWS:FIRST_BLOCK, :]
    half = ROWS // 2
    low = lanes((half, 2 * HD)) < HD
    diagonal = rows((ROWS, ROWS)) == lanes((ROWS, ROWS))
    seen = against(marks(), keys_ref)
    for j in range(PEERS):
        pair = pairs_ref[j].astype(F32)
        wide[j * ROWS : j * ROWS + half, :] = jnp.where(low, pair, F32(0.0))
        wide[j * ROWS + half : (j + 1) * ROWS, :] = jnp.where(
            low, pltpu.roll(pair, HD, 1), F32(0.0)
        )
        query = wide[j * ROWS : (j + 1) * ROWS, :].astype(BF16)
        masks = [diagonal if c == j else None for c in range(PEERS)]
        state_ref[j * ROWS : (j + 1) * ROWS, :] = level(query, keys_ref, masks, seen)
    picked = wide[pl.ds(middle, ROWS, stride=8), :]
    middle_ref[...] = picked.astype(BF16)
    narrow[...] = picked
    outer_ref[...] = narrow[pl.ds(stride, ROWS // 8, stride=8), :].astype(BF16)


def middle_kernel(offsets_ref, state_ref, query_ref, blocks_ref, out_ref, merged_ref, wide):
    middle, _ = shifts(offsets_ref)
    mine = lax.axis_index("blk") ^ BLOCK_TURN
    row, lane = rows((ROWS, ROWS)), lanes((ROWS, ROWS))
    count = ROWS // 2
    diagonal = lane == row % count + count * lax.rem(mine, 2)
    masks = [
        diagonal & (row // count == (c // 4) ^ HALF_TURN) & (lax.div(mine, 2) == c % 4)
        for c in range(PEERS)
    ]
    found = level(query_ref[...], blocks_ref, masks)
    both = merge(state_ref[pl.ds(middle, ROWS, stride=8), :], found)
    merged_ref[...] = both
    wide[...] = state_ref[...]
    wide[pl.ds(middle, ROWS, stride=8), :] = both
    half = ROWS // 2
    low = lanes((half, 2 * HD)) < HD
    for j in range(PEERS):
        one = divided(wide[j * ROWS : j * ROWS + half, :])
        two = divided(wide[j * ROWS + half : (j + 1) * ROWS, :])
        out_ref[j ^ HOME_TURN] = jnp.where(low, pltpu.roll(one, HD, 1), two).astype(BF16)


def outer_kernel(offsets_ref, merged_ref, query_ref, blocks_ref, before_ref, out_ref):
    middle, stride = shifts(offsets_ref)
    block, group = lax.axis_index("blk") ^ BLOCK_TURN, lax.axis_index("grp")
    count = ROWS // 8
    shape = (count, ROWS)
    row = rows(shape)
    place = ((row // 8) ^ HALF_TURN) * (ROWS // 2) + block * 8 + row % 8
    diagonal = lanes(shape) == place
    masks = [diagonal & (group == g) for g in GROUP_ORDER]
    found = level(query_ref[...], blocks_ref, masks)
    both = divided(merge(merged_ref[pl.ds(stride, count, stride=8), :], found))
    rolled = pltpu.roll(both, HD, 1)
    tile = 16
    token = middle + 8 * stride
    start = pl.multiple_of((token // tile) * tile, tile)
    here = rows((tile, 2 * HD)) == token - start
    low = lanes((1, 2 * HD)) < HD
    for j in range(PEERS):
        row = jnp.where(low, rolled[2 * j : 2 * j + 1, :], both[2 * j + 1 : 2 * j + 2, :])
        place = j ^ HOME_TURN
        kept = before_ref[place, pl.ds(start, tile), :].astype(F32)
        out_ref[place, pl.ds(start, tile), :] = jnp.where(here, row, kept).astype(BF16)


def project_kernel(blocks_ref, weight_ref, out_hbm, out_ref, sems):
    half = ROWS // 2
    low = lanes((half, 2 * HD)) < HD
    tops, bottoms = [], []
    places = [(h // HALF_HEADS * NEAR + h % HALF_HEADS) ^ HOME_TURN for h in range(HEADS)]
    for h in range(0, HEADS, 2):
        one, two = blocks_ref[places[h]].astype(F32), blocks_ref[places[h + 1]].astype(F32)
        tops.append(jnp.where(low, one, pltpu.roll(two, HD, 1)).astype(BF16))
        bottoms.append(jnp.where(low, pltpu.roll(one, HD, 1), two).astype(BF16))
    combined = jnp.concatenate(
        [jnp.concatenate(tops, axis=1), jnp.concatenate(bottoms, axis=1)], axis=0
    )
    copies = []
    for n in range(out_ref.shape[1] // THIRD):
        at = slice(n * THIRD, (n + 1) * THIRD)
        out_ref[:, at] = product_of(combined, weight_ref[:, at]).astype(BF16)
        copies.append(pltpu.make_async_copy(out_ref.at[:, at], out_hbm.at[:, at], sems.at[n]))
        copies[-1].start()
    for copy in copies:
        copy.wait()


def call(kernel, name, out_shape, in_specs, scratch=(), flops=0, moved=0, aliases=None, out_spec=VMEM):
    outs = jax.tree.map(lambda _: out_spec, out_shape)
    return pl.pallas_call(
        kernel,
        name=name,
        out_shape=out_shape,
        in_specs=in_specs,
        out_specs=outs,
        scratch_shapes=list(scratch),
        input_output_aliases=aliases or {},
        compiler_params=pltpu.CompilerParams(vmem_limit_bytes=40 * 2**20),
        cost_estimate=pl.CostEstimate(flops=flops, bytes_accessed=moved, transcendentals=0),
    )


def shaped(*shape, dtype=BF16):
    return jax.ShapeDtypeStruct(shape, dtype)


def per_device(queries, keys, values, valid, offsets, w_out):
    wide = pltpu.VMEM((PEERS * ROWS, 2 * HD), F32)
    narrow = pltpu.VMEM((ROWS, 2 * HD), F32)
    swap = functools.partial(lax.all_to_all, split_axis=0, concat_axis=0, tiled=True)

    whole = pltpu.VMEM((ROWS, HEADS * HD), BF16)
    given = (queries, keys, values, valid.reshape(1, ROWS))
    packed = call(
        pack_kernel,
        "pack",
        shaped(NEAR, 2 * FIRST_BLOCK, 2 * HD),
        [HBM] * 4,
        [whole, whole, whole, pltpu.VMEM((1, ROWS), jnp.int32), pltpu.SemaphoreType.DMA((4,))],
    )(*(pltpu.with_memory_space_constraint(a, pltpu.HBM) for a in given))
    near_groups = [[z * NEAR + (x ^ NEAR_TURN) for x in range(NEAR)] for z in range(2)]
    near = swap(packed, "set", axis_index_groups=near_groups)
    middle_send, cross = call(
        pick_middle_kernel,
        "pick_middle",
        (shaped(2 * PEERS, ROWS // 2, 2 * HD), shaped(NEAR, FIRST_BLOCK, 2 * HD)),
        [VMEM, VMEM],
    )(offsets, near)
    middle_groups = [
        [
            (b ^ BLOCK_TURN) * PEERS + (z ^ HALF_TURN) * NEAR + x
            for z in range(2)
            for b in range(PEERS)
        ]
        for x in range(NEAR)
    ]
    middle_blocks = swap(middle_send, ("blk", "set"), axis_index_groups=middle_groups)
    middle_blocks = middle_blocks.reshape(PEERS, ROWS, 2 * HD)
    far = lax.ppermute(cross, "set", [(i, (i + NEAR) % PEERS) for i in range(PEERS)])
    state, middle_query, outer_query = call(
        first_kernel,
        "first",
        (shaped(PEERS * ROWS, 2 * HD, dtype=F32), shaped(ROWS, 2 * HD), shaped(ROWS // 8, 2 * HD)),
        [VMEM, VMEM, VMEM],
        [
            pltpu.VMEM((PEERS * ROWS, 2 * HD), BF16),
            pltpu.VMEM((PEERS, ROWS // 2, 2 * HD), BF16),
            wide,
            narrow,
        ],
        flops=6_000_000_000,
        moved=2_000_000,
    )(offsets, near, far)
    outer_send = call(
        pick_outer_kernel,
        "pick_outer",
        shaped(PEERS, ROWS, 2 * HD),
        [VMEM, VMEM],
        [pltpu.VMEM((ROWS, 2 * HD), BF16), pltpu.SemaphoreType.DMA((PEERS,))],
        out_spec=HBM,
    )(offsets, middle_blocks)
    outer_blocks = swap(outer_send, "grp", axis_index_groups=[list(GROUP_ORDER)])
    before, merged = call(
        middle_kernel,
        "middle",
        (shaped(PEERS, ROWS // 2, 2 * HD), shaped(ROWS, 2 * HD, dtype=F32)),
        [VMEM, VMEM, VMEM, VMEM],
        [wide],
        flops=2_000_000_000,
        moved=2_000_000,
    )(offsets, state, middle_query, middle_blocks.reshape(PEERS * ROWS, 2 * HD))
    combined = call(
        outer_kernel,
        "outer",
        shaped(PEERS, ROWS // 2, 2 * HD),
        [VMEM, VMEM, VMEM, VMEM, VMEM],
        aliases={4: 0},
    )(offsets, merged, outer_query, outer_blocks.reshape(PEERS * ROWS, 2 * HD), before)
    home = swap(combined, "set", axis_index_groups=[[s ^ HOME_TURN for s in range(PEERS)]])
    width = w_out.shape[1]
    return call(
        project_kernel,
        "project",
        shaped(ROWS, width),
        [VMEM, VMEM],
        [pltpu.VMEM((ROWS, width), BF16), pltpu.SemaphoreType.DMA((width // THIRD,))],
        out_spec=HBM,
    )(home, w_out)


def solution(mesh):
    spread = P(("grp", "blk", "set"), None)
    return jax.shard_map(
        per_device,
        mesh=mesh,
        in_specs=(spread, spread, spread, P(("grp", "blk", "set")), P(), P()),
        out_specs=spread,
        check_vma=False,
    )
```
